32 devices in a mesh: dp: 8 (over z, x), head: 4 (over y, core).
Axes of the slice: x: 2, y: 2, z: 4, core: 2. Of those that a mesh axis runs over, the one named last changes fastest.
Arguments:
- cell_ids: int32 [1024, 64], P('dp'), may hold values from 0 to 31
- cell_mask: int32 [1024, 64], P('dp'), may hold values from 0 to 1
- labels: int32 [1024, 64], P('dp', 'head'), may hold values from 0 to 31
- abd_weights: float32 [4096, 8, 6144], P('dp', 'head'), may hold values from -4 to 4
- abd_first: float32 [4096, 8, 6144], P('dp', 'head'), may hold values from -8.6617505e-07 to 8.6617505e-07
- abd_second: float32 [4096, 8, 6144], P('dp', 'head'), may hold values from 4.95908e-16 to 1.983632e-15
- abd_gains: float32 [2, 4096], replicated, may hold values from 0.45 to 1.65
- abd_gains_first: float32 [2, 4096], replicated, may hold values from -1.9073486e-06 to 1.9073486e-06
- abd_gains_second: float32 [2, 4096], replicated, may hold values from 7.934528e-15 to 3.173811e-14
- aba_weights: float32 [64, 768], replicated, may hold values from -4 to 4
- aba_first: float32 [64, 768], replicated, may hold values from -4.7683716e-07 to 4.7683716e-07
- aba_second: float32 [64, 768], replicated, may hold values from 4.95908e-16 to 1.983632e-15
- aba_gains: float32 [2, 64], replicated, may hold values from 0.5 to 1.5
- aba_gains_first: float32 [2, 64], replicated, may hold values from -1.9073486e-06 to 1.9073486e-06
- aba_gains_second: float32 [2, 64], replicated, may hold values from 7.934528e-15 to 3.173811e-14
- embed_table: float32 [64, 33, 64], replicated, may hold values from -6 to 6
- embed_first: float32 [64, 33, 64], replicated, may hold values from -4.7683716e-07 to 4.7683716e-07
- embed_second: float32 [64, 33, 64], replicated, may hold values from 4.95908e-16 to 1.983632e-15
- output_table: float32 [64, 64, 32], P('head'), may hold values from -0.75 to 0.75
- output_first: float32 [64, 64, 32], P('head'), may hold values from -5.281555e-07 to 5.281555e-07
- output_second: float32 [64, 64, 32], P('head'), may hold values from 4.95908e-16 to 1.983632e-15
Outputs:
- loss_sum: float32 [], replicated
- weight_total: float32 [], replicated
- grad_norm: float32 [], replicated
- abd_new: float32 [4096, 8, 6144], P('dp', 'head')
- abd_first_new: float32 [4096, 8, 6144], P('dp', 'head')
- abd_second_new: float32 [4096, 8, 6144], P('dp', 'head')
- abd_gains_new: float32 [2, 4096], replicated
- abd_gains_first_new: float32 [2, 4096], replicated
- abd_gains_second_new: float32 [2, 4096], replicated
- aba_new: float32 [64, 768], replicated
- aba_first_new: float32 [64, 768], replicated
- aba_second_new: float32 [64, 768], replicated
- aba_gains_new: float32 [2, 64], replicated
- aba_gains_first_new: float32 [2, 64], replicated
- aba_gains_second_new: float32 [2, 64], replicated
- embed_new: float32 [64, 33, 64], replicated
- embed_first_new: float32 [64, 33, 64], replicated
- embed_second_new: float32 [64, 33, 64], replicated
- output_new: float32 [64, 64, 32], P('head')
- output_first_new: float32 [64, 64, 32], P('head')
- output_second_new: float32 [64, 64, 32], P('head')
The draws below stay inside these ranges and needn't reach their ends.
All inputs are finite; a program needn't handle non-finite values.
Results may differ from the reference program's by a relative error of at most 0.017.
Values may be sent and summed in bfloat16 or wider, within the bound.
No kernel may reach another device: no remote copies, remote signals or barrier semaphores. Data moves between devices by JAX's collectives and lax.ppermute only.
A program may use at most 640 MiB of HBM per device.

```python
import math
import jax
import jax.numpy as jnp
import numpy as np
from jax import lax

F = 64
E = 64
C = 32
H = 8
AH = 8
TOK_DEV = 128
STEP = 10
D = 4096
HD = 512
FF = 16384
COLS = 6144
TOKENS = 1024
PARAMS = 201650304
N_DP = 8


def scaled_normal(key, shape, scales):
    return jnp.clip(jax.random.normal(key, shape, jnp.float32), -4.0, 4.0) * scales


def rising_factor(count, slope):
    place = (jnp.arange(count).astype(jnp.float32) + 0.5) / count
    return (1.0 + slope * place) / (1.0 + 0.5 * slope)


def draw_abd_weights(key, part):
    key = jax.random.fold_in(key, 11)
    column = jnp.arange(COLS)
    hidden_units = FF // H
    scales = jnp.where(column < 3 * HD, D ** (-0.5), jnp.where(column < 4 * HD, (TOKENS / (2.7 * D)) ** 0.5, jnp.where(column < 4 * HD + hidden_units, D ** (-0.5), 1.5 * FF ** (-0.5))))
    return scaled_normal(key, (D, H, COLS), scales.astype(jnp.float32))


def draw_aba_weights(key, part):
    key = jax.random.fold_in(key, 13)
    column = jnp.arange(12 * E)
    scales = jnp.where(column < 3 * E, E ** (-0.5), jnp.where(column < 4 * E, (F / (2.7 * E)) ** 0.5, jnp.where(column < 8 * E, E ** (-0.5), 1.5 * (4 * E) ** (-0.5))))
    return scaled_normal(key, (E, 12 * E), scales.astype(jnp.float32))


def draw_abd_gains(key, part):
    key = jax.random.fold_in(key, 12)
    column = jnp.arange(D).astype(jnp.float32)
    rising = 0.5 + (column + 0.5) / D
    noise = jax.random.uniform(key, (2, D), jnp.float32, -0.1, 0.1)
    return rising[None, :] * (1.0 + noise)


def draw_abd_first(key, part):
    key = jax.random.fold_in(key, 15)
    slope = 2.0
    scales = rising_factor(D, slope)[:, None, None] * rising_factor(H, slope)[None, :, None]
    return scaled_normal(key, (D, H, COLS), 0.0011 * PARAMS ** (-0.5) * scales)


def draw_output_first(key, part):
    key = jax.random.fold_in(key, 16)
    slope = 2.0
    scales = rising_factor(F, slope)[:, None, None]
    return scaled_normal(key, (F, E, C), 0.0011 * PARAMS ** (-0.5) * scales)


def draw_cell_mask(key, part):
    key = jax.random.fold_in(key, 14)
    row_index = jnp.arange(TOKENS, dtype=jnp.int32)[:, None]
    attr_index = jnp.arange(F, dtype=jnp.int32)[None, :]
    row_rate = (TOKENS + 2 * row_index + 1) * 1024 // (2 * TOKENS)
    attr_rate = (F + 2 * attr_index + 1) * 1024 // (2 * F)
    threshold = row_rate * attr_rate * 15 // 100
    drawn = jax.random.randint(key, (TOKENS, F), 0, 1 << 20, jnp.int32)
    return (drawn < threshold).astype(jnp.int32)


def set_ends(result, rng, smallest, largest):
    longest = result.shape.index(max(result.shape))
    spots = []
    for shift in (0, 1):
        where = [jax.random.randint(jax.random.fold_in(rng, axis), (), 0, length) for axis, length in enumerate(result.shape)]
        where[longest] = (where[longest] + shift) % result.shape[longest]
        spots.append(tuple(where))
    return result.at[spots[0]].set(smallest).at[spots[1]].set(largest)


def level_of(rng, dims, shards, least, largest):
    factor_of = 1.0
    for position, parts in shards:
        steps = jax.random.uniform(jax.random.fold_in(jax.random.fold_in(rng, 6), position), (parts,), jnp.float32, least / len(shards), largest / len(shards))
        factor_of = factor_of * jnp.repeat(jnp.exp(steps), dims[position] // parts).reshape((-1,) + (1,) * (len(dims) - 1 - position))
    return factor_of


def rank_bounds(count, skew):
    weights = [(1 << 20) // math.isqrt(standing ** skew) + 1 for standing in range(1, count + 1)]
    width = 1 + sum(weights) // (1 << 30)
    return np.cumsum(np.array([max(1, weight // width) for weight in weights]))


def ranked_ids(own_key, dims, number_of, skew):
    grid = rank_bounds(number_of, skew)
    pick = jax.random.randint(jax.random.fold_in(own_key, 1), dims, 0, int(grid[number_of - 1]))
    rank = jnp.searchsorted(jnp.asarray(grid, jnp.int32), pick, side="right")
    return jax.random.permutation(jax.random.fold_in(own_key, 2), number_of)[rank].astype(jnp.int32)


def gaussian(own_key, shape, scale, most, split=(), held_as=jnp.bfloat16):
    entries = jax.random.normal(own_key, shape, jnp.float32) * scale
    if len(split) > 0:
        entries = level_of(own_key, shape, split, -0.22, 0.18) * entries
    return jnp.clip(entries, min=-most, max=most).astype(held_as)


def setup_inputs(seed: int = 0) -> dict:
    arg_keys = jax.random.split(jax.random.key(seed), 22)
    cell_ids = set_ends(jax.random.randint(arg_keys[0], (TOKENS, F), 0, C), jax.random.fold_in(arg_keys[0], 1), 0, C - 1).astype(jnp.int32)
    cell_mask = draw_cell_mask(jax.random.fold_in(arg_keys[21], 71), 0)
    labels = set_ends(ranked_ids(arg_keys[2], (TOKENS, F), C, 2), jax.random.fold_in(arg_keys[2], 3), 0, C - 1).astype(jnp.int32)
    abd_weights = draw_abd_weights(jax.random.fold_in(arg_keys[21], 71), 0)
    abd_first = draw_abd_first(jax.random.fold_in(arg_keys[21], 71), 0)
    abd_second = jnp.clip(jnp.exp(math.log(1.9836319425822454e-15) - 1.3862944 * jax.random.uniform(arg_keys[5], (D, H, COLS), jnp.float32) ** level_of(arg_keys[5], (D, H, COLS), ((0, 8), (1, 4)), -0.2, 0.2)), 4.959079856455613e-16, 1.9836319425822454e-15)
    abd_gains = draw_abd_gains(jax.random.fold_in(arg_keys[21], 71), 0)
    abd_gains_first = gaussian(arg_keys[7], (2, D), (0.0044 / PARAMS ** 0.5), 1.9073486328125e-06, (), jnp.float32)
    abd_gains_second = jnp.clip(jnp.exp(jax.random.uniform(arg_keys[8], (2, D), jnp.float32, math.log(7.934527770328981e-15), math.log(3.1738111081315926e-14))), 7.934527770328981e-15, 3.1738111081315926e-14)
    aba_weights = draw_aba_weights(jax.random.fold_in(arg_keys[21], 71), 0)
    aba_first = gaussian(arg_keys[10], (E, 12 * E), (0.0011 / PARAMS ** 0.5), 4.76837158203125e-07, (), jnp.float32)
    aba_second = jnp.clip(jnp.exp(jax.random.uniform(arg_keys[11], (E, 12 * E), jnp.float32, math.log(4.959079856455613e-16), math.log(1.9836319425822454e-15))), 4.959079856455613e-16, 1.9836319425822454e-15)
    aba_gains = jnp.clip(1.0 + 0.1 * jax.random.normal(arg_keys[12], (2, E), jnp.float32), 0.5, 1.5)
    aba_gains_first = gaussian(arg_keys[13], (2, E), (0.0044 / PARAMS ** 0.5), 1.9073486328125e-06, (), jnp.float32)
    aba_gains_second = jnp.clip(jnp.exp(jax.random.uniform(arg_keys[14], (2, E), jnp.float32, math.log(7.934527770328981e-15), math.log(3.1738111081315926e-14))), 7.934527770328981e-15, 3.1738111081315926e-14)
    embed_table = gaussian(arg_keys[15], (F, C + 1, E), 1.0, 6.0, (), jnp.float32)
    embed_first = gaussian(arg_keys[16], (F, C + 1, E), (0.0011 / PARAMS ** 0.5), 4.76837158203125e-07, (), jnp.float32)
    embed_second = jnp.clip(jnp.exp(jax.random.uniform(arg_keys[17], (F, C + 1, E), jnp.float32, math.log(4.959079856455613e-16), math.log(1.9836319425822454e-15))), 4.959079856455613e-16, 1.9836319425822454e-15)
    output_table = gaussian(arg_keys[18], (F, E, C), E ** -0.5, 0.75, ((0, 4),), jnp.float32)
    output_first = draw_output_first(jax.random.fold_in(arg_keys[21], 71), 0)
    output_second = jnp.clip(jnp.exp(math.log(1.9836319425822454e-15) - 1.3862944 * jax.random.uniform(arg_keys[20], (F, E, C), jnp.float32) ** level_of(arg_keys[20], (F, E, C), ((0, 4),), -0.2, 0.2)), 4.959079856455613e-16, 1.9836319425822454e-15)
    return dict(cell_ids=cell_ids, cell_mask=cell_mask, labels=labels, abd_weights=abd_weights, abd_first=abd_first, abd_second=abd_second, abd_gains=abd_gains, abd_gains_first=abd_gains_first, abd_gains_second=abd_gains_second, aba_weights=aba_weights, aba_first=aba_first, aba_second=aba_second, aba_gains=aba_gains, aba_gains_first=aba_gains_first, aba_gains_second=aba_gains_second, embed_table=embed_table, embed_first=embed_first, embed_second=embed_second, output_table=output_table, output_first=output_first, output_second=output_second)


HIGH_PRECISION = lax.Precision.HIGHEST
EPS_NORM = 1e-05
CLIP_LIMIT = 0.01
LEARN_RATE = 0.3
BETA_FIRST = 0.9
BETA_SECOND = 0.999
ADAM_EPSILON = 1e-08
WEIGHT_DECAY = 0.01

@jax.custom_vjp
def low(v):
    return lax.optimization_barrier(v.astype(jnp.bfloat16)).astype(jnp.float32)

@jax.custom_vjp
def low_back(v):
    return v

def low_keep(v):
    return (low(v), None)

def low_pass(kept, grad):
    return (grad,)

def back_keep(v):
    return (v, None)

def back_low(kept, grad):
    return (low(grad),)
low.defvjp(low_keep, low_pass)
low_back.defvjp(back_keep, back_low)

def layer_norm(values, gain_row):
    center = lax.optimization_barrier(jnp.mean(values, axis=-1, keepdims=True))
    centred = values - center
    spread = lax.optimization_barrier(jnp.mean(centred * centred, axis=-1, keepdims=True))
    return centred * lax.rsqrt(spread + EPS_NORM) * gain_row

def gelu_apply(values):
    return 0.5 * values * (1.0 + lax.erf(values * 0.7071067811865476))

def exact_product(spec, left, right):
    return jnp.einsum(spec, left, right, precision=HIGH_PRECISION)

def attention(queries, key_rows, value_rows, factor):
    scores = low_back(exact_product('...qd,...kd->...qk', queries, key_rows) * factor)
    softmax_probs = low(jax.nn.softmax(scores, axis=-1))
    return exact_product('...qk,...kd->...qd', softmax_probs, value_rows)

def abd_layer(inputs, weights, gain_rows):
    up_end = 4 * HD + FF // H
    normed = low(layer_norm(inputs, gain_rows[0]))
    triple = low_back(low(exact_product('nd,dhc->hnc', normed, weights[:, :, :3 * HD])))
    queries = triple[..., :HD]
    key_rows = triple[..., HD:2 * HD]
    value_rows = triple[..., 2 * HD:]
    blocks = queries.reshape(H, N_DP, TOK_DEV, HD).transpose(1, 0, 2, 3)
    attend_block = jax.checkpoint(lambda block: attention(block, key_rows, value_rows, HD ** (-0.5)))
    attended = lax.map(attend_block, blocks).transpose(1, 0, 2, 3).reshape(H, N_DP * TOK_DEV, HD)
    attended = low_back(low(attended))
    middle = inputs + low_back(exact_product('hnj,dhj->nd', attended, weights[:, :, 3 * HD:4 * HD]))

    def feed_block(row_block):
        second = low(layer_norm(row_block, gain_rows[1]))
        before = low_back(exact_product('nd,dhu->nhu', second, weights[:, :, 4 * HD:up_end]))
        hidden = low(gelu_apply(before))
        return row_block + low_back(exact_product('nhu,dhu->nd', hidden, weights[:, :, up_end:]))
    after = lax.map(jax.checkpoint(feed_block), middle.reshape(N_DP, TOK_DEV, F * E))
    return after.reshape(N_DP * TOK_DEV, F * E)

def aba_block(row_block, weights, gain_rows):
    size = E // AH
    normed = low(layer_norm(row_block, gain_rows[0]))
    projection = weights[:, :3 * E].reshape(E, 3, AH, size)
    triple = low_back(low(exact_product('rfe,eshd->srhfd', normed, projection)))
    attended = low_back(low(attention(triple[0], triple[1], triple[2], size ** (-0.5))))
    out_proj = weights[:, 3 * E:4 * E].reshape(E, AH, size)
    middle = row_block + low_back(exact_product('rhfd,ohd->rfo', attended, out_proj))
    second = low(layer_norm(middle, gain_rows[1]))
    before = low_back(exact_product('rfe,eu->rfu', second, weights[:, 4 * E:8 * E]))
    hidden = low(gelu_apply(before))
    return middle + low_back(exact_product('rfu,ou->rfo', hidden, weights[:, 8 * E:]))

def forward(abd_w, abd_g, aba_w, aba_g, embed, output, picked, mask_float, label_hot, class_weight):
    looked_up = embed[jnp.arange(F)[None, :], picked]
    embedded = looked_up.reshape(N_DP * TOK_DEV, F * E)
    after = abd_layer(embedded, low(abd_w), abd_g)
    narrow = low(aba_w)
    final = lax.map(jax.checkpoint(lambda block: aba_block(block, narrow, aba_g)), after.reshape(N_DP, TOK_DEV, F, E))
    final = final.reshape(N_DP * TOK_DEV, F, E)
    logits = low_back(exact_product('nfe,fec->nfc', low(final), low(output)))
    log_total = jax.nn.logsumexp(logits, axis=-1)
    target_logit = lax.optimization_barrier(jnp.sum(label_hot * logits, axis=-1))
    cell_weight = mask_float * lax.optimization_barrier(jnp.sum(label_hot * class_weight[None], axis=-1))
    loss_sum = jnp.sum(cell_weight * (log_total - target_logit))
    weight_total = jnp.sum(cell_weight)
    return (loss_sum / weight_total, (loss_sum, weight_total))

def adam_step(weight, gradient, first, second, clip_factor, decay, total_sq):
    scaled = gradient * clip_factor
    first_new = BETA_FIRST * first + (1.0 - BETA_FIRST) * scaled
    second_new = BETA_SECOND * second + (1.0 - BETA_SECOND) * scaled * scaled
    update = first_new / (1.0 - BETA_FIRST ** STEP) / (jnp.sqrt(second_new / (1.0 - BETA_SECOND ** STEP)) + ADAM_EPSILON) + decay * weight
    trust_ratio = jnp.sqrt(jnp.sum(weight * weight)) / (jnp.sqrt(jnp.sum(update * update)) + 1e-06)
    return (weight - LEARN_RATE * trust_ratio * update, first_new, second_new)

def reference(cell_ids, cell_mask, labels, abd_weights, abd_first, abd_second, abd_gains, abd_gains_first, abd_gains_second, aba_weights, aba_first, aba_second, aba_gains, aba_gains_first, aba_gains_second, embed_table, embed_first, embed_second, output_table, output_first, output_second):
    mask_float = cell_mask.astype(jnp.float32)
    picked = jnp.where(cell_mask == 1, C, cell_ids).astype(jnp.int32)
    label_hot = (labels[:, :, None] == jnp.arange(C, dtype=jnp.int32)[None, None, :]).astype(jnp.float32)
    counts = exact_product('nf,nfc->fc', mask_float, label_hot)
    class_weight = lax.rsqrt(1.0 + counts)
    parameters = (abd_weights, abd_gains, aba_weights, aba_gains, embed_table, output_table)

    def objective_of(abd_w, abd_g, aba_w, aba_g, embed, output):
        return forward(abd_w, abd_g, aba_w, aba_g, embed, output, picked, mask_float, label_hot, class_weight)
    objective, pull_back, totals = jax.vjp(objective_of, *parameters, has_aux=True)
    gradients = pull_back(jnp.ones_like(objective))
    grad_norm = jnp.sqrt(sum((jnp.sum(gradient * gradient) for gradient in gradients)))
    clip_factor = jnp.minimum(1.0, CLIP_LIMIT / (grad_norm + 1e-06))
    abd_triple = adam_step(abd_weights, gradients[0], abd_first, abd_second, clip_factor, WEIGHT_DECAY, None)
    gain_triple = adam_step(abd_gains, gradients[1], abd_gains_first, abd_gains_second, clip_factor, 0.0, None)
    aba_triple = adam_step(aba_weights, gradients[2], aba_first, aba_second, clip_factor, WEIGHT_DECAY, None)
    aba_gain_triple = adam_step(aba_gains, gradients[3], aba_gains_first, aba_gains_second, clip_factor, 0.0, None)
    embed_triple = adam_step(embed_table, gradients[4], embed_first, embed_second, clip_factor, WEIGHT_DECAY, None)
    output_triple = adam_step(output_table, gradients[5], output_first, output_second, clip_factor, WEIGHT_DECAY, None)
    return (totals[0], totals[1], grad_norm, abd_triple[0], abd_triple[1], abd_triple[2], gain_triple[0], gain_triple[1], gain_triple[2], aba_triple[0], aba_triple[1], aba_triple[2], aba_gain_triple[0], aba_gain_triple[1], aba_gain_triple[2], embed_triple[0], embed_triple[1], embed_triple[2], output_triple[0], output_triple[1], output_triple[2])
```

```python
import jax
import jax.experimental.pallas as pl
import jax.experimental.pallas.tpu as pltpu
import jax.numpy as jnp
from jax import lax
from jax.sharding import Mesh
from jax.sharding import PartitionSpec as P

H = 8
AH = 8
STEP = 10
HD = 512
FF = 16384


EPS_NORM = 1e-05
CLIP_LIMIT = 0.01
LEARN_RATE = 0.3
BETA_FIRST = 0.9
BETA_SECOND = 0.999
ADAM_EPSILON = 1e-08
WEIGHT_DECAY = 0.01


def layer_norm(values, gain_row):
    center = jnp.mean(values, axis=-1, keepdims=True)
    centred = values - center
    spread = jnp.mean(centred * centred, axis=-1, keepdims=True)
    return centred * lax.rsqrt(spread + EPS_NORM) * gain_row


def gelu_apply(values):
    return 0.5 * values * (1.0 + lax.erf(values * 0.7071067811865476))


def norm_back(values, gain_row, upstream):
    unused_value, pull_back = jax.vjp(layer_norm, values, gain_row)
    return pull_back(upstream)


def gelu_back(values, upstream):
    unused_value, pull_back = jax.vjp(gelu_apply, values)
    return pull_back(upstream)[0]


def attend_keys(queries, key_rows, value_rows, factor):
    scores = (
        jnp.einsum("...qd,...kd->...qk", queries, key_rows, preferred_element_type=jnp.float32)
        * factor
    )
    highest = jnp.max(scores, axis=-1, keepdims=True)
    weights = jnp.exp(scores - highest)
    totals = jnp.sum(weights, axis=-1, keepdims=True)
    result = jnp.einsum(
        "...qk,...kd->...qd",
        (weights / totals).astype(jnp.bfloat16),
        value_rows,
        preferred_element_type=jnp.float32,
    )
    return (result, highest + jnp.log(totals))


def attend_back(queries, key_rows, value_rows, log_total, result_grad, factor):
    scores = (
        jnp.einsum("...qd,...kd->...qk", queries, key_rows, preferred_element_type=jnp.float32)
        * factor
    )
    softmax_probs = jnp.exp(scores - log_total)
    prob_grad = jnp.einsum(
        "...qd,...kd->...qk", result_grad, value_rows, preferred_element_type=jnp.float32
    )
    score_grad = softmax_probs * (
        prob_grad - jnp.sum(softmax_probs * prob_grad, axis=-1, keepdims=True)
    )
    score_grad = score_grad.astype(jnp.bfloat16)
    query_grad = (
        jnp.einsum("...qk,...kd->...qd", score_grad, key_rows, preferred_element_type=jnp.float32)
        * factor
    )
    key_grad = (
        jnp.einsum("...qk,...qd->...kd", score_grad, queries, preferred_element_type=jnp.float32)
        * factor
    )
    value_grad = jnp.einsum(
        "...qk,...qd->...kd",
        softmax_probs.astype(jnp.bfloat16),
        result_grad,
        preferred_element_type=jnp.float32,
    )
    return (query_grad, key_grad, value_grad)


def aba_forward(row_block, weights, gain_rows):
    embed_width = weights.shape[0]
    row_count = row_block.shape[0]
    attr_count = row_block.shape[1] // embed_width
    size_each = embed_width // AH
    inputs = row_block.reshape(row_count, attr_count, embed_width)
    normed = layer_norm(inputs, gain_rows[0]).astype(jnp.bfloat16)
    projection = weights[:, : 3 * embed_width].reshape(embed_width, 3, AH, size_each)
    triple = jnp.einsum(
        "rfe,eshd->srhfd", normed, projection, preferred_element_type=jnp.float32
    ).astype(jnp.bfloat16)
    attended, log_total = attend_keys(triple[0], triple[1], triple[2], size_each ** (-0.5))
    attended = attended.astype(jnp.bfloat16)
    out_proj = weights[:, 3 * embed_width : 4 * embed_width].reshape(embed_width, AH, size_each)
    middle = inputs + jnp.einsum(
        "rhfd,ohd->rfo", attended, out_proj, preferred_element_type=jnp.float32
    )
    second = layer_norm(middle, gain_rows[1]).astype(jnp.bfloat16)
    before = jnp.einsum(
        "rfe,eu->rfu",
        second,
        weights[:, 4 * embed_width : 8 * embed_width],
        preferred_element_type=jnp.float32,
    )
    hidden = gelu_apply(before).astype(jnp.bfloat16)
    after = middle + jnp.einsum(
        "rfu,ou->rfo", hidden, weights[:, 8 * embed_width :], preferred_element_type=jnp.float32
    )
    return (
        after.reshape(row_count, attr_count * embed_width),
        (inputs, normed, triple, log_total, attended, middle, second, before, hidden),
    )


def aba_backward(upstream, stored, weights, gain_rows):
    inputs, normed, triple, log_total, attended, middle, second, before, hidden = stored
    row_count, attr_count, embed_width = inputs.shape
    size_each = embed_width // AH
    upstream = upstream.reshape(row_count, attr_count, embed_width)
    down_grad = upstream.astype(jnp.bfloat16)
    hidden_grad = jnp.einsum(
        "rfo,ou->rfu", down_grad, weights[:, 8 * embed_width :], preferred_element_type=jnp.float32
    )
    before_grad = gelu_back(before, hidden_grad).astype(jnp.bfloat16)
    second_grad = jnp.einsum(
        "rfu,eu->rfe",
        before_grad,
        weights[:, 4 * embed_width : 8 * embed_width],
        preferred_element_type=jnp.float32,
    )
    middle_part, gain_two = norm_back(middle, gain_rows[1], second_grad)
    middle_grad = upstream + middle_part
    branch_grad = middle_grad.astype(jnp.bfloat16)
    out_proj = weights[:, 3 * embed_width : 4 * embed_width].reshape(embed_width, AH, size_each)
    attended_grad = jnp.einsum(
        "rfo,ohd->rhfd", branch_grad, out_proj, preferred_element_type=jnp.float32
    ).astype(jnp.bfloat16)
    query_grad, key_grad, value_grad = attend_back(
        triple[0], triple[1], triple[2], log_total, attended_grad, size_each ** (-0.5)
    )
    triple_grad = jnp.stack([query_grad, key_grad, value_grad]).astype(jnp.bfloat16)
    projection = weights[:, : 3 * embed_width].reshape(embed_width, 3, AH, size_each)
    normed_grad = jnp.einsum(
        "srhfd,eshd->rfe", triple_grad, projection, preferred_element_type=jnp.float32
    )
    input_part, gain_one = norm_back(inputs, gain_rows[0], normed_grad)
    input_grad = middle_grad + input_part
    weight_grad = jnp.concatenate(
        [
            jnp.einsum(
                "rfe,srhfd->eshd", normed, triple_grad, preferred_element_type=jnp.float32
            ).reshape(embed_width, 3 * embed_width),
            jnp.einsum(
                "rfo,rhfd->ohd", branch_grad, attended, preferred_element_type=jnp.float32
            ).reshape(embed_width, embed_width),
            jnp.einsum("rfe,rfu->eu", second, before_grad, preferred_element_type=jnp.float32),
            jnp.einsum("rfo,rfu->ou", down_grad, hidden, preferred_element_type=jnp.float32),
        ],
        axis=1,
    )
    return (
        input_grad.reshape(row_count, attr_count * embed_width),
        weight_grad,
        jnp.stack([gain_one, gain_two]),
    )


def moments_of(weight, gradient, first, second, clip_factor, decay):
    scaled = gradient * clip_factor
    first_new = BETA_FIRST * first + (1.0 - BETA_FIRST) * scaled
    second_new = BETA_SECOND * second + (1.0 - BETA_SECOND) * scaled * scaled
    update = (
        first_new
        / (1.0 - BETA_FIRST**STEP)
        / (jnp.sqrt(second_new / (1.0 - BETA_SECOND**STEP)) + ADAM_EPSILON)
        + decay * weight
    )
    return (first_new, second_new, update)


def apply_trust(weight, update, weight_sq, update_sq):
    trust_ratio = jnp.sqrt(weight_sq) / (jnp.sqrt(update_sq) + 1e-06)
    return weight - LEARN_RATE * trust_ratio * update


def local_step(weight, gradient, first, second, clip_factor, decay):
    first_new, second_new, update = moments_of(weight, gradient, first, second, clip_factor, decay)
    return (
        apply_trust(weight, update, jnp.sum(weight * weight), jnp.sum(update * update)),
        first_new,
        second_new,
    )


LOW = jnp.bfloat16
WIDE = jnp.float32
GROUP = ("x", "h")
MEMBERS = 8
FIRST_SCALE = 1.0 / (1.0 - BETA_FIRST**STEP)
SECOND_SCALE = 1.0 / (1.0 - BETA_SECOND**STEP)


def dot(left, right, left_dim=1, right_dim=0):
    return lax.dot_general(
        left, right, (((left_dim,), (right_dim,)), ((), ())), preferred_element_type=WIDE
    )


def native_view(values):
    rows, heads, columns = values.shape
    return (
        values.reshape(rows, heads, columns // 128, 128)
        .transpose(0, 2, 1, 3)
        .reshape(rows, columns // 128 * heads, 128)
    )


def from_native(values, heads):
    rows, count, width = values.shape
    return (
        values.reshape(rows, count // heads, heads, width)
        .transpose(0, 2, 1, 3)
        .reshape(rows, heads, count // heads * width)
    )


def split_kernel(side_ref, weight_ref, own_ref, other_ref):
    first = side_ref[0] == 0
    for start in range(0, weight_ref.shape[1], 8):
        turned = jnp.swapaxes(weight_ref[:, start : start + 8, :], 0, 1)
        for pair in range(4):
            lanes = pl.ds((start // 2 + pair) * 128, 128)
            left, right = turned[2 * pair], turned[2 * pair + 1]
            own_ref[:, lanes] = jnp.where(first, left, right).astype(LOW)
            other_ref[:, lanes] = jnp.where(first, right, left).astype(LOW)


def split_heads(view, side, offset, width):
    rows = view.shape[0]
    depth = width // 64
    block = 64
    return pl.pallas_call(
        split_kernel,
        out_shape=[jax.ShapeDtypeStruct((rows, width), LOW)] * 2,
        grid=(rows // block,),
        in_specs=[
            pl.BlockSpec(memory_space=pltpu.SMEM),
            pl.BlockSpec((block, depth, 128), lambda i: (i, offset // width, 0)),
        ],
        out_specs=[pl.BlockSpec((block, width), lambda i: (i, 0))] * 2,
        compiler_params=pltpu.CompilerParams(vmem_limit_bytes=40 * 2**20),
        cost_estimate=pl.CostEstimate(
            flops=rows * width * 2, bytes_accessed=rows * width * 12, transcendentals=0
        ),
    )(side, view)


def moments_kernel(side_ref, clip_ref, weight_ref, first_ref, second_ref, *rest):
    gradients, (first_out, second_out, update_out, total_ref) = rest[:-4], rest[-4:]
    first = side_ref[0] == 0
    clip = clip_ref[0]

    @pl.when(pl.program_id(0) == 0)
    def _():
        total_ref[...] = jnp.zeros_like(total_ref)

    update_sq = jnp.zeros((8, 128), WIDE)
    weight_sq = jnp.zeros((8, 128), WIDE)
    start = 0
    for own_ref, other_ref in zip(gradients[0::2], gradients[1::2]):
        for column in range(0, own_ref.shape[1], 512):
            parts = []
            for lane in range(column, column + 512, 128):
                own = own_ref[:, lane : lane + 128].astype(WIDE)
                other = other_ref[:, lane : lane + 128].astype(WIDE)
                parts += [jnp.where(first, own, other), jnp.where(first, other, own)]
            scaled = jnp.swapaxes(jnp.stack(parts, axis=0), 0, 1) * clip
            here = pl.ds(start, 8)
            weight = weight_ref[:, here, :]
            first_new = BETA_FIRST * first_ref[:, here, :] + (1.0 - BETA_FIRST) * scaled
            second_new = (
                BETA_SECOND * second_ref[:, here, :] + (1.0 - BETA_SECOND) * scaled * scaled
            )
            first_out[:, here, :] = first_new
            second_out[:, here, :] = second_new
            update = (
                first_new * FIRST_SCALE / (jnp.sqrt(second_new * SECOND_SCALE) + ADAM_EPSILON)
                + WEIGHT_DECAY * weight
            )
            update_out[:, here, :] = update.astype(update_out.dtype)
            update_sq += jnp.sum(update * update, axis=0)
            weight_sq += jnp.sum(weight * weight, axis=0)
            start += 8
    total_ref[0] += update_sq
    total_ref[1] += weight_sq


def moments_step(side, clip, weight, first, second, gradients):
    rows, depth, _ = weight.shape
    block = 32
    whole = pl.BlockSpec((block, depth, 128), lambda i: (i, 0, 0))
    shape = jax.ShapeDtypeStruct(weight.shape, WIDE)
    return pl.pallas_call(
        moments_kernel,
        out_shape=[
            shape,
            shape,
            jax.ShapeDtypeStruct(weight.shape, LOW),
            jax.ShapeDtypeStruct((2, 8, 128), WIDE),
        ],
        grid=(rows // block,),
        in_specs=[pl.BlockSpec(memory_space=pltpu.SMEM)] * 2
        + [whole] * 3
        + [pl.BlockSpec((block, g.shape[1]), lambda i: (i, 0)) for g in gradients],
        out_specs=[whole] * 3 + [pl.BlockSpec((2, 8, 128), lambda i: (0, 0, 0))],
        compiler_params=pltpu.CompilerParams(vmem_limit_bytes=48 * 2**20),
        cost_estimate=pl.CostEstimate(
            flops=weight.size * 20, bytes_accessed=weight.size * 24, transcendentals=weight.size
        ),
    )(side, clip, weight, first, second, *gradients)


class Grid:
    def __init__(self, line, share, heads):
        self.line, self.share, self.heads = line, share, heads

    def place(self):
        return lax.axis_index("z"), lax.axis_index("x"), lax.axis_index("h")

    def pair(self, values, step):
        return lax.ppermute(values, GROUP, [(i, i ^ step) for i in range(MEMBERS)])

    def along(self, values, step):
        return lax.ppermute(values, "z", [(i, i ^ step) for i in range(self.line)])

    def flip(self, values):
        if self.share == 1:
            return values
        half = values.shape[-1] // 2
        return jnp.concatenate([values[..., half:], values[..., :half]], axis=-1)

    def absolute(self, values):
        if self.share == 1:
            return values
        return jnp.where(lax.axis_index("x") == 1, self.flip(values), values)

    def crossed(self, values, step):
        return self.flip(values) if step >= self.heads else values

    def spread(self, own):
        parts = [own] + [self.crossed(self.pair(own, d), d) for d in (2, 4, 6)]
        half = jnp.concatenate(parts, axis=0)
        return jnp.concatenate([half, self.pair(half, 1)], axis=0)

    def gathered_sum(self, values):
        rows = values.shape[0] // MEMBERS
        both = values[: 4 * rows].astype(WIDE) + self.pair(values[4 * rows :], 1).astype(WIDE)
        total = both[:rows]
        for k, d in enumerate((2, 4, 6), 1):
            sent = both[k * rows : (k + 1) * rows].astype(LOW)
            total = total + self.crossed(self.pair(sent, d), d).astype(WIDE)
        return total

    def group_total(self, values):
        values = values + self.pair(values, 1)
        return values + self.pair(values, 2) + self.pair(values, 4) + self.pair(values, 6)

    def line_list(self, values):
        if self.line == 4:
            return [values] + [self.along(values, d) for d in (1, 2, 3)]
        every = lax.all_gather(values, "z", axis=0)
        return [every[i] for i in range(self.line)]

    def line_total(self, values):
        if self.line == 4:
            return sum(self.line_list(values))
        return lax.psum(values, "z")

    def total(self, values):
        return self.line_total(self.group_total(values))

    def ordered(self, parts):
        z = lax.axis_index("z")
        low, high = z % 2 == 1, z // 2 == 1
        parts = [jnp.where(low, parts[q ^ 1], parts[q]) for q in range(4)]
        return [jnp.where(high, parts[q ^ 2], parts[q]) for q in range(4)]

    def line_gather(self, values):
        if self.line == 4:
            return self.ordered(self.line_list(values))
        return self.line_list(values)

    def to_rows(self, values):
        rows = values.shape[0] // self.line
        values = self.absolute(values)
        if self.line != 4:
            return lax.all_to_all(values, "z", split_axis=0, concat_axis=1, tiled=True)
        z = lax.axis_index("z")
        blocks = values.reshape(self.line, rows, values.shape[1])
        parts = [lax.dynamic_index_in_dim(blocks, z ^ d, 0, False) for d in range(4)]
        parts = [parts[0]] + [self.along(parts[d], d) for d in (1, 2, 3)]
        return jnp.concatenate(self.ordered(parts), axis=1)

    def from_rows(self, values):
        if self.line != 4:
            moved = lax.all_to_all(values, "z", split_axis=1, concat_axis=0, tiled=True)
            return self.absolute(moved)
        z = lax.axis_index("z")
        width = values.shape[1] // self.line
        parts = [
            lax.dynamic_slice_in_dim(values, (z ^ d) * width, width, 1) for d in range(4)
        ]
        parts = [parts[0]] + [self.along(parts[d], d) for d in (1, 2, 3)]
        return self.absolute(jnp.concatenate(self.ordered(parts), axis=0))

    def line_sum(self, values, pieces=8):
        if self.line != 4:
            return lax.psum(values.astype(WIDE), "z")
        z = lax.axis_index("z")
        rows = values.shape[0] // pieces
        chunks = [values[i * rows : (i + 1) * rows] for i in range(pieces)]
        upward, downward = [(0, 1), (1, 2), (2, 3)], [(3, 2), (2, 1), (1, 0)]
        ups, downs = [], []
        for step in range(pieces + 2):
            held = [chunks[min(max(step - i, 0), pieces - 1)] for i in range(3)]
            up = lax.select_n(jnp.minimum(z, 2), *held)
            down = lax.select_n(jnp.minimum(3 - z, 2), *held)
            if step > 0:
                up = (up.astype(WIDE) + ups[-1].astype(WIDE)).astype(LOW)
                down = (down.astype(WIDE) + downs[-1].astype(WIDE)).astype(LOW)
            ups.append(lax.ppermute(up, "z", upward))
            downs.append(lax.ppermute(down, "z", downward))
        results = []
        for i in range(pieces):
            below = lax.select_n(jnp.maximum(z - 1, 0), ups[i], ups[i + 1], ups[i + 2])
            above = lax.select_n(jnp.maximum(2 - z, 0), downs[i], downs[i + 1], downs[i + 2])
            results.append(chunks[i].astype(WIDE) + below.astype(WIDE) + above.astype(WIDE))
        return jnp.concatenate(results, axis=0)

    def trade(self, values):
        return lax.ppermute(values, "x", [(0, 1), (1, 0)])

    def into(self, acts, weights):
        width = acts.shape[1] // self.share
        return sum(
            dot(acts[:, i * width : (i + 1) * width], weights[i]) for i in range(self.share)
        )

    def out_of(self, acts, weights):
        return jnp.concatenate([dot(acts, w, 1, 1) for w in weights], axis=1)

    def local(self, values, axis):
        z, x, _ = self.place()
        size = values.shape[axis] // (self.line * self.share)
        blocks = [
            lax.dynamic_slice_in_dim(values, (z * self.share + (x ^ i)) * size, size, axis)
            for i in range(self.share)
        ]
        return jnp.concatenate(blocks, axis=axis)

    def line_stats(self, values, count):
        center = jnp.mean(values, axis=1)
        spread = jnp.sum(jnp.square(values - center[:, None]), axis=1)
        parts = self.line_list(jnp.stack([center, spread]))
        mean = sum(part[0] for part in parts) / self.line
        size = count // self.line
        square = sum(part[1] + size * jnp.square(part[0] - mean) for part in parts)
        return mean[:, None], lax.rsqrt(square / count + EPS_NORM)[:, None]


def split_three(values):
    high = lax.reduce_precision(values, 8, 7)
    rest = values - high
    middle = lax.reduce_precision(rest, 8, 7)
    return high.astype(LOW), middle.astype(LOW), (rest - middle).astype(LOW)


def per_device(grid, *arguments):
    (
        cell_ids,
        cell_mask,
        labels,
        abd_weights,
        abd_first,
        abd_second,
        abd_gains,
        abd_gains_first,
        abd_gains_second,
        aba_weights,
        aba_first,
        aba_second,
        aba_gains,
        aba_gains_first,
        aba_gains_second,
        embed_table,
        embed_first,
        embed_second,
        output_table,
        output_first,
        output_second,
    ) = arguments
    z, x, h = grid.place()
    share, line = grid.share, grid.line
    attr_count, classes, embed_width = (
        embed_table.shape[0],
        output_table.shape[2],
        embed_table.shape[2],
    )
    model_width = attr_count * embed_width
    own_tokens = cell_ids.shape[0] // grid.heads
    first_device = ((z == 0) & (x == 0)).astype(WIDE)
    lead = ((z == 0) & (x == 0) & (h == 0)).astype(WIDE)
    side = x.astype(jnp.int32)[None]
    unit = FF // H
    sections = ((0, 3 * HD), (3 * HD, HD), (4 * HD, unit), (4 * HD + unit, unit))

    weights = []
    if share == 2:
        weight_view = native_view(abd_weights)
        for offset, width in sections:
            own, other = split_heads(weight_view, side, offset, width)
            weights.append([own, grid.trade(other)])
    else:
        for offset, width in sections:
            weights.append([abd_weights[:, 0, offset : offset + width].astype(LOW)])
    qkv_w, out_w, up_w, down_w = weights

    def own_rows(values):
        return lax.dynamic_slice_in_dim(values, h * own_tokens, own_tokens, 0)

    picked = own_rows(jnp.where(cell_mask == 1, classes, cell_ids)).astype(LOW)
    picked = grid.local(jnp.concatenate(grid.line_gather(picked), axis=0), 1)
    picked = grid.spread(picked)
    local_attrs = picked.shape[1]
    entries = classes + 1
    table_rows = jnp.arange(local_attrs * entries, dtype=jnp.int32)
    row_attr, row_entry = table_rows // entries, table_rows % entries
    expand = (jnp.arange(local_attrs, dtype=jnp.int32)[:, None] == row_attr[None, :]).astype(LOW)
    hot = (dot(picked, expand) == row_entry.astype(WIDE)[None, :]).astype(LOW)
    own_block = row_attr[:, None] == (
        jnp.arange(local_attrs * embed_width, dtype=jnp.int32) // embed_width
    )
    table_local = grid.local(embed_table, 0).reshape(local_attrs * entries, embed_width)
    table_wide = jnp.where(own_block, jnp.tile(table_local, (1, local_attrs)), 0.0)
    high, middle_bits, low_bits = split_three(table_wide)
    embedded = dot(
        jnp.concatenate([hot, hot, hot], axis=1),
        jnp.concatenate([high, middle_bits, low_bits], axis=0),
    )
    tokens = embedded.shape[0]
    held = tokens // MEMBERS

    mask_own = own_rows(cell_mask).astype(WIDE)
    labels_own = own_rows(lax.all_gather(labels, "h", axis=1, tiled=True))
    label_hot = (labels_own[:, :, None] == jnp.arange(classes, dtype=jnp.int32)).astype(WIDE)
    counts = lax.psum(jnp.sum(mask_own[:, :, None] * label_hot, axis=0), ("z", "x", "h"))
    class_weight = lax.rsqrt(1.0 + counts)
    weight_total = jnp.sum(counts * class_weight)
    output_low = lax.all_gather(output_table.astype(LOW), "h", axis=0, tiled=True)

    gains = grid.local(abd_gains, 1)
    mean_one, scale_one = grid.line_stats(embedded, model_width)
    hat_one = (embedded - mean_one) * scale_one
    normed = (hat_one * gains[0]).astype(LOW)
    triple = grid.line_sum(grid.into(normed, qkv_w).astype(LOW)).astype(LOW)
    queries, key_rows, value_rows = triple[:, :HD], triple[:, HD : 2 * HD], triple[:, 2 * HD :]
    factor = HD ** (-0.5)
    scores = dot(queries, key_rows, 1, 1) * factor
    shifted = jnp.exp(scores - jnp.max(scores, axis=1, keepdims=True))
    probs = shifted / jnp.sum(shifted, axis=1, keepdims=True)
    probs_low = probs.astype(LOW)
    attended = dot(probs_low, value_rows).astype(LOW)
    middle = embedded[:held] + grid.gathered_sum(grid.out_of(attended, out_w).astype(LOW))
    mean_two, scale_two = grid.line_stats(middle, model_width)
    hat_two = (middle - mean_two) * scale_two
    second = grid.spread((hat_two * gains[1]).astype(LOW))
    before = grid.line_sum(grid.into(second, up_w).astype(LOW))
    hidden = gelu_apply(before).astype(LOW)
    after = middle + grid.gathered_sum(grid.out_of(hidden, down_w).astype(LOW))

    aba_low = aba_weights.astype(LOW)
    final, aba_stored = aba_forward(grid.to_rows(after), aba_low, aba_gains)
    final_low = final.reshape(own_tokens, attr_count, embed_width).astype(LOW)
    logits = jnp.einsum("tfe,fec->tfc", final_low, output_low, preferred_element_type=WIDE)
    highest = jnp.max(logits, axis=-1, keepdims=True)
    exped = jnp.exp(logits - highest)
    totals = jnp.sum(exped, axis=-1, keepdims=True)
    log_total = (highest + jnp.log(totals))[:, :, 0]
    cell_weight = mask_own * jnp.sum(label_hot * class_weight[None], axis=-1)
    loss_local = jnp.sum(cell_weight * (log_total - jnp.sum(label_hot * logits, axis=-1)))
    logit_grad = ((cell_weight / weight_total)[:, :, None] * (exped / totals - label_hot)).astype(
        LOW
    )
    final_grad = jnp.einsum("tfc,fec->tfe", logit_grad, output_low, preferred_element_type=WIDE)
    output_part = jnp.einsum("tfe,tfc->fec", final_low, logit_grad, preferred_element_type=WIDE)
    rows_grad, aba_grad, aba_gains_grad = aba_backward(
        final_grad.reshape(own_tokens, model_width), aba_stored, aba_low, aba_gains
    )
    aba_grad, aba_gains_grad = lax.psum((aba_grad, aba_gains_grad), ("z", "x", "h"))
    output_grad = lax.psum(
        lax.psum_scatter(output_part, "h", scatter_dimension=0, tiled=True), ("z", "x")
    )

    upstream = grid.from_rows(rows_grad.astype(LOW))
    down_grad = grid.spread(upstream)
    hidden_grad = grid.line_sum(grid.into(down_grad, down_w).astype(LOW))
    before_grad = gelu_back(before, hidden_grad).astype(LOW)
    second_grad = grid.gathered_sum(grid.out_of(before_grad, up_w).astype(LOW))
    gained = second_grad * gains[1]
    sums = grid.line_total(jnp.stack([jnp.sum(gained, axis=1), jnp.sum(gained * hat_two, axis=1)]))
    sums = sums / model_width
    middle_grad = upstream.astype(WIDE) + scale_two * (
        gained - sums[0][:, None] - hat_two * sums[1][:, None]
    )
    gain_two = jnp.sum(second_grad * hat_two, axis=0)
    branch_grad = grid.spread(middle_grad.astype(LOW))
    attended_grad = grid.line_sum(grid.into(branch_grad, out_w).astype(LOW)).astype(LOW)
    prob_grad = dot(attended_grad, value_rows, 1, 1)
    score_grad = probs * (prob_grad - jnp.sum(probs * prob_grad, axis=1, keepdims=True))
    score_grad = score_grad.astype(LOW)
    query_grad = dot(score_grad, key_rows) * factor
    key_grad = dot(score_grad, queries, 0, 0) * factor
    value_grad = dot(probs_low, attended_grad, 0, 0)
    triple_grad = jnp.concatenate([query_grad, key_grad, value_grad], axis=1).astype(LOW)

    width = normed.shape[1] // share
    gradients, gradient_sq = [], 0.0
    for acts, upper in (
        (down_grad, hidden),
        (second, before_grad),
        (branch_grad, attended),
        (normed, triple_grad),
    ):
        parts = [
            dot(acts[:, i * width : (i + 1) * width], upper, 0, 0).astype(LOW)
            for i in range(share)
        ]
        for part in parts:
            gradient_sq = gradient_sq + jnp.sum(jnp.square(part.astype(WIDE)))
        if share == 2:
            parts[1] = grid.trade(parts[1])
        gradients = parts + gradients

    normed_grad = grid.out_of(triple_grad, qkv_w)
    gained = normed_grad * gains[0]
    sums = jnp.stack([jnp.sum(gained, axis=1), jnp.sum(gained * hat_one, axis=1)])
    places = (0, 2, 4, 6, 1, 3, 5, 7)
    own_sums = sums[:, :held]
    for k in range(1, MEMBERS):
        own_sums = own_sums + grid.pair(sums[:, k * held : (k + 1) * held], places[k])
    own_sums = grid.line_total(own_sums) / model_width
    gain_one = jnp.sum(normed_grad * hat_one, axis=0)
    own_part = middle_grad - scale_one[:held] * (
        own_sums[0][:, None] + hat_one[:held] * own_sums[1][:, None]
    )
    spread_grad = scale_one * gained
    table_grad = 0.0
    for piece in split_three(spread_grad)[:2]:
        table_grad = table_grad + dot(hot, piece, 0, 0)
    for piece in split_three(own_part)[:2]:
        table_grad = table_grad + dot(hot[:held], piece, 0, 0)
    fold = (
        jnp.arange(local_attrs * embed_width, dtype=jnp.int32)[:, None] % embed_width
        == jnp.arange(embed_width, dtype=jnp.int32)
    ).astype(WIDE)
    table_grad = jnp.dot(
        jnp.where(own_block, table_grad, 0.0), fold, precision=lax.Precision.HIGHEST
    )
    table_grad = table_grad.reshape(share, -1)
    gain_grad = jnp.stack([gain_one, gain_two]).reshape(2, share, -1).transpose(1, 0, 2)
    packed = jnp.concatenate([table_grad, gain_grad.reshape(share, -1)], axis=1)
    if share == 2:
        packed = jnp.where(x == 1, packed[::-1], packed)
    table_size = table_grad.shape[1]
    packed = packed.reshape(-1, 128)
    packed = jnp.stack(grid.line_gather(grid.group_total(packed)))
    packed = packed.reshape(line * share, -1)
    embed_grad = packed[:, :table_size].reshape(embed_table.shape)
    abd_gains_grad = (
        packed[:, table_size:].reshape(line * share, 2, -1).transpose(1, 0, 2).reshape(2, -1)
    )

    output_sq = first_device * jnp.sum(output_grad * output_grad)
    summed = grid.total(jnp.stack([gradient_sq, output_sq, loss_local]))
    replicated_sq = (
        jnp.sum(abd_gains_grad * abd_gains_grad)
        + jnp.sum(aba_grad * aba_grad)
        + jnp.sum(aba_gains_grad * aba_gains_grad)
        + jnp.sum(embed_grad * embed_grad)
    )
    grad_norm = jnp.sqrt(summed[0] + summed[1] + replicated_sq)
    loss_sum = summed[2]
    clip_factor = jnp.minimum(1.0, CLIP_LIMIT / (grad_norm + 1e-06))
    if share == 2:
        first_view, second_view, abd_update, squares = moments_step(
            side,
            clip_factor[None],
            weight_view,
            native_view(abd_first),
            native_view(abd_second),
            gradients,
        )
        abd_first_new = from_native(first_view, share)
        abd_second_new = from_native(second_view, share)
        abd_update_sq, abd_weight_sq = jnp.sum(squares[0]), jnp.sum(squares[1])
    else:
        abd_grad = jnp.concatenate(gradients, axis=1)[:, None, :].astype(WIDE)
        abd_first_new, abd_second_new, abd_update = moments_of(
            abd_weights, abd_grad, abd_first, abd_second, clip_factor, WEIGHT_DECAY
        )
        abd_update_sq, abd_weight_sq = (
            jnp.sum(abd_update * abd_update),
            jnp.sum(abd_weights * abd_weights),
        )
    output_first_new, output_second_new, output_update = moments_of(
        output_table, output_grad, output_first, output_second, clip_factor, WEIGHT_DECAY
    )
    trust_sums = grid.total(
        jnp.stack(
            [
                abd_update_sq,
                first_device * jnp.sum(output_update * output_update),
                abd_weight_sq,
                first_device * jnp.sum(output_table * output_table),
            ]
        )
    )
    if share == 2:
        abd_new = from_native(
            apply_trust(weight_view, abd_update.astype(WIDE), trust_sums[2], trust_sums[0]), share
        )
    else:
        abd_new = apply_trust(abd_weights, abd_update, trust_sums[2], trust_sums[0])
    output_new = apply_trust(output_table, output_update, trust_sums[3], trust_sums[1])
    gain_triple = local_step(
        abd_gains, abd_gains_grad, abd_gains_first, abd_gains_second, clip_factor, 0.0
    )
    aba_triple = local_step(aba_weights, aba_grad, aba_first, aba_second, clip_factor, WEIGHT_DECAY)
    aba_gain_triple = local_step(
        aba_gains, aba_gains_grad, aba_gains_first, aba_gains_second, clip_factor, 0.0
    )
    embed_triple = local_step(
        embed_table, embed_grad, embed_first, embed_second, clip_factor, WEIGHT_DECAY
    )
    return (
        loss_sum,
        weight_total,
        grad_norm,
        abd_new,
        abd_first_new,
        abd_second_new,
        *gain_triple,
        *aba_triple,
        *aba_gain_triple,
        *embed_triple,
        output_new,
        output_first_new,
        output_second_new,
    )


def solution(mesh):
    rows, heads = mesh.shape["dp"], mesh.shape["head"]
    share = H // heads
    line = rows // share
    devices = Mesh(mesh.devices.reshape(line, share, heads), ("z", "x", "h"))
    tokens, table = P(("z", "x"), None), P("h", None, None)
    weight = P(("z", "x"), "h", None)
    in_specs = (
        (tokens, tokens, P(("z", "x"), "h"), weight, weight, weight) + (P(),) * 12 + (table,) * 3
    )
    out_specs = (P(),) * 3 + (weight,) * 3 + (P(),) * 12 + (table,) * 3

    def step(*arguments):
        return per_device(Grid(line, share, heads), *arguments)

    return jax.shard_map(
        step, mesh=devices, in_specs=in_specs, out_specs=out_specs, check_vma=False
    )
```

```python
import functools

import jax
import jax.experimental.pallas as pl
import jax.experimental.pallas.tpu as pltpu
import jax.numpy as jnp
from jax import lax
from jax.sharding import Mesh
from jax.sharding import PartitionSpec as P

H = 8
AH = 8
STEP = 10
HD = 512
FF = 16384


EPS_NORM = 1e-05
CLIP_LIMIT = 0.01
LEARN_RATE = 0.3
BETA_FIRST = 0.9
BETA_SECOND = 0.999
ADAM_EPSILON = 1e-08
WEIGHT_DECAY = 0.01


def layer_norm(values, gain_row):
    center = jnp.mean(values, axis=-1, keepdims=True)
    centred = values - center
    spread = jnp.mean(centred * centred, axis=-1, keepdims=True)
    return centred * lax.rsqrt(spread + EPS_NORM) * gain_row


def gelu_apply(values):
    return 0.5 * values * (1.0 + lax.erf(values * 0.7071067811865476))


def norm_back(values, gain_row, upstream):
    unused_value, pull_back = jax.vjp(layer_norm, values, gain_row)
    return pull_back(upstream)


def gelu_back(values, upstream):
    unused_value, pull_back = jax.vjp(gelu_apply, values)
    return pull_back(upstream)[0]


def attend_keys(queries, key_rows, value_rows, factor):
    scores = (
        jnp.einsum("...qd,...kd->...qk", queries, key_rows, preferred_element_type=jnp.float32)
        * factor
    )
    highest = jnp.max(scores, axis=-1, keepdims=True)
    weights = jnp.exp(scores - highest)
    totals = jnp.sum(weights, axis=-1, keepdims=True)
    result = jnp.einsum(
        "...qk,...kd->...qd",
        (weights / totals).astype(jnp.bfloat16),
        value_rows,
        preferred_element_type=jnp.float32,
    )
    return (result, highest + jnp.log(totals))


def attend_back(queries, key_rows, value_rows, log_total, result_grad, factor):
    scores = (
        jnp.einsum("...qd,...kd->...qk", queries, key_rows, preferred_element_type=jnp.float32)
        * factor
    )
    softmax_probs = jnp.exp(scores - log_total)
    prob_grad = jnp.einsum(
        "...qd,...kd->...qk", result_grad, value_rows, preferred_element_type=jnp.float32
    )
    score_grad = softmax_probs * (
        prob_grad - jnp.sum(softmax_probs * prob_grad, axis=-1, keepdims=True)
    )
    score_grad = score_grad.astype(jnp.bfloat16)
    query_grad = (
        jnp.einsum("...qk,...kd->...qd", score_grad, key_rows, preferred_element_type=jnp.float32)
        * factor
    )
    key_grad = (
        jnp.einsum("...qk,...qd->...kd", score_grad, queries, preferred_element_type=jnp.float32)
        * factor
    )
    value_grad = jnp.einsum(
        "...qk,...qd->...kd",
        softmax_probs.astype(jnp.bfloat16),
        result_grad,
        preferred_element_type=jnp.float32,
    )
    return (query_grad, key_grad, value_grad)


def aba_forward(row_block, weights, gain_rows):
    embed_width = weights.shape[0]
    row_count = row_block.shape[0]
    attr_count = row_block.shape[1] // embed_width
    size_each = embed_width // AH
    inputs = row_block.reshape(row_count, attr_count, embed_width)
    normed = layer_norm(inputs, gain_rows[0]).astype(jnp.bfloat16)
    projection = weights[:, : 3 * embed_width].reshape(embed_width, 3, AH, size_each)
    triple = jnp.einsum(
        "rfe,eshd->srhfd", normed, projection, preferred_element_type=jnp.float32
    ).astype(jnp.bfloat16)
    attended, log_total = attend_keys(triple[0], triple[1], triple[2], size_each ** (-0.5))
    attended = attended.astype(jnp.bfloat16)
    out_proj = weights[:, 3 * embed_width : 4 * embed_width].reshape(embed_width, AH, size_each)
    middle = inputs + jnp.einsum(
        "rhfd,ohd->rfo", attended, out_proj, preferred_element_type=jnp.float32
    )
    second = layer_norm(middle, gain_rows[1]).astype(jnp.bfloat16)
    before = jnp.einsum(
        "rfe,eu->rfu",
        second,
        weights[:, 4 * embed_width : 8 * embed_width],
        preferred_element_type=jnp.float32,
    )
    hidden = gelu_apply(before).astype(jnp.bfloat16)
    after = middle + jnp.einsum(
        "rfu,ou->rfo", hidden, weights[:, 8 * embed_width :], preferred_element_type=jnp.float32
    )
    return (
        after.reshape(row_count, attr_count * embed_width),
        (inputs, normed, triple, log_total, attended, middle, second, before, hidden),
    )


def aba_backward(upstream, stored, weights, gain_rows):
    inputs, normed, triple, log_total, attended, middle, second, before, hidden = stored
    row_count, attr_count, embed_width = inputs.shape
    size_each = embed_width // AH
    upstream = upstream.reshape(row_count, attr_count, embed_width)
    down_grad = upstream.astype(jnp.bfloat16)
    hidden_grad = jnp.einsum(
        "rfo,ou->rfu", down_grad, weights[:, 8 * embed_width :], preferred_element_type=jnp.float32
    )
    before_grad = gelu_back(before, hidden_grad).astype(jnp.bfloat16)
    second_grad = jnp.einsum(
        "rfu,eu->rfe",
        before_grad,
        weights[:, 4 * embed_width : 8 * embed_width],
        preferred_element_type=jnp.float32,
    )
    middle_part, gain_two = norm_back(middle, gain_rows[1], second_grad)
    middle_grad = upstream + middle_part
    branch_grad = middle_grad.astype(jnp.bfloat16)
    out_proj = weights[:, 3 * embed_width : 4 * embed_width].reshape(embed_width, AH, size_each)
    attended_grad = jnp.einsum(
        "rfo,ohd->rhfd", branch_grad, out_proj, preferred_element_type=jnp.float32
    ).astype(jnp.bfloat16)
    query_grad, key_grad, value_grad = attend_back(
        triple[0], triple[1], triple[2], log_total, attended_grad, size_each ** (-0.5)
    )
    triple_grad = jnp.stack([query_grad, key_grad, value_grad]).astype(jnp.bfloat16)
    projection = weights[:, : 3 * embed_width].reshape(embed_width, 3, AH, size_each)
    normed_grad = jnp.einsum(
        "srhfd,eshd->rfe", triple_grad, projection, preferred_element_type=jnp.float32
    )
    input_part, gain_one = norm_back(inputs, gain_rows[0], normed_grad)
    input_grad = middle_grad + input_part
    weight_grad = jnp.concatenate(
        [
            jnp.einsum(
                "rfe,srhfd->eshd", normed, triple_grad, preferred_element_type=jnp.float32
            ).reshape(embed_width, 3 * embed_width),
            jnp.einsum(
                "rfo,rhfd->ohd", branch_grad, attended, preferred_element_type=jnp.float32
            ).reshape(embed_width, embed_width),
            jnp.einsum("rfe,rfu->eu", second, before_grad, preferred_element_type=jnp.float32),
            jnp.einsum("rfo,rfu->ou", down_grad, hidden, preferred_element_type=jnp.float32),
        ],
        axis=1,
    )
    return (
        input_grad.reshape(row_count, attr_count * embed_width),
        weight_grad,
        jnp.stack([gain_one, gain_two]),
    )


def moments_of(weight, gradient, first, second, clip_factor, decay):
    scaled = gradient * clip_factor
    first_new = BETA_FIRST * first + (1.0 - BETA_FIRST) * scaled
    second_new = BETA_SECOND * second + (1.0 - BETA_SECOND) * scaled * scaled
    update = (
        first_new
        / (1.0 - BETA_FIRST**STEP)
        / (jnp.sqrt(second_new / (1.0 - BETA_SECOND**STEP)) + ADAM_EPSILON)
        + decay * weight
    )
    return (first_new, second_new, update)


def apply_trust(weight, update, weight_sq, update_sq):
    trust_ratio = jnp.sqrt(weight_sq) / (jnp.sqrt(update_sq) + 1e-06)
    return weight - LEARN_RATE * trust_ratio * update


def local_step(weight, gradient, first, second, clip_factor, decay):
    first_new, second_new, update = moments_of(weight, gradient, first, second, clip_factor, decay)
    return (
        apply_trust(weight, update, jnp.sum(weight * weight), jnp.sum(update * update)),
        first_new,
        second_new,
    )


LOW = jnp.bfloat16
WIDE = jnp.float32
SHARERS = 4
FIRST_SCALE = 1.0 / (1.0 - BETA_FIRST**STEP)
SECOND_SCALE = 1.0 / (1.0 - BETA_SECOND**STEP)
UNITS = FF // H
SECTIONS = ((0, 3, HD), (3 * HD, 1, HD), (4 * HD, 1, UNITS), (4 * HD + UNITS, 1, UNITS))


def dot(left, right, left_dim=1, right_dim=0):
    return lax.dot_general(
        left, right, (((left_dim,), (right_dim,)), ((), ())), preferred_element_type=WIDE
    )


def native_view(values):
    rows, heads, columns = values.shape
    return (
        values.reshape(rows, heads, columns // 128, 128)
        .transpose(0, 2, 1, 3)
        .reshape(rows, columns // 128 * heads, 128)
    )


def from_native(values, heads):
    rows, count, width = values.shape
    return (
        values.reshape(rows, count // heads, heads, width)
        .transpose(0, 2, 1, 3)
        .reshape(rows, heads, count // heads * width)
    )


def tile_pairs(parts, width):
    each = width // 128
    return [
        (part * each + i, part * each + each // 2 + i)
        for part in range(parts)
        for i in range(each // 2)
    ]


def exchange(flag, left, right):
    return jnp.where(flag, right, left), jnp.where(flag, left, right)


def cross(q_flag, p_flag, values):
    a, b = exchange(p_flag, values[0], values[1])
    c, d = exchange(p_flag, values[2], values[3])
    a, c = exchange(q_flag, a, c)
    b, d = exchange(q_flag, b, d)
    return a, b, c, d


def split_kernel(parts, width, side_ref, weight_ref, *out_refs):
    q_flag, p_flag = side_ref[0] == 1, side_ref[1] == 1
    turned = {}
    for tile, (left, right) in enumerate(tile_pairs(parts, width)):
        for place in (left, right):
            group = place // 4
            if group not in turned:
                turned[group] = jnp.swapaxes(weight_ref[:, group * 8 : group * 8 + 8, :], 0, 1)
        values = [turned[t // 4][t % 4 * 2 + head] for head in range(2) for t in (left, right)]
        lanes = pl.ds(tile * 128, 128)
        for ref, value in zip(out_refs, cross(q_flag, p_flag, values)):
            ref[:, lanes] = value.astype(LOW)


def split_weights(view, side, offset, parts, width):
    rows = view.shape[0]
    total = parts * width
    depth = total // 64
    block = 32
    return pl.pallas_call(
        functools.partial(split_kernel, parts, width),
        out_shape=[jax.ShapeDtypeStruct((rows, total // 2), LOW)] * SHARERS,
        grid=(rows // block,),
        in_specs=[
            pl.BlockSpec(memory_space=pltpu.SMEM),
            pl.BlockSpec((block, depth, 128), lambda i: (i, offset // total, 0)),
        ],
        out_specs=[pl.BlockSpec((block, total // 2), lambda i: (i, 0))] * SHARERS,
        compiler_params=pltpu.CompilerParams(vmem_limit_bytes=40 * 2**20),
        cost_estimate=pl.CostEstimate(
            flops=rows * total * 2, bytes_accessed=rows * total * 12, transcendentals=0
        ),
    )(side, view)


def moments_kernel(side_ref, clip_ref, weight_ref, first_ref, second_ref, *rest):
    gradients, (first_out, second_out, update_out, total_ref) = rest[:-4], rest[-4:]
    q_flag, p_flag = side_ref[0] == 1, side_ref[1] == 1
    clip = clip_ref[0]

    @pl.when(pl.program_id(0) == 0)
    def _():
        total_ref[...] = jnp.zeros_like(total_ref)

    update_sq = jnp.zeros((8, 128), WIDE)
    weight_sq = jnp.zeros((8, 128), WIDE)
    for index, (offset, parts, width) in enumerate(SECTIONS):
        refs = gradients[SHARERS * index : SHARERS * (index + 1)]
        places = {}
        for tile, (left, right) in enumerate(tile_pairs(parts, width)):
            values = [ref[:, tile * 128 : tile * 128 + 128].astype(WIDE) for ref in refs]
            a, b, c, d = cross(q_flag, p_flag, values)
            places[2 * left], places[2 * right] = a, b
            places[2 * left + 1], places[2 * right + 1] = c, d
            for group in (left // 4, right // 4):
                rows = range(group * 8, group * 8 + 8)
                if any(row not in places for row in rows):
                    continue
                scaled = jnp.swapaxes(jnp.stack([places.pop(r) for r in rows], axis=0), 0, 1) * clip
                here = pl.ds(offset // 64 + group * 8, 8)
                weight = weight_ref[:, here, :]
                first_new = BETA_FIRST * first_ref[:, here, :] + (1.0 - BETA_FIRST) * scaled
                second_new = (
                    BETA_SECOND * second_ref[:, here, :] + (1.0 - BETA_SECOND) * scaled * scaled
                )
                first_out[:, here, :] = first_new
                second_out[:, here, :] = second_new
                update = (
                    first_new * FIRST_SCALE / (jnp.sqrt(second_new * SECOND_SCALE) + ADAM_EPSILON)
                    + WEIGHT_DECAY * weight
                )
                update_out[:, here, :] = update.astype(update_out.dtype)
                update_sq += jnp.sum(update * update, axis=0)
                weight_sq += jnp.sum(weight * weight, axis=0)
    total_ref[0] += update_sq
    total_ref[1] += weight_sq


def moments_step(side, clip, weight, first, second, gradients):
    rows, depth, _ = weight.shape
    block = 32
    whole = pl.BlockSpec((block, depth, 128), lambda i: (i, 0, 0))
    shape = jax.ShapeDtypeStruct(weight.shape, WIDE)
    return pl.pallas_call(
        moments_kernel,
        out_shape=[
            shape,
            shape,
            jax.ShapeDtypeStruct(weight.shape, LOW),
            jax.ShapeDtypeStruct((2, 8, 128), WIDE),
        ],
        grid=(rows // block,),
        in_specs=[pl.BlockSpec(memory_space=pltpu.SMEM)] * 2
        + [whole] * 3
        + [pl.BlockSpec((block, g.shape[1]), lambda i: (i, 0)) for g in gradients],
        out_specs=[whole] * 3 + [pl.BlockSpec((2, 8, 128), lambda i: (0, 0, 0))],
        compiler_params=pltpu.CompilerParams(vmem_limit_bytes=48 * 2**20),
        cost_estimate=pl.CostEstimate(
            flops=weight.size * 20, bytes_accessed=weight.size * 24, transcendentals=weight.size
        ),
    )(side, clip, weight, first, second, *gradients)


class Grid:
    def __init__(self, rows, heads):
        self.rows, self.heads = rows // SHARERS, heads
        self.each = H // heads
        self.parts = SHARERS // self.each
        self.members = SHARERS * heads
        self.shape = (self.rows, self.each, self.parts, heads)
        self.evens = range(2, self.members, 2)

    def sharer(self):
        return lax.axis_index("q") * self.parts + lax.axis_index("p")

    def pair(self, values, step):
        return lax.ppermute(values, ("q", "p", "h"), [(i, i ^ step) for i in range(self.members)])

    def trade(self, values, step):
        return lax.ppermute(values, ("q", "p"), [(i, i ^ step) for i in range(SHARERS)])

    def moved(self, values, step):
        turn = step // self.heads
        if turn == 0:
            return values
        blocks = jnp.split(values, SHARERS, axis=-1)
        return jnp.concatenate([blocks[j ^ turn] for j in range(SHARERS)], axis=-1)

    def spread(self, own):
        parts = [own] + [self.moved(self.pair(own, d), d) for d in self.evens]
        half = jnp.concatenate(parts, axis=0)
        return half, self.pair(half, 1)

    def gathered_sum(self, half, other):
        rows = half.shape[0] // (self.members // 2)
        both = half.astype(WIDE) + self.pair(other, 1).astype(WIDE)
        total = both[:rows]
        for k, d in enumerate(self.evens, 1):
            sent = both[k * rows : (k + 1) * rows].astype(LOW)
            total = total + self.moved(self.pair(sent, d), d).astype(WIDE)
        return total

    def group_total(self, values):
        step = 1
        while step < self.members:
            values = values + self.pair(values, step)
            step *= 2
        return values

    def facing(self, values):
        return lax.ppermute(values, "a", [(0, 1), (1, 0)])

    def row_list(self, values):
        if self.rows == 2:
            return [values, self.facing(values)]
        every = lax.all_gather(values, "a", axis=0)
        return [every[i] for i in range(self.rows)]

    def row_gather(self, values):
        parts = self.row_list(values)
        if self.rows == 2:
            flag = lax.axis_index("a") == 1
            parts = exchange(flag, *parts)
        return list(parts)

    def row_sum(self, values):
        if self.rows == 2:
            return values.astype(WIDE) + self.facing(values).astype(WIDE)
        return lax.psum(values.astype(WIDE), "a")

    def total(self, values):
        return self.row_sum(self.group_total(values))

    def ordered(self, parts):
        place = self.sharer()
        low, high = place % 2 == 1, place // 2 == 1
        parts = [jnp.where(low, parts[j ^ 1], parts[j]) for j in range(SHARERS)]
        return [jnp.where(high, parts[j ^ 2], parts[j]) for j in range(SHARERS)]

    def absolute(self, values):
        return jnp.concatenate(self.ordered(jnp.split(values, SHARERS, axis=-1)), axis=-1)

    def to_rows(self, values):
        values = self.absolute(values)
        if self.rows != 2:
            return lax.all_to_all(values, "a", split_axis=0, concat_axis=1, tiled=True)
        flag = lax.axis_index("a") == 1
        kept, sent = exchange(flag, *jnp.split(values, 2, axis=0))
        return jnp.concatenate(exchange(flag, kept, self.facing(sent)), axis=1)

    def from_rows(self, values):
        if self.rows != 2:
            return self.absolute(
                lax.all_to_all(values, "a", split_axis=1, concat_axis=0, tiled=True)
            )
        flag = lax.axis_index("a") == 1
        kept, sent = exchange(flag, *jnp.split(values, 2, axis=1))
        moved = jnp.concatenate(exchange(flag, kept, self.facing(sent)), axis=0)
        return self.absolute(moved)

    def renamed(self, values, step):
        block = values.shape[0] // self.members
        span = 1
        while span < self.members // 2:
            if step // 2 & span:
                halves = values.reshape(-1, 2, span * block, values.shape[1])
                values = jnp.stack([halves[:, 1], halves[:, 0]], axis=1).reshape(values.shape)
            span *= 2
        return values

    def columns(self, values):
        found = [values]
        for d in range(1, self.parts):
            got = lax.ppermute(values, "p", [(i, i ^ d) for i in range(self.parts)])
            found.append(self.renamed(got, d * self.heads))
        return jnp.concatenate(found, axis=1)

    def local(self, values, axis):
        size = values.shape[axis] // (self.rows * SHARERS)
        first, place = lax.axis_index("a") * SHARERS, self.sharer()
        return [
            lax.dynamic_slice_in_dim(values, (first + (place ^ j)) * size, size, axis)
            for j in range(SHARERS)
        ]

    def stats(self, values, count):
        center = jnp.mean(values, axis=1)
        spread = jnp.sum(jnp.square(values - center[:, None]), axis=1)
        parts = self.row_list(jnp.stack([center, spread]))
        mean = sum(part[0] for part in parts) / self.rows
        size = count // self.rows
        square = sum(part[1] + size * jnp.square(part[0] - mean) for part in parts)
        return mean[:, None], lax.rsqrt(square / count + EPS_NORM)[:, None]

    def split_plain(self, values, parts, width):
        rows = values.shape[0]
        values = values.astype(LOW).reshape(rows, self.each, parts, self.parts, -1)
        values = values.transpose(1, 3, 0, 2, 4).reshape(SHARERS, rows, -1)
        return [
            lax.dynamic_index_in_dim(values, self.sharer() ^ j, 0, False) for j in range(SHARERS)
        ]

    def merge_plain(self, pieces, parts, width):
        values = jnp.stack(self.ordered(pieces))
        rows = values.shape[1]
        values = values.reshape(self.each, self.parts, rows, parts, -1)
        return values.transpose(2, 0, 3, 1, 4).reshape(rows, self.each, parts * width)


def tied(*values):
    return lax.optimization_barrier(values)


def split_three(values):
    high = lax.reduce_precision(values, 8, 7)
    rest = values - high
    middle = lax.reduce_precision(rest, 8, 7)
    return high.astype(LOW), middle.astype(LOW), (rest - middle).astype(LOW)


def per_device(grid, *arguments):
    (
        cell_ids,
        cell_mask,
        labels,
        abd_weights,
        abd_first,
        abd_second,
        abd_gains,
        abd_gains_first,
        abd_gains_second,
        aba_weights,
        aba_first,
        aba_second,
        aba_gains,
        aba_gains_first,
        aba_gains_second,
        embed_table,
        embed_first,
        embed_second,
        output_table,
        output_first,
        output_second,
    ) = arguments
    h = lax.axis_index("h")
    attr_count, entries, embed_width = embed_table.shape
    classes = output_table.shape[2]
    model_width = attr_count * embed_width
    own_tokens = cell_ids.shape[0] // grid.heads
    first_device = ((lax.axis_index("a") == 0) & (grid.sharer() == 0)).astype(WIDE)
    native = grid.each == 2
    side = jnp.stack([lax.axis_index("q"), lax.axis_index("p")]).astype(jnp.int32)

    pieces = []
    weight_view = native_view(abd_weights) if native else None
    for offset, parts, width in SECTIONS:
        if native:
            pieces.append(split_weights(weight_view, side, offset, parts, width))
        else:
            columns = abd_weights[:, :, offset : offset + parts * width]
            pieces.append(grid.split_plain(columns, parts, width))
    qkv_pieces, out_pieces, up_pieces, down_pieces = pieces

    def traded(values):
        return [values[0]] + [grid.trade(values[j], j) for j in (1, 2, 3)]

    qkv_w = jnp.concatenate(traded(qkv_pieces), axis=0)

    def own_rows(values):
        return lax.dynamic_slice_in_dim(values, h * own_tokens, own_tokens, 0)

    picked = own_rows(jnp.where(cell_mask == 1, classes, cell_ids)).astype(LOW)
    picked = jnp.concatenate(grid.row_gather(picked), axis=0)
    picked = grid.spread(jnp.concatenate(grid.local(picked, 1), axis=1))
    picked = jnp.concatenate(picked, axis=0)
    local_attrs = picked.shape[1]
    tokens = picked.shape[0]
    held = tokens // grid.members
    block_attrs = local_attrs // SHARERS
    table_rows = jnp.arange(block_attrs * entries, dtype=jnp.int32)
    row_attr, row_entry = table_rows // entries, (table_rows % entries).astype(WIDE)
    own_block = row_attr[:, None] == (
        jnp.arange(block_attrs * embed_width, dtype=jnp.int32) // embed_width
    )
    hots, embedded = [], []
    for j, table in enumerate(grid.local(embed_table, 0)):
        expand = (
            jnp.arange(local_attrs, dtype=jnp.int32)[:, None]
            == j * block_attrs + row_attr[None, :]
        ).astype(LOW)
        hot = (dot(picked, expand) == row_entry[None, :]).astype(LOW)
        hots.append(hot)
        table = table.reshape(block_attrs * entries, embed_width)
        table = jnp.where(own_block, jnp.tile(table, (1, block_attrs)), 0.0)
        embedded.append(
            dot(
                jnp.concatenate([hot, hot, hot], axis=1),
                jnp.concatenate(split_three(table), axis=0),
            )
        )
    embedded = jnp.concatenate(embedded, axis=1)

    mask_own = own_rows(cell_mask).astype(WIDE)
    label_parts = labels.reshape(grid.heads, own_tokens, -1).astype(LOW)
    label_sent = [
        lax.dynamic_index_in_dim(label_parts, h ^ d, 0, False) for d in range(grid.heads)
    ]
    tables_low = output_table.astype(LOW)
    label_got, table_got = [label_sent[0]], [tables_low]
    for d in range(1, grid.heads):
        label_got.append(grid.pair(label_sent[d], d))
        table_got.append(grid.pair(tables_low, d))

    def by_head(parts):
        for bit in range((grid.heads - 1).bit_length()):
            flag = (h >> bit) % 2 == 1
            parts = [
                jnp.where(flag, parts[d ^ (1 << bit)], parts[d]) for d in range(grid.heads)
            ]
        return parts

    labels_own = jnp.concatenate(by_head(label_got), axis=1).astype(jnp.int32)
    output_low = jnp.concatenate(by_head(table_got), axis=0)
    label_hot = (labels_own[:, :, None] == jnp.arange(classes, dtype=jnp.int32)).astype(WIDE)
    counts = jnp.sum(mask_own[:, :, None] * label_hot, axis=0)

    gains = jnp.concatenate(grid.local(abd_gains, 1), axis=1)
    mean_one, scale_one = grid.stats(embedded, model_width)
    hat_one = (embedded - mean_one) * scale_one
    normed = (hat_one * gains[0]).astype(LOW)
    triple, out_pieces, up_pieces = tied(dot(normed, qkv_w).astype(LOW), out_pieces, up_pieces)
    triple = grid.row_sum(triple).astype(LOW)
    out_w = jnp.concatenate(traded(out_pieces), axis=0)
    up_w = jnp.concatenate(traded(up_pieces), axis=0)
    counts = grid.total(counts)
    triple, out_w, up_w, counts, label_hot, output_low, down_pieces = tied(
        triple, out_w, up_w, counts, label_hot, output_low, down_pieces
    )
    class_weight = lax.rsqrt(1.0 + counts)
    weight_total = jnp.sum(counts * class_weight)
    part = HD // grid.parts
    query_own, key_own, value_own = (triple[:, i * part : (i + 1) * part] for i in range(3))
    queries, key_rows = grid.columns(query_own), grid.columns(key_own)
    value_rows = grid.columns(value_own)
    factor = HD ** (-0.5)
    scores = dot(queries, key_rows, 1, 1) * factor
    shifted = jnp.exp(scores - jnp.max(scores, axis=1, keepdims=True))
    probs = shifted / jnp.sum(shifted, axis=1, keepdims=True)
    probs_low = probs.astype(LOW)
    attended = jnp.split(dot(probs_low, value_own).astype(LOW), 2, axis=0)
    branch = [dot(a, out_w, 1, 1).astype(LOW) for a in attended]
    middle = embedded[:held] + grid.gathered_sum(*branch)
    mean_two, scale_two = grid.stats(middle, model_width)
    hat_two = (middle - mean_two) * scale_two
    second = grid.spread((hat_two * gains[1]).astype(LOW))
    before, down_pieces = tied([dot(a, up_w).astype(LOW) for a in second], down_pieces)
    before = [grid.row_sum(b) for b in before]
    down_w = jnp.concatenate(traded(down_pieces), axis=0)
    before, down_w = tied(before, down_w)
    hidden = [gelu_apply(b).astype(LOW) for b in before]
    after = middle + grid.gathered_sum(*[dot(a, down_w, 1, 1).astype(LOW) for a in hidden])

    aba_low = aba_weights.astype(LOW)
    final, aba_stored = aba_forward(grid.to_rows(after), aba_low, aba_gains)
    final_low = final.reshape(own_tokens, attr_count, embed_width).astype(LOW)
    logits = jnp.einsum("tfe,fec->tfc", final_low, output_low, preferred_element_type=WIDE)
    highest = jnp.max(logits, axis=-1, keepdims=True)
    exped = jnp.exp(logits - highest)
    totals = jnp.sum(exped, axis=-1, keepdims=True)
    log_total = (highest + jnp.log(totals))[:, :, 0]
    cell_weight = mask_own * jnp.sum(label_hot * class_weight[None], axis=-1)
    loss_local = jnp.sum(cell_weight * (log_total - jnp.sum(label_hot * logits, axis=-1)))
    logit_grad = ((cell_weight / weight_total)[:, :, None] * (exped / totals - label_hot)).astype(
        LOW
    )
    final_grad = jnp.einsum("tfc,fec->tfe", logit_grad, output_low, preferred_element_type=WIDE)
    output_part = jnp.einsum("tfe,tfc->fec", final_low, logit_grad, preferred_element_type=WIDE)
    rows_grad, aba_part, aba_gains_part = aba_backward(
        final_grad.reshape(own_tokens, model_width), aba_stored, aba_low, aba_gains
    )

    width = normed.shape[1] // SHARERS
    gradient_sq = []

    def row_gradients(acts, uppers):
        found = []
        for j in range(SHARERS):
            cut = slice(j * width, (j + 1) * width)
            piece = sum(dot(a[:, cut], u, 0, 0) for a, u in zip(acts, uppers)).astype(LOW)
            gradient_sq.append(jnp.sum(jnp.square(piece.astype(WIDE))))
            found.append(piece)
        return found

    upstream = grid.from_rows(rows_grad.astype(LOW))
    down_grad = grid.spread(upstream)
    hidden_grad, output_part, aba_part, aba_gains_part = tied(
        [dot(a, down_w).astype(LOW) for a in down_grad], output_part, aba_part, aba_gains_part
    )
    hidden_grad = [grid.row_sum(g) for g in hidden_grad]
    down_gradient = traded(row_gradients(down_grad, hidden))

    small = jnp.concatenate([aba_part.reshape(-1), aba_gains_part.reshape(-1)])
    blocks = output_part.reshape(grid.heads, -1)
    bits = (grid.heads - 1).bit_length()
    for bit in range(bits):
        flag = (h >> bit) % 2 == 1
        halves = blocks.reshape(-1, 2, blocks.shape[1])
        kept, sent = exchange(flag, halves[:, 0], halves[:, 1])
        got = grid.pair(jnp.concatenate([sent.reshape(-1), small]).reshape(-1, 128), 1 << bit)
        got = got.reshape(-1)
        blocks = kept + got[: sent.size].reshape(kept.shape)
        small = small + got[sent.size :]
    packed = jnp.concatenate([blocks.reshape(-1), small]).reshape(-1, 128)
    for step in (grid.heads, 2 * grid.heads):
        packed = packed + grid.pair(packed, step)
    packed = grid.row_sum(packed).reshape(-1)
    output_grad = packed[: blocks.size].reshape(output_table.shape)
    aba_grad = packed[blocks.size : blocks.size + aba_weights.size].reshape(aba_weights.shape)
    aba_gains_grad = packed[blocks.size + aba_weights.size :].reshape(aba_gains.shape)

    hidden_grad, down_gradient, output_grad, aba_grad, aba_gains_grad = tied(
        hidden_grad, down_gradient, output_grad, aba_grad, aba_gains_grad
    )

    before_grad = [gelu_back(b, g).astype(LOW) for b, g in zip(before, hidden_grad)]
    second_grad = grid.gathered_sum(*[dot(a, up_w, 1, 1).astype(LOW) for a in before_grad])
    gained = second_grad * gains[1]
    sums = jnp.stack([jnp.sum(gained, axis=1), jnp.sum(gained * hat_two, axis=1)])
    sums = sum(grid.row_list(sums)) / model_width
    middle_grad = upstream.astype(WIDE) + scale_two * (
        gained - sums[0][:, None] - hat_two * sums[1][:, None]
    )
    gain_two = jnp.sum(second_grad * hat_two, axis=0)
    branch_grad = grid.spread(middle_grad.astype(LOW))
    attended_grad, up_gradient, out_gradient = tied(
        jnp.concatenate([dot(a, out_w).astype(LOW) for a in branch_grad], axis=0),
        row_gradients(second, before_grad),
        row_gradients(branch_grad, attended),
    )
    attended_grad = grid.row_sum(attended_grad).astype(LOW)
    up_gradient, out_gradient = traded(up_gradient), traded(out_gradient)
    prob_grad = dot(grid.columns(attended_grad), value_rows, 1, 1)
    score_grad = probs * (prob_grad - jnp.sum(probs * prob_grad, axis=1, keepdims=True))
    score_grad = score_grad.astype(LOW)
    query_grad = dot(score_grad, key_own) * factor
    key_grad = dot(score_grad, query_own, 0, 0) * factor
    value_grad = dot(probs_low, attended_grad, 0, 0)
    triple_grad = jnp.concatenate([query_grad, key_grad, value_grad], axis=1).astype(LOW)
    table_part = [
        sum(dot(hot[:held], piece, 0, 0) for piece in split_three(block)[:2])
        for hot, block in zip(hots, jnp.split(middle_grad, SHARERS, axis=1))
    ]
    triple_grad, up_gradient, out_gradient, table_part = tied(
        triple_grad, up_gradient, out_gradient, table_part
    )
    qkv_gradient = traded(row_gradients([normed], [triple_grad]))
    gradients = qkv_gradient + out_gradient + up_gradient + down_gradient

    normed_grad = dot(triple_grad, qkv_w, 1, 1)
    gained = normed_grad * gains[0]
    sums = jnp.stack([jnp.sum(gained, axis=1), jnp.sum(gained * hat_one, axis=1)])
    sums = sum(grid.row_list(sums)) / model_width
    gain_one = jnp.sum(normed_grad * hat_one, axis=0)
    spread_grad = scale_one * (gained - sums[0][:, None] - hat_one * sums[1][:, None])
    fold = (
        jnp.arange(block_attrs * embed_width, dtype=jnp.int32)[:, None] % embed_width
        == jnp.arange(embed_width, dtype=jnp.int32)
    ).astype(WIDE)
    records = []
    for j, block in enumerate(jnp.split(spread_grad, SHARERS, axis=1)):
        grad = table_part[j] + sum(dot(hots[j], piece, 0, 0) for piece in split_three(block)[:2])
        grad = jnp.dot(jnp.where(own_block, grad, 0.0), fold, precision=lax.Precision.HIGHEST)
        cut = slice(j * width, (j + 1) * width)
        records.append(jnp.concatenate([grad.reshape(-1), gain_one[cut], gain_two[cut]]))
    table_size = block_attrs * entries * embed_width
    packed = jnp.stack(grid.ordered(records)).reshape(-1, 128)
    packed = jnp.stack(grid.row_gather(grid.group_total(packed)))
    packed = packed.reshape(grid.rows * SHARERS, -1)
    embed_grad = packed[:, :table_size].reshape(embed_table.shape)
    abd_gains_grad = packed[:, table_size:].reshape(-1, 2, width).transpose(1, 0, 2)
    abd_gains_grad = abd_gains_grad.reshape(2, model_width)

    output_sq = first_device * jnp.sum(output_grad * output_grad)
    summed = grid.total(jnp.stack([sum(gradient_sq), output_sq, loss_local]))
    replicated_sq = (
        jnp.sum(abd_gains_grad * abd_gains_grad)
        + jnp.sum(aba_grad * aba_grad)
        + jnp.sum(aba_gains_grad * aba_gains_grad)
        + jnp.sum(embed_grad * embed_grad)
    )
    grad_norm = jnp.sqrt(summed[0] + summed[1] + replicated_sq)
    loss_sum = summed[2]
    clip_factor = jnp.minimum(1.0, CLIP_LIMIT / (grad_norm + 1e-06))
    if native:
        first_view, second_view, abd_update, squares = moments_step(
            side,
            clip_factor[None],
            weight_view,
            native_view(abd_first),
            native_view(abd_second),
            gradients,
        )
        abd_first_new = from_native(first_view, grid.each)
        abd_second_new = from_native(second_view, grid.each)
        abd_update_sq, abd_weight_sq = jnp.sum(squares[0]), jnp.sum(squares[1])
    else:
        merged = [
            grid.merge_plain(gradients[SHARERS * i : SHARERS * (i + 1)], parts, width)
            for i, (_, parts, width) in enumerate(SECTIONS)
        ]
        abd_grad = jnp.concatenate(merged, axis=2).astype(WIDE)
        abd_first_new, abd_second_new, abd_update = moments_of(
            abd_weights, abd_grad, abd_first, abd_second, clip_factor, WEIGHT_DECAY
        )
        abd_update_sq, abd_weight_sq = (
            jnp.sum(abd_update * abd_update),
            jnp.sum(abd_weights * abd_weights),
        )
    output_first_new, output_second_new, output_update = moments_of(
        output_table, output_grad, output_first, output_second, clip_factor, WEIGHT_DECAY
    )
    trust_sums = grid.total(
        jnp.stack(
            [
                abd_update_sq,
                first_device * jnp.sum(output_update * output_update),
                abd_weight_sq,
                first_device * jnp.sum(output_table * output_table),
            ]
        )
    )
    if native:
        abd_new = from_native(
            apply_trust(weight_view, abd_update.astype(WIDE), trust_sums[2], trust_sums[0]),
            grid.each,
        )
    else:
        abd_new = apply_trust(abd_weights, abd_update, trust_sums[2], trust_sums[0])
    output_new = apply_trust(output_table, output_update, trust_sums[3], trust_sums[1])
    gain_triple = local_step(
        abd_gains, abd_gains_grad, abd_gains_first, abd_gains_second, clip_factor, 0.0
    )
    aba_triple = local_step(aba_weights, aba_grad, aba_first, aba_second, clip_factor, WEIGHT_DECAY)
    aba_gain_triple = local_step(
        aba_gains, aba_gains_grad, aba_gains_first, aba_gains_second, clip_factor, 0.0
    )
    embed_triple = local_step(
        embed_table, embed_grad, embed_first, embed_second, clip_factor, WEIGHT_DECAY
    )
    return (
        loss_sum,
        weight_total,
        grad_norm,
        abd_new,
        abd_first_new,
        abd_second_new,
        *gain_triple,
        *aba_triple,
        *aba_gain_triple,
        *embed_triple,
        output_new,
        output_first_new,
        output_second_new,
    )


def solution(mesh):
    grid = Grid(mesh.shape["dp"], mesh.shape["head"])
    devices = Mesh(mesh.devices.reshape(grid.shape), ("a", "q", "p", "h"))
    rows = ("a", "q", "p")
    tokens, table = P(rows, None), P("h", None, None)
    weight = P(rows, "h", None)
    in_specs = (tokens, tokens, P(rows, "h"), weight, weight, weight) + (P(),) * 12 + (table,) * 3
    out_specs = (P(),) * 3 + (weight,) * 3 + (P(),) * 12 + (table,) * 3
    return jax.shard_map(
        functools.partial(per_device, grid),
        mesh=devices,
        in_specs=in_specs,
        out_specs=out_specs,
        check_vma=False,
    )
```

```python
import functools

import jax
import jax.experimental.pallas as pl
import jax.experimental.pallas.tpu as pltpu
import jax.numpy as jnp
from jax import lax
from jax.sharding import Mesh
from jax.sharding import PartitionSpec as P

H = 8
AH = 8
STEP = 10
HD = 512
FF = 16384


EPS_NORM = 1e-05
CLIP_LIMIT = 0.01
LEARN_RATE = 0.3
BETA_FIRST = 0.9
BETA_SECOND = 0.999
ADAM_EPSILON = 1e-08
WEIGHT_DECAY = 0.01


def layer_norm(values, gain_row):
    center = jnp.mean(values, axis=-1, keepdims=True)
    centred = values - center
    spread = jnp.mean(centred * centred, axis=-1, keepdims=True)
    return centred * lax.rsqrt(spread + EPS_NORM) * gain_row


def gelu_apply(values):
    return 0.5 * values * (1.0 + lax.erf(values * 0.7071067811865476))


def norm_back(values, gain_row, upstream):
    unused_value, pull_back = jax.vjp(layer_norm, values, gain_row)
    return pull_back(upstream)


def gelu_back(values, upstream):
    unused_value, pull_back = jax.vjp(gelu_apply, values)
    return pull_back(upstream)[0]


def attend_keys(queries, key_rows, value_rows, factor):
    scores = (
        jnp.einsum("...qd,...kd->...qk", queries, key_rows, preferred_element_type=jnp.float32)
        * factor
    )
    highest = jnp.max(scores, axis=-1, keepdims=True)
    weights = jnp.exp(scores - highest)
    totals = jnp.sum(weights, axis=-1, keepdims=True)
    result = jnp.einsum(
        "...qk,...kd->...qd",
        (weights / totals).astype(jnp.bfloat16),
        value_rows,
        preferred_element_type=jnp.float32,
    )
    return (result, highest + jnp.log(totals))


def attend_back(queries, key_rows, value_rows, log_total, result_grad, factor):
    scores = (
        jnp.einsum("...qd,...kd->...qk", queries, key_rows, preferred_element_type=jnp.float32)
        * factor
    )
    softmax_probs = jnp.exp(scores - log_total)
    prob_grad = jnp.einsum(
        "...qd,...kd->...qk", result_grad, value_rows, preferred_element_type=jnp.float32
    )
    score_grad = softmax_probs * (
        prob_grad - jnp.sum(softmax_probs * prob_grad, axis=-1, keepdims=True)
    )
    score_grad = score_grad.astype(jnp.bfloat16)
    query_grad = (
        jnp.einsum("...qk,...kd->...qd", score_grad, key_rows, preferred_element_type=jnp.float32)
        * factor
    )
    key_grad = (
        jnp.einsum("...qk,...qd->...kd", score_grad, queries, preferred_element_type=jnp.float32)
        * factor
    )
    value_grad = jnp.einsum(
        "...qk,...qd->...kd",
        softmax_probs.astype(jnp.bfloat16),
        result_grad,
        preferred_element_type=jnp.float32,
    )
    return (query_grad, key_grad, value_grad)


def aba_forward(row_block, weights, gain_rows):
    embed_width = weights.shape[0]
    row_count = row_block.shape[0]
    attr_count = row_block.shape[1] // embed_width
    size_each = embed_width // AH
    inputs = row_block.reshape(row_count, attr_count, embed_width)
    normed = layer_norm(inputs, gain_rows[0]).astype(jnp.bfloat16)
    projection = weights[:, : 3 * embed_width].reshape(embed_width, 3, AH, size_each)
    triple = jnp.einsum(
        "rfe,eshd->srhfd", normed, projection, preferred_element_type=jnp.float32
    ).astype(jnp.bfloat16)
    attended, log_total = attend_keys(triple[0], triple[1], triple[2], size_each ** (-0.5))
    attended = attended.astype(jnp.bfloat16)
    out_proj = weights[:, 3 * embed_width : 4 * embed_width].reshape(embed_width, AH, size_each)
    middle = inputs + jnp.einsum(
        "rhfd,ohd->rfo", attended, out_proj, preferred_element_type=jnp.float32
    )
    second = layer_norm(middle, gain_rows[1]).astype(jnp.bfloat16)
    before = jnp.einsum(
        "rfe,eu->rfu",
        second,
        weights[:, 4 * embed_width : 8 * embed_width],
        preferred_element_type=jnp.float32,
    )
    hidden = gelu_apply(before).astype(jnp.bfloat16)
    after = middle + jnp.einsum(
        "rfu,ou->rfo", hidden, weights[:, 8 * embed_width :], preferred_element_type=jnp.float32
    )
    return (
        after.reshape(row_count, attr_count * embed_width),
        (inputs, normed, triple, log_total, attended, middle, second, before, hidden),
    )


def aba_backward(upstream, stored, weights, gain_rows):
    inputs, normed, triple, log_total, attended, middle, second, before, hidden = stored
    row_count, attr_count, embed_width = inputs.shape
    size_each = embed_width // AH
    upstream = upstream.reshape(row_count, attr_count, embed_width)
    down_grad = upstream.astype(jnp.bfloat16)
    hidden_grad = jnp.einsum(
        "rfo,ou->rfu", down_grad, weights[:, 8 * embed_width :], preferred_element_type=jnp.float32
    )
    before_grad = gelu_back(before, hidden_grad).astype(jnp.bfloat16)
    second_grad = jnp.einsum(
        "rfu,eu->rfe",
        before_grad,
        weights[:, 4 * embed_width : 8 * embed_width],
        preferred_element_type=jnp.float32,
    )
    middle_part, gain_two = norm_back(middle, gain_rows[1], second_grad)
    middle_grad = upstream + middle_part
    branch_grad = middle_grad.astype(jnp.bfloat16)
    out_proj = weights[:, 3 * embed_width : 4 * embed_width].reshape(embed_width, AH, size_each)
    attended_grad = jnp.einsum(
        "rfo,ohd->rhfd", branch_grad, out_proj, preferred_element_type=jnp.float32
    ).astype(jnp.bfloat16)
    query_grad, key_grad, value_grad = attend_back(
        triple[0], triple[1], triple[2], log_total, attended_grad, size_each ** (-0.5)
    )
    triple_grad = jnp.stack([query_grad, key_grad, value_grad]).astype(jnp.bfloat16)
    projection = weights[:, : 3 * embed_width].reshape(embed_width, 3, AH, size_each)
    normed_grad = jnp.einsum(
        "srhfd,eshd->rfe", triple_grad, projection, preferred_element_type=jnp.float32
    )
    input_part, gain_one = norm_back(inputs, gain_rows[0], normed_grad)
    input_grad = middle_grad + input_part
    weight_grad = jnp.concatenate(
        [
            jnp.einsum(
                "rfe,srhfd->eshd", normed, triple_grad, preferred_element_type=jnp.float32
            ).reshape(embed_width, 3 * embed_width),
            jnp.einsum(
                "rfo,rhfd->ohd", branch_grad, attended, preferred_element_type=jnp.float32
            ).reshape(embed_width, embed_width),
            jnp.einsum("rfe,rfu->eu", second, before_grad, preferred_element_type=jnp.float32),
            jnp.einsum("rfo,rfu->ou", down_grad, hidden, preferred_element_type=jnp.float32),
        ],
        axis=1,
    )
    return (
        input_grad.reshape(row_count, attr_count * embed_width),
        weight_grad,
        jnp.stack([gain_one, gain_two]),
    )


def moments_of(weight, gradient, first, second, clip_factor, decay):
    scaled = gradient * clip_factor
    first_new = BETA_FIRST * first + (1.0 - BETA_FIRST) * scaled
    second_new = BETA_SECOND * second + (1.0 - BETA_SECOND) * scaled * scaled
    update = (
        first_new
        / (1.0 - BETA_FIRST**STEP)
        / (jnp.sqrt(second_new / (1.0 - BETA_SECOND**STEP)) + ADAM_EPSILON)
        + decay * weight
    )
    return (first_new, second_new, update)


def apply_trust(weight, update, weight_sq, update_sq):
    trust_ratio = jnp.sqrt(weight_sq) / (jnp.sqrt(update_sq) + 1e-06)
    return weight - LEARN_RATE * trust_ratio * update


def local_step(weight, gradient, first, second, clip_factor, decay):
    first_new, second_new, update = moments_of(weight, gradient, first, second, clip_factor, decay)
    return (
        apply_trust(weight, update, jnp.sum(weight * weight), jnp.sum(update * update)),
        first_new,
        second_new,
    )


LOW = jnp.bfloat16
WIDE = jnp.float32
SHARERS = 4
FIRST_SCALE = 1.0 / (1.0 - BETA_FIRST**STEP)
SECOND_SCALE = 1.0 / (1.0 - BETA_SECOND**STEP)
UNITS = FF // H
SOURCES = ((0, 0), (1, 0), (1, HD // 2), (2, 0))
SECTIONS = ((0, 3, HD), (3 * HD, 1, HD), (4 * HD, 1, UNITS), (4 * HD + UNITS, 1, UNITS))


def dot(left, right, left_dim=1, right_dim=0):
    return lax.dot_general(
        left, right, (((left_dim,), (right_dim,)), ((), ())), preferred_element_type=WIDE
    )


def native_view(values):
    rows, heads, columns = values.shape
    return (
        values.reshape(rows, heads, columns // 128, 128)
        .transpose(0, 2, 1, 3)
        .reshape(rows, columns // 128 * heads, 128)
    )


def from_native(values, heads):
    rows, count, width = values.shape
    return (
        values.reshape(rows, count // heads, heads, width)
        .transpose(0, 2, 1, 3)
        .reshape(rows, heads, count // heads * width)
    )


def tile_pairs(parts, width):
    each = width // 128
    return [
        (part * each + i, part * each + each // 2 + i)
        for part in range(parts)
        for i in range(each // 2)
    ]


def exchange(flag, left, right):
    return jnp.where(flag, right, left), jnp.where(flag, left, right)


def cross(q_flag, p_flag, values):
    a, b = exchange(p_flag, values[0], values[1])
    c, d = exchange(p_flag, values[2], values[3])
    a, c = exchange(q_flag, a, c)
    b, d = exchange(q_flag, b, d)
    return a, b, c, d


def split_kernel(sections, side_ref, *refs):
    weight_refs, out_refs = refs[: len(sections)], refs[len(sections) :]
    q_flag, p_flag = side_ref[0] == 1, side_ref[1] == 1
    lane = 0
    for weight_ref, (_, parts, width) in zip(weight_refs, sections):
        turned = {}
        for left, right in tile_pairs(parts, width):
            for group in (left // 4, right // 4):
                if group not in turned:
                    rows = weight_ref[:, group * 8 : group * 8 + 8, :]
                    turned[group] = jnp.swapaxes(rows, 0, 1)
            values = [
                turned[t // 4][t % 4 * 2 + head] for head in range(2) for t in (left, right)
            ]
            for ref, value in zip(out_refs, cross(q_flag, p_flag, values)):
                ref[:, lane : lane + 128] = value.astype(LOW)
            lane += 128


def split_weights(view, side, sections):
    rows = view.shape[0]
    total = sum(parts * width for _, parts, width in sections)
    block = 32

    def section_spec(offset, size):
        return pl.BlockSpec((block, size // 64, 128), lambda i: (i, offset // size, 0))

    return pl.pallas_call(
        functools.partial(split_kernel, sections),
        out_shape=[jax.ShapeDtypeStruct((rows, total // 2), LOW)] * SHARERS,
        grid=(rows // block,),
        in_specs=[pl.BlockSpec(memory_space=pltpu.SMEM)]
        + [section_spec(offset, parts * width) for offset, parts, width in sections],
        out_specs=[pl.BlockSpec((block, total // 2), lambda i: (i, 0))] * SHARERS,
        compiler_params=pltpu.CompilerParams(vmem_limit_bytes=40 * 2**20),
        cost_estimate=pl.CostEstimate(
            flops=rows * total * 2, bytes_accessed=rows * total * 12, transcendentals=0
        ),
    )(side, *[view] * len(sections))


def moments_kernel(side_ref, clip_ref, weight_ref, first_ref, second_ref, *rest):
    gradients, (first_out, second_out, update_out, total_ref) = rest[:-4], rest[-4:]
    q_flag, p_flag = side_ref[0] == 1, side_ref[1] == 1
    clip = clip_ref[0]

    @pl.when(pl.program_id(0) == 0)
    def _():
        total_ref[...] = jnp.zeros_like(total_ref)

    update_sq = jnp.zeros((8, 128), WIDE)
    weight_sq = jnp.zeros((8, 128), WIDE)
    for (offset, parts, width), (index, lane) in zip(SECTIONS, SOURCES):
        refs = gradients[SHARERS * index : SHARERS * (index + 1)]
        places = {}
        for tile, (left, right) in enumerate(tile_pairs(parts, width)):
            lanes = slice(lane + tile * 128, lane + tile * 128 + 128)
            values = [ref[:, lanes].astype(WIDE) for ref in refs]
            a, b, c, d = cross(q_flag, p_flag, values)
            places[2 * left], places[2 * right] = a, b
            places[2 * left + 1], places[2 * right + 1] = c, d
            for group in (left // 4, right // 4):
                rows = range(group * 8, group * 8 + 8)
                if any(row not in places for row in rows):
                    continue
                scaled = jnp.swapaxes(jnp.stack([places.pop(r) for r in rows], axis=0), 0, 1) * clip
                here = pl.ds(offset // 64 + group * 8, 8)
                weight = weight_ref[:, here, :]
                first_new = BETA_FIRST * first_ref[:, here, :] + (1.0 - BETA_FIRST) * scaled
                second_new = (
                    BETA_SECOND * second_ref[:, here, :] + (1.0 - BETA_SECOND) * scaled * scaled
                )
                first_out[:, here, :] = first_new
                second_out[:, here, :] = second_new
                update = (
                    first_new * FIRST_SCALE / (jnp.sqrt(second_new * SECOND_SCALE) + ADAM_EPSILON)
                    + WEIGHT_DECAY * weight
                )
                update_out[:, here, :] = update.astype(update_out.dtype)
                update_sq += jnp.sum(update * update, axis=0)
                weight_sq += jnp.sum(weight * weight, axis=0)
    total_ref[0] += update_sq
    total_ref[1] += weight_sq


def moments_step(side, clip, weight, first, second, gradients):
    rows, depth, _ = weight.shape
    block = 32
    whole = pl.BlockSpec((block, depth, 128), lambda i: (i, 0, 0))
    shape = jax.ShapeDtypeStruct(weight.shape, WIDE)
    return pl.pallas_call(
        moments_kernel,
        out_shape=[
            shape,
            shape,
            jax.ShapeDtypeStruct(weight.shape, LOW),
            jax.ShapeDtypeStruct((2, 8, 128), WIDE),
        ],
        grid=(rows // block,),
        in_specs=[pl.BlockSpec(memory_space=pltpu.SMEM)] * 2
        + [whole] * 3
        + [pl.BlockSpec((block, g.shape[1]), lambda i: (i, 0)) for g in gradients],
        out_specs=[whole] * 3 + [pl.BlockSpec((2, 8, 128), lambda i: (0, 0, 0))],
        compiler_params=pltpu.CompilerParams(vmem_limit_bytes=48 * 2**20),
        cost_estimate=pl.CostEstimate(
            flops=weight.size * 20, bytes_accessed=weight.size * 24, transcendentals=weight.size
        ),
    )(side, clip, weight, first, second, *gradients)


def join_kernel(*refs):
    rows = refs[0].shape[0]
    for k, ref in enumerate(refs[:-1]):
        refs[-1][k * rows : (k + 1) * rows, :] = ref[...]


def join_blocks(parts, turns):
    rows, columns = parts[0].shape
    width = columns // SHARERS
    return pl.pallas_call(
        join_kernel,
        out_shape=jax.ShapeDtypeStruct((len(parts) * rows, columns), parts[0].dtype),
        grid=(SHARERS,),
        in_specs=[pl.BlockSpec((rows, width), lambda j, t=t: (0, j ^ t)) for t in turns],
        out_specs=pl.BlockSpec((len(parts) * rows, width), lambda j: (0, j)),
        cost_estimate=pl.CostEstimate(
            flops=0, bytes_accessed=4 * len(parts) * rows * columns, transcendentals=0
        ),
    )(*parts)


def part_kernel(*refs):
    count = len(refs) // 3
    for left, right, out in zip(refs[:count], refs[count : 2 * count], refs[2 * count :]):
        out[...] = (left[...].astype(WIDE) + right[...].astype(WIDE)).astype(out.dtype)


def part_sums(left, right, turns):
    rows, columns = left.shape[0] // len(turns), left.shape[1]
    width = columns // SHARERS
    specs = [
        pl.BlockSpec((rows, width), lambda j, k=k, t=t: (k, j ^ t)) for k, t in enumerate(turns)
    ]
    return pl.pallas_call(
        part_kernel,
        out_shape=[
            jax.ShapeDtypeStruct((rows, columns), LOW if k else WIDE) for k in range(len(turns))
        ],
        grid=(SHARERS,),
        in_specs=specs + specs,
        out_specs=[pl.BlockSpec((rows, width), lambda j: (0, j))] * len(turns),
        cost_estimate=pl.CostEstimate(
            flops=left.size, bytes_accessed=6 * left.size, transcendentals=0
        ),
    )(*[left] * len(turns), *[right] * len(turns))


class Grid:
    def __init__(self, rows, heads):
        self.rows, self.heads = rows // SHARERS, heads
        self.each = H // heads
        self.parts = SHARERS // self.each
        self.members = SHARERS * heads
        self.shape = (self.rows, self.each, self.parts, heads)
        self.evens = range(2, self.members, 2)

    def sharer(self):
        return lax.axis_index("q") * self.parts + lax.axis_index("p")

    def pair(self, values, step):
        return lax.ppermute(values, ("q", "p", "h"), [(i, i ^ step) for i in range(self.members)])

    def trade(self, values, step):
        return lax.ppermute(values, ("q", "p"), [(i, i ^ step) for i in range(SHARERS)])

    def turns(self):
        return [0] + [d // self.heads for d in self.evens]

    def spread(self, own):
        parts = [own] + [self.pair(own, d) for d in self.evens]
        half = join_blocks(parts, self.turns())
        return half, self.pair(half, 1)

    def gathered_sum(self, half, other):
        parts = part_sums(half, self.pair(other, 1), self.turns())
        total = parts[0]
        for part, d in zip(parts[1:], self.evens):
            total = total + self.pair(part, d).astype(WIDE)
        return total

    def group_total(self, values):
        step = 1
        while step < self.members:
            values = values + self.pair(values, step)
            step *= 2
        return values

    def every(self, values):
        step = 1
        while step < self.members:
            values = jnp.concatenate([values, self.pair(values, step)], axis=0)
            step *= 2
        step = 1
        while step < self.rows:
            moved = lax.ppermute(values, "a", [(i, i ^ step) for i in range(self.rows)])
            values = jnp.concatenate([values, moved], axis=0)
            step *= 2
        return values

    def facing(self, values):
        return lax.ppermute(values, "a", [(0, 1), (1, 0)])

    def row_list(self, values):
        if self.rows == 2:
            return [values, self.facing(values)]
        every = lax.all_gather(values, "a", axis=0)
        return [every[i] for i in range(self.rows)]

    def row_gather(self, values):
        parts = self.row_list(values)
        if self.rows == 2:
            flag = lax.axis_index("a") == 1
            parts = exchange(flag, *parts)
        return list(parts)

    def row_sum(self, values):
        if self.rows == 2:
            return values.astype(WIDE) + self.facing(values).astype(WIDE)
        return lax.psum(values.astype(WIDE), "a")

    def total(self, values):
        return self.row_sum(self.group_total(values))

    def ordered(self, parts):
        place = self.sharer()
        low, high = place % 2 == 1, place // 2 == 1
        parts = [jnp.where(low, parts[j ^ 1], parts[j]) for j in range(SHARERS)]
        return [jnp.where(high, parts[j ^ 2], parts[j]) for j in range(SHARERS)]

    def absolute(self, values):
        return jnp.concatenate(self.ordered(jnp.split(values, SHARERS, axis=-1)), axis=-1)

    def to_rows(self, values):
        values = self.absolute(values)
        if self.rows != 2:
            return lax.all_to_all(values, "a", split_axis=0, concat_axis=1, tiled=True)
        flag = lax.axis_index("a") == 1
        kept, sent = exchange(flag, *jnp.split(values, 2, axis=0))
        return jnp.concatenate(exchange(flag, kept, self.facing(sent)), axis=1)

    def from_rows(self, values):
        if self.rows != 2:
            return self.absolute(
                lax.all_to_all(values, "a", split_axis=1, concat_axis=0, tiled=True)
            )
        flag = lax.axis_index("a") == 1
        kept, sent = exchange(flag, *jnp.split(values, 2, axis=1))
        moved = jnp.concatenate(exchange(flag, kept, self.facing(sent)), axis=0)
        return self.absolute(moved)

    def renamed(self, values, step):
        block = values.shape[0] // self.members
        span = 1
        while span < self.members // 2:
            if step // 2 & span:
                halves = values.reshape(-1, 2, span * block, values.shape[1])
                values = jnp.stack([halves[:, 1], halves[:, 0]], axis=1).reshape(values.shape)
            span *= 2
        return values

    def columns(self, values):
        found = [values]
        for d in range(1, self.parts):
            got = lax.ppermute(values, "p", [(i, i ^ d) for i in range(self.parts)])
            found.append(self.renamed(got, d * self.heads))
        return jnp.concatenate(found, axis=1)

    def local(self, values, axis):
        size = values.shape[axis] // (self.rows * SHARERS)
        first, place = lax.axis_index("a") * SHARERS, self.sharer()
        return [
            lax.dynamic_slice_in_dim(values, (first + (place ^ j)) * size, size, axis)
            for j in range(SHARERS)
        ]

    def stats(self, values, count):
        center = jnp.mean(values, axis=1)
        spread = jnp.sum(jnp.square(values - center[:, None]), axis=1)
        parts = self.row_list(jnp.stack([center, spread]))
        mean = sum(part[0] for part in parts) / self.rows
        size = count // self.rows
        square = sum(part[1] + size * jnp.square(part[0] - mean) for part in parts)
        return mean[:, None], lax.rsqrt(square / count + EPS_NORM)[:, None]

    def split_plain(self, values, parts, width):
        rows = values.shape[0]
        values = values.astype(LOW).reshape(rows, self.each, parts, self.parts, -1)
        values = values.transpose(1, 3, 0, 2, 4).reshape(SHARERS, rows, -1)
        return [
            lax.dynamic_index_in_dim(values, self.sharer() ^ j, 0, False) for j in range(SHARERS)
        ]

    def merge_plain(self, pieces, parts, width):
        values = jnp.stack(self.ordered(pieces))
        rows = values.shape[1]
        values = values.reshape(self.each, self.parts, rows, parts, -1)
        return values.transpose(2, 0, 3, 1, 4).reshape(rows, self.each, parts * width)


def tied(*values):
    return lax.optimization_barrier(values)


def split_three(values):
    high = lax.reduce_precision(values, 8, 7)
    rest = values - high
    middle = lax.reduce_precision(rest, 8, 7)
    return high.astype(LOW), middle.astype(LOW), (rest - middle).astype(LOW)


def per_device(grid, *arguments):
    (
        cell_ids,
        cell_mask,
        labels,
        abd_weights,
        abd_first,
        abd_second,
        abd_gains,
        abd_gains_first,
        abd_gains_second,
        aba_weights,
        aba_first,
        aba_second,
        aba_gains,
        aba_gains_first,
        aba_gains_second,
        embed_table,
        embed_first,
        embed_second,
        output_table,
        output_first,
        output_second,
    ) = arguments
    h = lax.axis_index("h")
    attr_count, entries, embed_width = embed_table.shape
    classes = output_table.shape[2]
    model_width = attr_count * embed_width
    own_tokens = cell_ids.shape[0] // grid.heads
    first_device = ((lax.axis_index("a") == 0) & (grid.sharer() == 0)).astype(WIDE)
    native = grid.each == 2
    side = jnp.stack([lax.axis_index("q"), lax.axis_index("p")]).astype(jnp.int32)

    def own_rows(values):
        return lax.dynamic_slice_in_dim(values, h * own_tokens, own_tokens, 0)

    attrs_held = labels.shape[1]
    mask_held = lax.dynamic_slice_in_dim(cell_mask, h * attrs_held, attrs_held, 1)
    codes = jnp.where(mask_held == 1, labels, -1).reshape(own_tokens, attr_count)
    picked = own_rows(jnp.where(cell_mask == 1, classes, cell_ids))
    gathered = grid.every(jnp.concatenate([picked, codes], axis=1).astype(LOW))
    tokens = gathered.shape[0]
    picked_all = gathered[:, :attr_count]
    codes_all = gathered[:, attr_count:].reshape(-1, grid.heads, own_tokens, attr_count)
    device = (lax.axis_index("a") * SHARERS + grid.sharer()) * grid.heads + h

    def by_head(parts):
        for bit in range((grid.heads - 1).bit_length()):
            flag = (h >> bit) % 2 == 1
            parts = [
                jnp.where(flag, parts[d ^ (1 << bit)], parts[d]) for d in range(grid.heads)
            ]
        return parts

    def pieces_of(sections):
        if native:
            return split_weights(weight_view, side, sections)
        found = []
        for offset, parts, size in sections:
            columns = abd_weights[:, :, offset : offset + parts * size]
            found.append(grid.split_plain(columns, parts, size))
        return [jnp.concatenate(piece, axis=1) for piece in zip(*found)]

    def traded(values):
        return [values[0]] + [grid.trade(values[j], j) for j in (1, 2, 3)]

    weight_view = native_view(abd_weights) if native else None
    qkv_pieces, picked_all, side = tied(pieces_of(SECTIONS[:1]), picked_all, side)
    qkv_w = traded(qkv_pieces)
    qkv_w, other_pieces = tied(qkv_w, pieces_of(SECTIONS[1:]))
    qkv_w = jnp.concatenate(qkv_w, axis=0)
    others = traded(other_pieces)

    held = tokens // grid.members
    place = jnp.arange(tokens, dtype=jnp.int32)
    owner, inside = place // held, place % held
    owner = 2 * (owner % (grid.members // 2)) + owner // (grid.members // 2)
    owner = owner ^ (grid.sharer() * grid.heads + h)
    source = (inside // own_tokens * grid.members + owner) ^ device
    row_of = source * own_tokens + inside % own_tokens
    picked = dot((row_of[:, None] == place[None, :]).astype(LOW), picked_all).astype(LOW)
    picked = jnp.concatenate(grid.local(picked, 1), axis=1)
    local_attrs = picked.shape[1]
    block_attrs = local_attrs // SHARERS
    table_rows = jnp.arange(block_attrs * entries, dtype=jnp.int32)
    row_attr, row_entry = table_rows // entries, (table_rows % entries).astype(WIDE)
    block_columns = jnp.arange(block_attrs * embed_width, dtype=jnp.int32)
    own_block = row_attr[:, None] == block_columns // embed_width
    fold = (
        block_columns[:, None] % embed_width == jnp.arange(embed_width, dtype=jnp.int32)
    ).astype(LOW)
    table = jnp.concatenate(grid.local(embed_table, 0), axis=0).reshape(-1, embed_width)
    tables = [dot(piece, fold, 1, 1).astype(LOW) for piece in split_three(table)]
    hots, embedded = [], []
    for j in range(SHARERS):
        expand = (
            jnp.arange(local_attrs, dtype=jnp.int32)[:, None]
            == j * block_attrs + row_attr[None, :]
        ).astype(LOW)
        hot = (dot(picked, expand) == row_entry[None, :]).astype(LOW)
        hots.append(hot)
        cut = slice(j * row_attr.size, (j + 1) * row_attr.size)
        wide = [jnp.where(own_block, piece[cut], 0.0) for piece in tables]
        embedded.append(
            dot(jnp.concatenate([hot, hot, hot], axis=1), jnp.concatenate(wide, axis=0))
        )
    embedded = jnp.concatenate(embedded, axis=1)

    kinds = jnp.arange(classes, dtype=jnp.int32).astype(WIDE)
    mask_own = own_rows(cell_mask).astype(WIDE)
    counts, own_codes = [], []
    for d in range(grid.heads):
        found = (codes_all[:, d].reshape(-1, attr_count)[:, :, None].astype(WIDE) == kinds)
        found = jnp.sum(found.astype(WIDE), axis=0)
        counts.append(jnp.sum(found.reshape(-1, attrs_held, classes), axis=0))
        own_codes.append(own_rows(codes_all[0, d].reshape(-1, attrs_held)))
    counts = jnp.concatenate(by_head(counts), axis=0)
    own_codes = jnp.concatenate(by_head(own_codes), axis=1)
    label_hot = (own_codes.astype(WIDE)[:, :, None] == kinds).astype(WIDE)
    class_weight = lax.rsqrt(1.0 + counts)
    weight_total = jnp.sum(counts * class_weight)
    tables_low = output_table.astype(LOW)[None]
    step = 1
    while step < grid.heads:
        tables_low = jnp.concatenate([tables_low, grid.pair(tables_low, step)], axis=0)
        step *= 2
    output_low = jnp.concatenate(by_head(list(tables_low)), axis=0)

    out_size, up_size = HD * grid.each // SHARERS, UNITS * grid.each // SHARERS
    gains = jnp.concatenate(grid.local(abd_gains, 1), axis=1)
    mean_one, scale_one = grid.stats(embedded, model_width)
    hat_one = (embedded - mean_one) * scale_one
    normed = (hat_one * gains[0]).astype(LOW)
    triple = grid.row_sum(dot(normed, qkv_w).astype(LOW)).astype(LOW)
    triple, class_weight, weight_total, label_hot, output_low = tied(
        triple, class_weight, weight_total, label_hot, output_low
    )
    part = HD // grid.parts
    query_own, key_own, value_own = (triple[:, i * part : (i + 1) * part] for i in range(3))
    queries, key_rows = grid.columns(query_own), grid.columns(key_own)
    value_rows = grid.columns(value_own)
    factor = HD ** (-0.5)
    scores = dot(queries, key_rows, 1, 1) * factor
    shifted = jnp.exp(scores - jnp.max(scores, axis=1, keepdims=True))
    probs = shifted / jnp.sum(shifted, axis=1, keepdims=True)
    probs_low = probs.astype(LOW)
    attended, others = tied(dot(probs_low, value_own).astype(LOW), others)
    out_w, up_w, down_w = (
        jnp.concatenate([piece[:, start : start + size] for piece in others], axis=0)
        for start, size in ((0, out_size), (out_size, up_size), (out_size + up_size, up_size))
    )
    attended = jnp.split(attended, 2, axis=0)
    branch = [dot(a, out_w, 1, 1).astype(LOW) for a in attended]
    middle = embedded[:held] + grid.gathered_sum(*branch)
    mean_two, scale_two = grid.stats(middle, model_width)
    hat_two = (middle - mean_two) * scale_two
    second = grid.spread((hat_two * gains[1]).astype(LOW))
    before = jnp.concatenate([dot(a, up_w).astype(LOW) for a in second], axis=0)
    before = jnp.split(grid.row_sum(before), 2, axis=0)
    hidden = [gelu_apply(b).astype(LOW) for b in before]
    after = middle + grid.gathered_sum(*[dot(a, down_w, 1, 1).astype(LOW) for a in hidden])

    aba_low = aba_weights.astype(LOW)
    final, aba_stored = aba_forward(grid.to_rows(after), aba_low, aba_gains)
    final_low = final.reshape(own_tokens, attr_count, embed_width).astype(LOW)
    logits = jnp.einsum("tfe,fec->tfc", final_low, output_low, preferred_element_type=WIDE)
    highest = jnp.max(logits, axis=-1, keepdims=True)
    exped = jnp.exp(logits - highest)
    totals = jnp.sum(exped, axis=-1, keepdims=True)
    log_total = (highest + jnp.log(totals))[:, :, 0]
    cell_weight = mask_own * jnp.sum(label_hot * class_weight[None], axis=-1)
    loss_local = jnp.sum(cell_weight * (log_total - jnp.sum(label_hot * logits, axis=-1)))
    logit_grad = ((cell_weight / weight_total)[:, :, None] * (exped / totals - label_hot)).astype(
        LOW
    )
    final_grad = jnp.einsum("tfc,fec->tfe", logit_grad, output_low, preferred_element_type=WIDE)
    output_part = jnp.einsum("tfe,tfc->fec", final_low, logit_grad, preferred_element_type=WIDE)
    rows_grad, aba_part, aba_gains_part = aba_backward(
        final_grad.reshape(own_tokens, model_width), aba_stored, aba_low, aba_gains
    )

    width = normed.shape[1] // SHARERS
    gradient_sq = []

    def row_gradients(acts, uppers):
        found = []
        for j in range(SHARERS):
            cut = slice(j * width, (j + 1) * width)
            piece = sum(dot(a[:, cut], u, 0, 0) for a, u in zip(acts, uppers)).astype(LOW)
            gradient_sq.append(jnp.sum(jnp.square(piece.astype(WIDE))))
            found.append(piece)
        return found

    upstream = grid.from_rows(rows_grad.astype(LOW))
    down_grad = grid.spread(upstream)
    hidden_grad, output_part, aba_part, aba_gains_part = tied(
        jnp.concatenate([dot(a, down_w).astype(LOW) for a in down_grad], axis=0),
        output_part,
        aba_part,
        aba_gains_part,
    )
    hidden_grad = grid.row_sum(hidden_grad)
    down_gradient = traded(row_gradients(down_grad, hidden))

    small = jnp.concatenate([aba_part.reshape(-1), aba_gains_part.reshape(-1)])
    blocks = output_part.reshape(grid.heads, -1)
    bits = (grid.heads - 1).bit_length()
    for bit in range(bits):
        flag = (h >> bit) % 2 == 1
        halves = blocks.reshape(-1, 2, blocks.shape[1])
        kept, sent = exchange(flag, halves[:, 0], halves[:, 1])
        got = grid.pair(jnp.concatenate([sent.reshape(-1), small]).reshape(-1, 128), 1 << bit)
        got = got.reshape(-1)
        blocks = kept + got[: sent.size].reshape(kept.shape)
        small = small + got[sent.size :]
    packed = jnp.concatenate([blocks.reshape(-1), small]).reshape(-1, 128)
    for step in (grid.heads, 2 * grid.heads):
        packed = packed + grid.pair(packed, step)
    packed = grid.row_sum(packed).reshape(-1)
    output_grad = packed[: blocks.size].reshape(output_table.shape)
    aba_grad = packed[blocks.size : blocks.size + aba_weights.size].reshape(aba_weights.shape)
    aba_gains_grad = packed[blocks.size + aba_weights.size :].reshape(aba_gains.shape)

    hidden_grad, down_gradient, output_grad, aba_grad, aba_gains_grad = tied(
        hidden_grad, down_gradient, output_grad, aba_grad, aba_gains_grad
    )

    before_grad = [gelu_back(b, g).astype(LOW) for b, g in zip(before, jnp.split(hidden_grad, 2, axis=0))]
    second_grad = grid.gathered_sum(*[dot(a, up_w, 1, 1).astype(LOW) for a in before_grad])
    gained = second_grad * gains[1]
    sums = jnp.stack([jnp.sum(gained, axis=1), jnp.sum(gained * hat_two, axis=1)])
    sums = sum(grid.row_list(sums)) / model_width
    middle_grad = upstream.astype(WIDE) + scale_two * (
        gained - sums[0][:, None] - hat_two * sums[1][:, None]
    )
    gain_two = jnp.sum(second_grad * hat_two, axis=0)
    branch_grad = grid.spread(middle_grad.astype(LOW))
    attended_grad = jnp.concatenate([dot(a, out_w).astype(LOW) for a in branch_grad], axis=0)
    attended_grad, second, attended = tied(attended_grad, second, attended)
    attended_grad = grid.row_sum(attended_grad).astype(LOW)
    out_gradient, up_gradient = (
        row_gradients(branch_grad, attended),
        row_gradients(second, before_grad),
    )
    other_gradient = traded(
        [jnp.concatenate(pair, axis=1) for pair in zip(out_gradient, up_gradient)]
    )
    prob_grad = dot(grid.columns(attended_grad), value_rows, 1, 1)
    score_grad = probs * (prob_grad - jnp.sum(probs * prob_grad, axis=1, keepdims=True))
    score_grad = score_grad.astype(LOW)
    query_grad = dot(score_grad, key_own) * factor
    key_grad = dot(score_grad, query_own, 0, 0) * factor
    value_grad = dot(probs_low, attended_grad, 0, 0)
    triple_grad = jnp.concatenate([query_grad, key_grad, value_grad], axis=1).astype(LOW)
    table_part = [
        dot(hot[:held], block, 0, 0)
        for hot, block in zip(hots, jnp.split(middle_grad.astype(LOW), SHARERS, axis=1))
    ]
    triple_grad, table_part = tied(triple_grad, table_part)
    qkv_gradient = row_gradients([normed], [triple_grad])
    triple_grad, qkv_gradient = tied(triple_grad, qkv_gradient)

    normed_grad = dot(triple_grad, qkv_w, 1, 1)
    gained = normed_grad * gains[0]
    sums = jnp.stack([jnp.sum(gained, axis=1), jnp.sum(gained * hat_one, axis=1)])
    sums = sum(grid.row_list(sums)) / model_width
    gain_one = jnp.sum(normed_grad * hat_one, axis=0)
    spread_grad = scale_one * (gained - sums[0][:, None] - hat_one * sums[1][:, None])
    records = []
    for j, block in enumerate(jnp.split(spread_grad.astype(LOW), SHARERS, axis=1)):
        grad = table_part[j] + dot(hots[j], block, 0, 0)
        grad = jnp.where(own_block, grad, 0.0)
        grad = jnp.dot(grad, fold.astype(WIDE), precision=lax.Precision.HIGHEST)
        cut = slice(j * width, (j + 1) * width)
        records.append(jnp.concatenate([grad.reshape(-1), gain_one[cut], gain_two[cut]]))
    table_size = block_attrs * entries * embed_width
    packed = jnp.stack(grid.ordered(records)).reshape(-1, 128)
    packed = grid.group_total(packed)
    packed, qkv_gradient = tied(packed, traded(qkv_gradient))
    gradients = qkv_gradient + other_gradient + down_gradient
    packed = jnp.stack(grid.row_gather(packed))
    packed = packed.reshape(grid.rows * SHARERS, -1)
    embed_grad = packed[:, :table_size].reshape(embed_table.shape)
    abd_gains_grad = packed[:, table_size:].reshape(-1, 2, width).transpose(1, 0, 2)
    abd_gains_grad = abd_gains_grad.reshape(2, model_width)

    output_sq = first_device * jnp.sum(output_grad * output_grad)
    summed = grid.total(jnp.stack([sum(gradient_sq), output_sq, loss_local]))
    replicated_sq = (
        jnp.sum(abd_gains_grad * abd_gains_grad)
        + jnp.sum(aba_grad * aba_grad)
        + jnp.sum(aba_gains_grad * aba_gains_grad)
        + jnp.sum(embed_grad * embed_grad)
    )
    grad_norm = jnp.sqrt(summed[0] + summed[1] + replicated_sq)
    loss_sum = summed[2]
    clip_factor = jnp.minimum(1.0, CLIP_LIMIT / (grad_norm + 1e-06))
    if native:
        first_view, second_view, abd_update, squares = moments_step(
            side,
            clip_factor[None],
            weight_view,
            native_view(abd_first),
            native_view(abd_second),
            gradients,
        )
        abd_first_new = from_native(first_view, grid.each)
        abd_second_new = from_native(second_view, grid.each)
        abd_update_sq, abd_weight_sq = jnp.sum(squares[0]), jnp.sum(squares[1])
    else:
        qkv_g, other_g, down_g = (gradients[SHARERS * i : SHARERS * (i + 1)] for i in range(3))
        split_g = (qkv_g, [g[:, :out_size] for g in other_g], [g[:, out_size:] for g in other_g], down_g)
        merged = [
            grid.merge_plain(pieces, parts, size)
            for pieces, (_, parts, size) in zip(split_g, SECTIONS)
        ]
        abd_grad = jnp.concatenate(merged, axis=2).astype(WIDE)
        abd_first_new, abd_second_new, abd_update = moments_of(
            abd_weights, abd_grad, abd_first, abd_second, clip_factor, WEIGHT_DECAY
        )
        abd_update_sq, abd_weight_sq = (
            jnp.sum(abd_update * abd_update),
            jnp.sum(abd_weights * abd_weights),
        )
    output_first_new, output_second_new, output_update = moments_of(
        output_table, output_grad, output_first, output_second, clip_factor, WEIGHT_DECAY
    )
    trust_sums = grid.total(
        jnp.stack(
            [
                abd_update_sq,
                first_device * jnp.sum(output_update * output_update),
                abd_weight_sq,
                first_device * jnp.sum(output_table * output_table),
            ]
        )
    )
    if native:
        abd_new = from_native(
            apply_trust(weight_view, abd_update.astype(WIDE), trust_sums[2], trust_sums[0]),
            grid.each,
        )
    else:
        abd_new = apply_trust(abd_weights, abd_update, trust_sums[2], trust_sums[0])
    output_new = apply_trust(output_table, output_update, trust_sums[3], trust_sums[1])
    gain_triple = local_step(
        abd_gains, abd_gains_grad, abd_gains_first, abd_gains_second, clip_factor, 0.0
    )
    aba_triple = local_step(aba_weights, aba_grad, aba_first, aba_second, clip_factor, WEIGHT_DECAY)
    aba_gain_triple = local_step(
        aba_gains, aba_gains_grad, aba_gains_first, aba_gains_second, clip_factor, 0.0
    )
    embed_triple = local_step(
        embed_table, embed_grad, embed_first, embed_second, clip_factor, WEIGHT_DECAY
    )
    return (
        loss_sum,
        weight_total,
        grad_norm,
        abd_new,
        abd_first_new,
        abd_second_new,
        *gain_triple,
        *aba_triple,
        *aba_gain_triple,
        *embed_triple,
        output_new,
        output_first_new,
        output_second_new,
    )


def solution(mesh):
    grid = Grid(mesh.shape["dp"], mesh.shape["head"])
    devices = Mesh(mesh.devices.reshape(grid.shape), ("a", "q", "p", "h"))
    rows = ("a", "q", "p")
    tokens, table = P(rows, None), P("h", None, None)
    weight = P(rows, "h", None)
    in_specs = (tokens, tokens, P(rows, "h"), weight, weight, weight) + (P(),) * 12 + (table,) * 3
    out_specs = (P(),) * 3 + (weight,) * 3 + (P(),) * 12 + (table,) * 3
    return jax.shard_map(
        functools.partial(per_device, grid),
        mesh=devices,
        in_specs=in_specs,
        out_specs=out_specs,
        check_vma=False,
    )
```

```python
import functools

import jax
import jax.experimental.pallas as pl
import jax.experimental.pallas.tpu as pltpu
import jax.numpy as jnp
from jax import lax
from jax.sharding import Mesh
from jax.sharding import PartitionSpec as P

H = 8
AH = 8
STEP = 10
HD = 512
FF = 16384


EPS_NORM = 1e-05
CLIP_LIMIT = 0.01
LEARN_RATE = 0.3
BETA_FIRST = 0.9
BETA_SECOND = 0.999
ADAM_EPSILON = 1e-08
WEIGHT_DECAY = 0.01


def layer_norm(values, gain_row):
    center = jnp.mean(values, axis=-1, keepdims=True)
    centred = values - center
    spread = jnp.mean(centred * centred, axis=-1, keepdims=True)
    return centred * lax.rsqrt(spread + EPS_NORM) * gain_row


def gelu_apply(values):
    return 0.5 * values * (1.0 + lax.erf(values * 0.7071067811865476))


def norm_back(values, gain_row, upstream):
    unused_value, pull_back = jax.vjp(layer_norm, values, gain_row)
    return pull_back(upstream)


def gelu_back(values, upstream):
    unused_value, pull_back = jax.vjp(gelu_apply, values)
    return pull_back(upstream)[0]


def attend_keys(queries, key_rows, value_rows, factor):
    scores = (
        jnp.einsum("...qd,...kd->...qk", queries, key_rows, preferred_element_type=jnp.float32)
        * factor
    )
    highest = jnp.max(scores, axis=-1, keepdims=True)
    weights = jnp.exp(scores - highest)
    totals = jnp.sum(weights, axis=-1, keepdims=True)
    result = jnp.einsum(
        "...qk,...kd->...qd",
        (weights / totals).astype(jnp.bfloat16),
        value_rows,
        preferred_element_type=jnp.float32,
    )
    return (result, highest + jnp.log(totals))


def attend_back(queries, key_rows, value_rows, log_total, result_grad, factor):
    scores = (
        jnp.einsum("...qd,...kd->...qk", queries, key_rows, preferred_element_type=jnp.float32)
        * factor
    )
    softmax_probs = jnp.exp(scores - log_total)
    prob_grad = jnp.einsum(
        "...qd,...kd->...qk", result_grad, value_rows, preferred_element_type=jnp.float32
    )
    score_grad = softmax_probs * (
        prob_grad - jnp.sum(softmax_probs * prob_grad, axis=-1, keepdims=True)
    )
    score_grad = score_grad.astype(jnp.bfloat16)
    query_grad = (
        jnp.einsum("...qk,...kd->...qd", score_grad, key_rows, preferred_element_type=jnp.float32)
        * factor
    )
    key_grad = (
        jnp.einsum("...qk,...qd->...kd", score_grad, queries, preferred_element_type=jnp.float32)
        * factor
    )
    value_grad = jnp.einsum(
        "...qk,...qd->...kd",
        softmax_probs.astype(jnp.bfloat16),
        result_grad,
        preferred_element_type=jnp.float32,
    )
    return (query_grad, key_grad, value_grad)


def aba_forward(row_block, weights, gain_rows):
    embed_width = weights.shape[0]
    row_count = row_block.shape[0]
    attr_count = row_block.shape[1] // embed_width
    size_each = embed_width // AH
    inputs = row_block.reshape(row_count, attr_count, embed_width)
    normed = layer_norm(inputs, gain_rows[0]).astype(jnp.bfloat16)
    projection = weights[:, : 3 * embed_width].reshape(embed_width, 3, AH, size_each)
    triple = jnp.einsum(
        "rfe,eshd->srhfd", normed, projection, preferred_element_type=jnp.float32
    ).astype(jnp.bfloat16)
    attended, log_total = attend_keys(triple[0], triple[1], triple[2], size_each ** (-0.5))
    attended = attended.astype(jnp.bfloat16)
    out_proj = weights[:, 3 * embed_width : 4 * embed_width].reshape(embed_width, AH, size_each)
    middle = inputs + jnp.einsum(
        "rhfd,ohd->rfo", attended, out_proj, preferred_element_type=jnp.float32
    )
    second = layer_norm(middle, gain_rows[1]).astype(jnp.bfloat16)
    before = jnp.einsum(
        "rfe,eu->rfu",
        second,
        weights[:, 4 * embed_width : 8 * embed_width],
        preferred_element_type=jnp.float32,
    )
    hidden = gelu_apply(before).astype(jnp.bfloat16)
    after = middle + jnp.einsum(
        "rfu,ou->rfo", hidden, weights[:, 8 * embed_width :], preferred_element_type=jnp.float32
    )
    return (
        after.reshape(row_count, attr_count * embed_width),
        (inputs, normed, triple, log_total, attended, middle, second, before, hidden),
    )


def aba_backward(upstream, stored, weights, gain_rows):
    inputs, normed, triple, log_total, attended, middle, second, before, hidden = stored
    row_count, attr_count, embed_width = inputs.shape
    size_each = embed_width // AH
    upstream = upstream.reshape(row_count, attr_count, embed_width)
    down_grad = upstream.astype(jnp.bfloat16)
    hidden_grad = jnp.einsum(
        "rfo,ou->rfu", down_grad, weights[:, 8 * embed_width :], preferred_element_type=jnp.float32
    )
    before_grad = gelu_back(before, hidden_grad).astype(jnp.bfloat16)
    second_grad = jnp.einsum(
        "rfu,eu->rfe",
        before_grad,
        weights[:, 4 * embed_width : 8 * embed_width],
        preferred_element_type=jnp.float32,
    )
    middle_part, gain_two = norm_back(middle, gain_rows[1], second_grad)
    middle_grad = upstream + middle_part
    branch_grad = middle_grad.astype(jnp.bfloat16)
    out_proj = weights[:, 3 * embed_width : 4 * embed_width].reshape(embed_width, AH, size_each)
    attended_grad = jnp.einsum(
        "rfo,ohd->rhfd", branch_grad, out_proj, preferred_element_type=jnp.float32
    ).astype(jnp.bfloat16)
    query_grad, key_grad, value_grad = attend_back(
        triple[0], triple[1], triple[2], log_total, attended_grad, size_each ** (-0.5)
    )
    triple_grad = jnp.stack([query_grad, key_grad, value_grad]).astype(jnp.bfloat16)
    projection = weights[:, : 3 * embed_width].reshape(embed_width, 3, AH, size_each)
    normed_grad = jnp.einsum(
        "srhfd,eshd->rfe", triple_grad, projection, preferred_element_type=jnp.float32
    )
    input_part, gain_one = norm_back(inputs, gain_rows[0], normed_grad)
    input_grad = middle_grad + input_part
    weight_grad = jnp.concatenate(
        [
            jnp.einsum(
                "rfe,srhfd->eshd", normed, triple_grad, preferred_element_type=jnp.float32
            ).reshape(embed_width, 3 * embed_width),
            jnp.einsum(
                "rfo,rhfd->ohd", branch_grad, attended, preferred_element_type=jnp.float32
            ).reshape(embed_width, embed_width),
            jnp.einsum("rfe,rfu->eu", second, before_grad, preferred_element_type=jnp.float32),
            jnp.einsum("rfo,rfu->ou", down_grad, hidden, preferred_element_type=jnp.float32),
        ],
        axis=1,
    )
    return (
        input_grad.reshape(row_count, attr_count * embed_width),
        weight_grad,
        jnp.stack([gain_one, gain_two]),
    )


def moments_of(weight, gradient, first, second, clip_factor, decay):
    scaled = gradient * clip_factor
    first_new = BETA_FIRST * first + (1.0 - BETA_FIRST) * scaled
    second_new = BETA_SECOND * second + (1.0 - BETA_SECOND) * scaled * scaled
    update = (
        first_new
        / (1.0 - BETA_FIRST**STEP)
        / (jnp.sqrt(second_new / (1.0 - BETA_SECOND**STEP)) + ADAM_EPSILON)
        + decay * weight
    )
    return (first_new, second_new, update)


def apply_trust(weight, update, weight_sq, update_sq):
    trust_ratio = jnp.sqrt(weight_sq) / (jnp.sqrt(update_sq) + 1e-06)
    return weight - LEARN_RATE * trust_ratio * update


def local_step(weight, gradient, first, second, clip_factor, decay):
    first_new, second_new, update = moments_of(weight, gradient, first, second, clip_factor, decay)
    return (
        apply_trust(weight, update, jnp.sum(weight * weight), jnp.sum(update * update)),
        first_new,
        second_new,
    )


LOW = jnp.bfloat16
WIDE = jnp.float32
SHARERS = 4
FIRST_SCALE = 1.0 / (1.0 - BETA_FIRST**STEP)
SECOND_SCALE = 1.0 / (1.0 - BETA_SECOND**STEP)
UNITS = FF // H
SOURCES = ((0, 0), (0, 3 * HD // 2), (1, 0), (2, 0))
SECTIONS = ((0, 3, HD), (3 * HD, 1, HD), (4 * HD, 1, UNITS), (4 * HD + UNITS, 1, UNITS))


def dot(left, right, left_dim=1, right_dim=0):
    return lax.dot_general(
        left, right, (((left_dim,), (right_dim,)), ((), ())), preferred_element_type=WIDE
    )


def native_view(values):
    rows, heads, columns = values.shape
    return (
        values.reshape(rows, heads, columns // 128, 128)
        .transpose(0, 2, 1, 3)
        .reshape(rows, columns // 128 * heads, 128)
    )


def from_native(values, heads):
    rows, count, width = values.shape
    return (
        values.reshape(rows, count // heads, heads, width)
        .transpose(0, 2, 1, 3)
        .reshape(rows, heads, count // heads * width)
    )


def tile_pairs(parts, width):
    each = width // 128
    return [
        (part * each + i, part * each + each // 2 + i)
        for part in range(parts)
        for i in range(each // 2)
    ]


def exchange(flag, left, right):
    return jnp.where(flag, right, left), jnp.where(flag, left, right)


def cross(q_flag, p_flag, values):
    a, b = exchange(p_flag, values[0], values[1])
    c, d = exchange(p_flag, values[2], values[3])
    a, c = exchange(q_flag, a, c)
    b, d = exchange(q_flag, b, d)
    return a, b, c, d


def split_kernel(sections, side_ref, *refs):
    weight_refs, out_refs = refs[: len(sections)], refs[len(sections) :]
    q_flag, p_flag = side_ref[0] == 1, side_ref[1] == 1
    lane = 0
    for weight_ref, (_, parts, width) in zip(weight_refs, sections):
        turned = {}
        for left, right in tile_pairs(parts, width):
            for group in (left // 4, right // 4):
                if group not in turned:
                    rows = weight_ref[:, group * 8 : group * 8 + 8, :]
                    turned[group] = jnp.swapaxes(rows, 0, 1)
            values = [
                turned[t // 4][t % 4 * 2 + head] for head in range(2) for t in (left, right)
            ]
            for ref, value in zip(out_refs, cross(q_flag, p_flag, values)):
                ref[:, lane : lane + 128] = value.astype(LOW)
            lane += 128


def split_weights(view, side, sections):
    rows = view.shape[0]
    total = sum(parts * width for _, parts, width in sections)
    block = 32

    def section_spec(offset, size):
        return pl.BlockSpec((block, size // 64, 128), lambda i: (i, offset // size, 0))

    return pl.pallas_call(
        functools.partial(split_kernel, sections),
        out_shape=[jax.ShapeDtypeStruct((rows, total // 2), LOW)] * SHARERS,
        grid=(rows // block,),
        in_specs=[pl.BlockSpec(memory_space=pltpu.SMEM)]
        + [section_spec(offset, parts * width) for offset, parts, width in sections],
        out_specs=[pl.BlockSpec((block, total // 2), lambda i: (i, 0))] * SHARERS,
        compiler_params=pltpu.CompilerParams(vmem_limit_bytes=40 * 2**20),
        cost_estimate=pl.CostEstimate(flops=1, bytes_accessed=1, transcendentals=0),
    )(side, *[view] * len(sections))


def moments_kernel(side_ref, clip_ref, weight_ref, first_ref, second_ref, *rest):
    gradients, (first_out, second_out, update_out, total_ref) = rest[:-4], rest[-4:]
    q_flag, p_flag = side_ref[0] == 1, side_ref[1] == 1
    clip = clip_ref[0]

    @pl.when(pl.program_id(0) == 0)
    def _():
        total_ref[...] = jnp.zeros_like(total_ref)

    update_sq = jnp.zeros((8, 128), WIDE)
    weight_sq = jnp.zeros((8, 128), WIDE)
    for (offset, parts, width), (index, lane) in zip(SECTIONS, SOURCES):
        refs = gradients[SHARERS * index : SHARERS * (index + 1)]
        places = {}
        for tile, (left, right) in enumerate(tile_pairs(parts, width)):
            lanes = slice(lane + tile * 128, lane + tile * 128 + 128)
            values = [ref[:, lanes].astype(WIDE) for ref in refs]
            a, b, c, d = cross(q_flag, p_flag, values)
            places[2 * left], places[2 * right] = a, b
            places[2 * left + 1], places[2 * right + 1] = c, d
            for group in (left // 4, right // 4):
                rows = range(group * 8, group * 8 + 8)
                if any(row not in places for row in rows):
                    continue
                scaled = jnp.swapaxes(jnp.stack([places.pop(r) for r in rows], axis=0), 0, 1) * clip
                here = pl.ds(offset // 64 + group * 8, 8)
                weight = weight_ref[:, here, :]
                first_new = BETA_FIRST * first_ref[:, here, :] + (1.0 - BETA_FIRST) * scaled
                second_new = (
                    BETA_SECOND * second_ref[:, here, :] + (1.0 - BETA_SECOND) * scaled * scaled
                )
                first_out[:, here, :] = first_new
                second_out[:, here, :] = second_new
                update = (
                    first_new * FIRST_SCALE / (jnp.sqrt(second_new * SECOND_SCALE) + ADAM_EPSILON)
                    + WEIGHT_DECAY * weight
                )
                update_out[:, here, :] = update.astype(update_out.dtype)
                update_sq += jnp.sum(update * update, axis=0)
                weight_sq += jnp.sum(weight * weight, axis=0)
    total_ref[0] += update_sq
    total_ref[1] += weight_sq


def moments_step(side, clip, weight, first, second, gradients):
    rows, depth, _ = weight.shape
    block = 32
    whole = pl.BlockSpec((block, depth, 128), lambda i: (i, 0, 0))
    shape = jax.ShapeDtypeStruct(weight.shape, WIDE)
    return pl.pallas_call(
        moments_kernel,
        out_shape=[
            shape,
            shape,
            jax.ShapeDtypeStruct(weight.shape, LOW),
            jax.ShapeDtypeStruct((2, 8, 128), WIDE),
        ],
        grid=(rows // block,),
        in_specs=[pl.BlockSpec(memory_space=pltpu.SMEM)] * 2
        + [whole] * 3
        + [pl.BlockSpec((block, g.shape[1]), lambda i: (i, 0)) for g in gradients],
        out_specs=[whole] * 3 + [pl.BlockSpec((2, 8, 128), lambda i: (0, 0, 0))],
        compiler_params=pltpu.CompilerParams(vmem_limit_bytes=48 * 2**20),
        cost_estimate=pl.CostEstimate(
            flops=weight.size * 20, bytes_accessed=weight.size * 24, transcendentals=weight.size
        ),
    )(side, clip, weight, first, second, *gradients)


def embed_kernel(picked_ref, expand_ref, entry_ref, table_ref, fold_ref, block_ref, hot_ref, out_ref):
    hot = (dot(picked_ref[...], expand_ref[0]) == entry_ref[...]).astype(LOW)
    hot_ref[0] = hot
    total = 0.0
    for i in (2, 1, 0):
        wide = (dot(table_ref[0, i], fold_ref[...], 1, 1) * block_ref[...]).astype(LOW)
        total = total + dot(hot, wide)
    out_ref[...] = total


def embed_tokens(picked, expand, entry, table, fold, block):
    tokens, rows, width = picked.shape[0], entry.shape[1], fold.shape[0]
    return pl.pallas_call(
        embed_kernel,
        out_shape=[
            jax.ShapeDtypeStruct((SHARERS, tokens, rows), LOW),
            jax.ShapeDtypeStruct((tokens, SHARERS * width), WIDE),
        ],
        grid=(SHARERS,),
        in_specs=[
            pl.BlockSpec(picked.shape, lambda j: (0, 0)),
            pl.BlockSpec((1, *expand.shape[1:]), lambda j: (j, 0, 0)),
            pl.BlockSpec(entry.shape, lambda j: (0, 0)),
            pl.BlockSpec((1, *table.shape[1:]), lambda j: (j, 0, 0, 0)),
            pl.BlockSpec(fold.shape, lambda j: (0, 0)),
            pl.BlockSpec(block.shape, lambda j: (0, 0)),
        ],
        out_specs=[
            pl.BlockSpec((1, tokens, rows), lambda j: (j, 0, 0)),
            pl.BlockSpec((tokens, width), lambda j: (0, j)),
        ],
        compiler_params=pltpu.CompilerParams(vmem_limit_bytes=40 * 2**20),
        cost_estimate=pl.CostEstimate(flops=1, bytes_accessed=1, transcendentals=0),
    )(picked, expand, entry, table, fold, block)


def join_kernel(*refs):
    rows = refs[0].shape[0]
    for k, ref in enumerate(refs[:-1]):
        refs[-1][k * rows : (k + 1) * rows, :] = ref[...]


def join_blocks(parts, turns):
    rows, columns = parts[0].shape
    width = columns // SHARERS
    return pl.pallas_call(
        join_kernel,
        out_shape=jax.ShapeDtypeStruct((len(parts) * rows, columns), parts[0].dtype),
        grid=(SHARERS,),
        in_specs=[pl.BlockSpec((rows, width), lambda j, t=t: (0, j ^ t)) for t in turns],
        out_specs=pl.BlockSpec((len(parts) * rows, width), lambda j: (0, j)),
        cost_estimate=pl.CostEstimate(
            flops=0, bytes_accessed=4 * len(parts) * rows * columns, transcendentals=0
        ),
    )(*parts)


def part_kernel(*refs):
    count = len(refs) // 3
    for left, right, out in zip(refs[:count], refs[count : 2 * count], refs[2 * count :]):
        out[...] = (left[...].astype(WIDE) + right[...].astype(WIDE)).astype(out.dtype)


def part_sums(left, right, turns):
    rows, columns = left.shape[0] // len(turns), left.shape[1]
    width = columns // SHARERS
    specs = [
        pl.BlockSpec((rows, width), lambda j, k=k, t=t: (k, j ^ t)) for k, t in enumerate(turns)
    ]
    return pl.pallas_call(
        part_kernel,
        out_shape=[
            jax.ShapeDtypeStruct((rows, columns), LOW if k else WIDE) for k in range(len(turns))
        ],
        grid=(SHARERS,),
        in_specs=specs + specs,
        out_specs=[pl.BlockSpec((rows, width), lambda j: (0, j))] * len(turns),
        cost_estimate=pl.CostEstimate(
            flops=left.size, bytes_accessed=6 * left.size, transcendentals=0
        ),
    )(*[left] * len(turns), *[right] * len(turns))


class Grid:
    def __init__(self, rows, heads):
        self.rows, self.heads = rows // SHARERS, heads
        self.each = H // heads
        self.parts = SHARERS // self.each
        self.members = SHARERS * heads
        self.shape = (self.rows, self.each, self.parts, heads)
        self.evens = range(2, self.members, 2)

    def sharer(self):
        return lax.axis_index("q") * self.parts + lax.axis_index("p")

    def pair(self, values, step):
        return lax.ppermute(values, ("q", "p", "h"), [(i, i ^ step) for i in range(self.members)])

    def trade(self, values, step):
        return lax.ppermute(values, ("q", "p"), [(i, i ^ step) for i in range(SHARERS)])

    def turns(self):
        return [0] + [d // self.heads for d in self.evens]

    def spread(self, own):
        parts = [own] + [self.pair(own, d) for d in self.evens]
        half = join_blocks(parts, self.turns())
        return half, self.pair(half, 1)

    def gathered_sum(self, half, other):
        parts = part_sums(half, self.pair(other, 1), self.turns())
        total = parts[0]
        for part, d in zip(parts[1:], self.evens):
            total = total + self.pair(part, d).astype(WIDE)
        return total

    def group_total(self, values):
        step = 1
        while step < self.members:
            values = values + self.pair(values, step)
            step *= 2
        return values

    def every(self, values):
        step = 1
        while step < self.members:
            values = jnp.concatenate([values, self.pair(values, step)], axis=0)
            step *= 2
        step = 1
        while step < self.rows:
            moved = lax.ppermute(values, "a", [(i, i ^ step) for i in range(self.rows)])
            values = jnp.concatenate([values, moved], axis=0)
            step *= 2
        return values

    def facing(self, values):
        return lax.ppermute(values, "a", [(0, 1), (1, 0)])

    def row_list(self, values):
        if self.rows == 2:
            return [values, self.facing(values)]
        every = lax.all_gather(values, "a", axis=0)
        return [every[i] for i in range(self.rows)]

    def row_gather(self, values):
        parts = self.row_list(values)
        if self.rows == 2:
            flag = lax.axis_index("a") == 1
            parts = exchange(flag, *parts)
        return list(parts)

    def row_sum(self, values):
        if self.rows == 2:
            return values.astype(WIDE) + self.facing(values).astype(WIDE)
        return lax.psum(values.astype(WIDE), "a")

    def total(self, values):
        return self.row_sum(self.group_total(values))

    def ordered(self, parts):
        place = self.sharer()
        low, high = place % 2 == 1, place // 2 == 1
        parts = [jnp.where(low, parts[j ^ 1], parts[j]) for j in range(SHARERS)]
        return [jnp.where(high, parts[j ^ 2], parts[j]) for j in range(SHARERS)]

    def absolute(self, values):
        return jnp.concatenate(self.ordered(jnp.split(values, SHARERS, axis=-1)), axis=-1)

    def to_rows(self, values):
        values = self.absolute(values)
        if self.rows != 2:
            return lax.all_to_all(values, "a", split_axis=0, concat_axis=1, tiled=True)
        flag = lax.axis_index("a") == 1
        kept, sent = exchange(flag, *jnp.split(values, 2, axis=0))
        return jnp.concatenate(exchange(flag, kept, self.facing(sent)), axis=1)

    def from_rows(self, values):
        if self.rows != 2:
            return self.absolute(
                lax.all_to_all(values, "a", split_axis=1, concat_axis=0, tiled=True)
            )
        flag = lax.axis_index("a") == 1
        kept, sent = exchange(flag, *jnp.split(values, 2, axis=1))
        moved = jnp.concatenate(exchange(flag, kept, self.facing(sent)), axis=0)
        return self.absolute(moved)

    def renamed(self, values, step):
        block = values.shape[0] // self.members
        span = 1
        while span < self.members // 2:
            if step // 2 & span:
                halves = values.reshape(-1, 2, span * block, values.shape[1])
                values = jnp.stack([halves[:, 1], halves[:, 0]], axis=1).reshape(values.shape)
            span *= 2
        return values

    def columns(self, values):
        found = [values]
        for d in range(1, self.parts):
            got = lax.ppermute(values, "p", [(i, i ^ d) for i in range(self.parts)])
            found.append(self.renamed(got, d * self.heads))
        return jnp.concatenate(found, axis=1)

    def local(self, values, axis):
        size = values.shape[axis] // (self.rows * SHARERS)
        first, place = lax.axis_index("a") * SHARERS, self.sharer()
        return [
            lax.dynamic_slice_in_dim(values, (first + (place ^ j)) * size, size, axis)
            for j in range(SHARERS)
        ]

    def stats(self, values, count):
        center = jnp.mean(values, axis=1)
        spread = jnp.sum(jnp.square(values - center[:, None]), axis=1)
        parts = self.row_list(jnp.stack([center, spread]))
        mean = sum(part[0] for part in parts) / self.rows
        size = count // self.rows
        square = sum(part[1] + size * jnp.square(part[0] - mean) for part in parts)
        return mean[:, None], lax.rsqrt(square / count + EPS_NORM)[:, None]

    def split_plain(self, values, parts, width):
        rows = values.shape[0]
        values = values.astype(LOW).reshape(rows, self.each, parts, self.parts, -1)
        values = values.transpose(1, 3, 0, 2, 4).reshape(SHARERS, rows, -1)
        return [
            lax.dynamic_index_in_dim(values, self.sharer() ^ j, 0, False) for j in range(SHARERS)
        ]

    def merge_plain(self, pieces, parts, width):
        values = jnp.stack(self.ordered(pieces))
        rows = values.shape[1]
        values = values.reshape(self.each, self.parts, rows, parts, -1)
        return values.transpose(2, 0, 3, 1, 4).reshape(rows, self.each, parts * width)


def tied(*values):
    return lax.optimization_barrier(values)


def split_three(values):
    high = lax.reduce_precision(values, 8, 7)
    rest = values - high
    middle = lax.reduce_precision(rest, 8, 7)
    return high.astype(LOW), middle.astype(LOW), (rest - middle).astype(LOW)


def per_device(grid, *arguments):
    (
        cell_ids,
        cell_mask,
        labels,
        abd_weights,
        abd_first,
        abd_second,
        abd_gains,
        abd_gains_first,
        abd_gains_second,
        aba_weights,
        aba_first,
        aba_second,
        aba_gains,
        aba_gains_first,
        aba_gains_second,
        embed_table,
        embed_first,
        embed_second,
        output_table,
        output_first,
        output_second,
    ) = arguments
    h = lax.axis_index("h")
    attr_count, entries, embed_width = embed_table.shape
    classes = output_table.shape[2]
    model_width = attr_count * embed_width
    own_tokens = cell_ids.shape[0] // grid.heads
    first_device = ((lax.axis_index("a") == 0) & (grid.sharer() == 0)).astype(WIDE)
    native = grid.each == 2
    side = jnp.stack([lax.axis_index("q"), lax.axis_index("p")]).astype(jnp.int32)

    def own_rows(values):
        return lax.dynamic_slice_in_dim(values, h * own_tokens, own_tokens, 0)

    attrs_held = labels.shape[1]
    mask_held = lax.dynamic_slice_in_dim(cell_mask, h * attrs_held, attrs_held, 1)
    codes = jnp.where(mask_held == 1, labels, -1).reshape(own_tokens, attr_count)
    picked = own_rows(jnp.where(cell_mask == 1, classes, cell_ids))
    gathered = grid.every(jnp.concatenate([picked, codes], axis=1).astype(LOW))
    tokens = gathered.shape[0]
    picked_all = gathered[:, :attr_count]
    codes_all = gathered[:, attr_count:].reshape(-1, grid.heads, own_tokens, attr_count)
    device = (lax.axis_index("a") * SHARERS + grid.sharer()) * grid.heads + h

    def by_head(parts):
        for bit in range((grid.heads - 1).bit_length()):
            flag = (h >> bit) % 2 == 1
            parts = [
                jnp.where(flag, parts[d ^ (1 << bit)], parts[d]) for d in range(grid.heads)
            ]
        return parts

    def pieces_of(sections):
        if native:
            return split_weights(weight_view, side, sections)
        found = []
        for offset, parts, size in sections:
            columns = abd_weights[:, :, offset : offset + parts * size]
            found.append(grid.split_plain(columns, parts, size))
        return [jnp.concatenate(piece, axis=1) for piece in zip(*found)]

    def traded(values):
        return [values[0]] + [grid.trade(values[j], j) for j in (1, 2, 3)]

    weight_view = native_view(abd_weights) if native else None
    qkv_pieces, picked_all, side, table = tied(
        pieces_of(SECTIONS[:1]), picked_all, side, embed_table
    )
    qkv_w = traded(qkv_pieces)
    picked_all, other_pieces = tied(picked_all, pieces_of(SECTIONS[1:3]))
    qkv_w, other_pieces, side = tied(qkv_w, other_pieces, side)
    qkv_w = jnp.concatenate(qkv_w, axis=0)
    others = traded(other_pieces)

    held = tokens // grid.members
    place = jnp.arange(tokens, dtype=jnp.int32)
    owner, inside = place // held, place % held
    owner = 2 * (owner % (grid.members // 2)) + owner // (grid.members // 2)
    owner = owner ^ (grid.sharer() * grid.heads + h)
    source = (inside // own_tokens * grid.members + owner) ^ device
    row_of = source * own_tokens + inside % own_tokens
    picked = dot((row_of[:, None] == place[None, :]).astype(LOW), picked_all).astype(LOW)
    picked = jnp.concatenate(grid.local(picked, 1), axis=1)
    local_attrs = picked.shape[1]
    block_attrs = local_attrs // SHARERS
    table_rows = jnp.arange(block_attrs * entries, dtype=jnp.int32)
    row_attr, row_entry = table_rows // entries, (table_rows % entries).astype(WIDE)
    block_columns = jnp.arange(block_attrs * embed_width, dtype=jnp.int32)
    own_block = row_attr[:, None] == block_columns // embed_width
    fold = (
        block_columns[:, None] % embed_width == jnp.arange(embed_width, dtype=jnp.int32)
    ).astype(LOW)
    table = jnp.stack(grid.local(table, 0)).reshape(SHARERS, row_attr.size, embed_width)
    places = jnp.arange(local_attrs, dtype=jnp.int32)
    expand = places[None, :, None] == (
        jnp.arange(SHARERS, dtype=jnp.int32)[:, None, None] * block_attrs + row_attr[None, None, :]
    )
    hots, embedded = embed_tokens(
        picked,
        expand.astype(LOW),
        row_entry[None, :],
        jnp.stack(split_three(table), axis=1),
        fold,
        own_block.astype(WIDE),
    )

    kinds = jnp.arange(classes, dtype=jnp.int32).astype(WIDE)
    mask_own = own_rows(cell_mask).astype(WIDE)
    counts, own_codes = [], []
    for d in range(grid.heads):
        found = (codes_all[:, d].reshape(-1, attr_count)[:, :, None].astype(WIDE) == kinds)
        found = jnp.sum(found.astype(WIDE), axis=0)
        counts.append(jnp.sum(found.reshape(-1, attrs_held, classes), axis=0))
        own_codes.append(own_rows(codes_all[0, d].reshape(-1, attrs_held)))
    counts = jnp.concatenate(by_head(counts), axis=0)
    own_codes = jnp.concatenate(by_head(own_codes), axis=1)
    label_hot = (own_codes.astype(WIDE)[:, :, None] == kinds).astype(WIDE)
    class_weight = lax.rsqrt(1.0 + counts)
    weight_total = jnp.sum(counts * class_weight)
    tables_low = output_table.astype(LOW)[None]
    step = 1
    while step < grid.heads:
        tables_low = jnp.concatenate([tables_low, grid.pair(tables_low, step)], axis=0)
        step *= 2
    output_low = jnp.concatenate(by_head(list(tables_low)), axis=0)

    out_size, up_size = HD * grid.each // SHARERS, UNITS * grid.each // SHARERS
    gains = jnp.concatenate(grid.local(abd_gains, 1), axis=1)
    mean_one, scale_one = grid.stats(embedded, model_width)
    hat_one = (embedded - mean_one) * scale_one
    normed = (hat_one * gains[0]).astype(LOW)
    triple = grid.row_sum(dot(normed, qkv_w).astype(LOW)).astype(LOW)
    triple, others, class_weight, weight_total, label_hot, output_low, down_pieces = tied(
        triple, others, class_weight, weight_total, label_hot, output_low, pieces_of(SECTIONS[3:])
    )
    part = HD // grid.parts
    query_own, key_own, value_own = (triple[:, i * part : (i + 1) * part] for i in range(3))
    queries, key_rows = grid.columns(query_own), grid.columns(key_own)
    value_rows = grid.columns(value_own)
    factor = HD ** (-0.5)
    scores = dot(queries, key_rows, 1, 1) * factor
    shifted = jnp.exp(scores - jnp.max(scores, axis=1, keepdims=True))
    probs = shifted / jnp.sum(shifted, axis=1, keepdims=True)
    probs_low = probs.astype(LOW)
    attended = dot(probs_low, value_own).astype(LOW)
    out_w = jnp.concatenate([piece[:, :out_size] for piece in others], axis=0)
    up_w = jnp.concatenate([piece[:, out_size:] for piece in others], axis=0)
    attended = jnp.split(attended, 2, axis=0)
    branch = [dot(a, out_w, 1, 1).astype(LOW) for a in attended]
    middle = embedded[:held] + grid.gathered_sum(*branch)
    mean_two, scale_two = grid.stats(middle, model_width)
    hat_two = (middle - mean_two) * scale_two
    second = grid.spread((hat_two * gains[1]).astype(LOW))
    before = jnp.concatenate([dot(a, up_w).astype(LOW) for a in second], axis=0)
    before, down_pieces = tied(before, down_pieces)
    before, down_w, up_turned, qkv_turned = tied(
        grid.row_sum(before), traded(down_pieces), up_w.T, qkv_w.T
    )
    down_w = jnp.concatenate(down_w, axis=0)
    before = jnp.split(before, 2, axis=0)
    hidden = [gelu_apply(b).astype(LOW) for b in before]
    after = middle + grid.gathered_sum(*[dot(a, down_w, 1, 1).astype(LOW) for a in hidden])

    aba_low = aba_weights.astype(LOW)
    final, aba_stored = aba_forward(grid.to_rows(after), aba_low, aba_gains)
    final_low = final.reshape(own_tokens, attr_count, embed_width).astype(LOW)
    logits = jnp.einsum("tfe,fec->tfc", final_low, output_low, preferred_element_type=WIDE)
    highest = jnp.max(logits, axis=-1, keepdims=True)
    exped = jnp.exp(logits - highest)
    totals = jnp.sum(exped, axis=-1, keepdims=True)
    log_total = (highest + jnp.log(totals))[:, :, 0]
    cell_weight = mask_own * jnp.sum(label_hot * class_weight[None], axis=-1)
    loss_local = jnp.sum(cell_weight * (log_total - jnp.sum(label_hot * logits, axis=-1)))
    logit_grad = ((cell_weight / weight_total)[:, :, None] * (exped / totals - label_hot)).astype(
        LOW
    )
    final_grad = jnp.einsum("tfc,fec->tfe", logit_grad, output_low, preferred_element_type=WIDE)
    output_part = jnp.einsum("tfe,tfc->fce", final_low, logit_grad, preferred_element_type=WIDE)
    rows_grad, aba_part, aba_gains_part = aba_backward(
        final_grad.reshape(own_tokens, model_width), aba_stored, aba_low, aba_gains
    )

    width = normed.shape[1] // SHARERS
    gradient_sq = []

    def row_gradients(acts, uppers):
        found = []
        for j in range(SHARERS):
            cut = slice(j * width, (j + 1) * width)
            piece = sum(dot(a[:, cut], u, 0, 0) for a, u in zip(acts, uppers)).astype(LOW)
            gradient_sq.append(jnp.sum(jnp.square(piece.astype(WIDE))))
            found.append(piece)
        return found

    upstream = grid.from_rows(rows_grad.astype(LOW))
    down_grad = grid.spread(upstream)
    hidden_grad = jnp.concatenate([dot(a, down_w).astype(LOW) for a in down_grad], axis=0)
    hidden_grad = grid.row_sum(hidden_grad)
    down_gradient = traded(row_gradients(down_grad, hidden))

    hidden_grad, down_gradient, output_part, aba_part, aba_gains_part = tied(
        hidden_grad, down_gradient, output_part, aba_part, aba_gains_part
    )

    small = jnp.concatenate([aba_part.reshape(-1), aba_gains_part.reshape(-1)])
    blocks = output_part.reshape(grid.heads, -1)
    bits = (grid.heads - 1).bit_length()
    for bit in range(bits):
        flag = (h >> bit) % 2 == 1
        halves = blocks.reshape(-1, 2, blocks.shape[1])
        kept, sent = exchange(flag, halves[:, 0], halves[:, 1])
        got = grid.pair(jnp.concatenate([sent.reshape(-1), small]).reshape(-1, 128), 1 << bit)
        got = got.reshape(-1)
        blocks = kept + got[: sent.size].reshape(kept.shape)
        small = small + got[sent.size :]
    packed = jnp.concatenate([blocks.reshape(-1), small]).reshape(-1, 128)
    for step in (grid.heads, 2 * grid.heads):
        packed = packed + grid.pair(packed, step)
    packed = grid.row_sum(packed).reshape(-1)
    output_grad = packed[: blocks.size].reshape(-1, classes, embed_width)
    aba_grad = packed[blocks.size : blocks.size + aba_weights.size].reshape(aba_weights.shape)
    aba_gains_grad = packed[blocks.size + aba_weights.size :].reshape(aba_gains.shape)


    before_grad = [gelu_back(b, g).astype(LOW) for b, g in zip(before, jnp.split(hidden_grad, 2, axis=0))]
    second_grad = grid.gathered_sum(*[dot(a, up_turned).astype(LOW) for a in before_grad])
    gained = second_grad * gains[1]
    sums = jnp.stack([jnp.sum(gained, axis=1), jnp.sum(gained * hat_two, axis=1)])
    sums = sum(grid.row_list(sums)) / model_width
    middle_grad = upstream.astype(WIDE) + scale_two * (
        gained - sums[0][:, None] - hat_two * sums[1][:, None]
    )
    middle_grad, up_gradient, output_grad, aba_grad, aba_gains_grad = tied(
        middle_grad, row_gradients(second, before_grad), output_grad, aba_grad, aba_gains_grad
    )
    up_gradient = traded(up_gradient)
    gain_two = jnp.sum(second_grad * hat_two, axis=0)
    branch_grad = grid.spread(middle_grad.astype(LOW))
    attended_grad = jnp.concatenate([dot(a, out_w).astype(LOW) for a in branch_grad], axis=0)
    attended_grad, attended = tied(attended_grad, attended)
    attended_grad, up_gradient = tied(grid.row_sum(attended_grad).astype(LOW), up_gradient)
    out_gradient = row_gradients(branch_grad, attended)
    prob_grad = dot(grid.columns(attended_grad), value_rows, 1, 1)
    score_grad = probs * (prob_grad - jnp.sum(probs * prob_grad, axis=1, keepdims=True))
    score_grad = score_grad.astype(LOW)
    query_grad = dot(score_grad, key_own) * factor
    key_grad = dot(score_grad, query_own, 0, 0) * factor
    value_grad = dot(probs_low, attended_grad, 0, 0)
    triple_grad = jnp.concatenate([query_grad, key_grad, value_grad], axis=1).astype(LOW)
    table_part = [
        dot(hot[:held], block, 0, 0)
        for hot, block in zip(hots, jnp.split(middle_grad.astype(LOW), SHARERS, axis=1))
    ]
    triple_grad, table_part, out_gradient = tied(triple_grad, table_part, out_gradient)
    qkv_gradient = row_gradients([normed], [triple_grad])
    qkv_gradient = [jnp.concatenate(pair, axis=1) for pair in zip(qkv_gradient, out_gradient)]
    triple_grad, qkv_gradient = tied(triple_grad, qkv_gradient)

    normed_grad = dot(triple_grad, qkv_turned)
    gained = normed_grad * gains[0]
    sums = jnp.stack([jnp.sum(gained, axis=1), jnp.sum(gained * hat_one, axis=1)])
    sums = sum(grid.row_list(sums)) / model_width
    gain_one = jnp.sum(normed_grad * hat_one, axis=0)
    spread_grad = scale_one * (gained - sums[0][:, None] - hat_one * sums[1][:, None])
    records = []
    for j, block in enumerate(jnp.split(spread_grad.astype(LOW), SHARERS, axis=1)):
        grad = table_part[j] + dot(hots[j], block, 0, 0)
        grad = jnp.where(own_block, grad, 0.0)
        grad = jnp.dot(grad, fold.astype(WIDE), precision=lax.Precision.HIGHEST)
        cut = slice(j * width, (j + 1) * width)
        records.append(jnp.concatenate([grad.reshape(-1), gain_one[cut], gain_two[cut]]))
    table_size = block_attrs * entries * embed_width
    packed = jnp.stack(grid.ordered(records)).reshape(-1, 128)
    output_sq = first_device * jnp.sum(output_grad * output_grad)
    scalars = jnp.stack([sum(gradient_sq), output_sq, loss_local])
    lane = jnp.arange(8 * 128, dtype=jnp.int32).reshape(8, 128)
    scalars = sum(jnp.where(lane == i, scalars[i], 0.0) for i in range(3))
    packed, qkv_gradient = tied(packed, traded(qkv_gradient))
    gradients = qkv_gradient + up_gradient + down_gradient
    packed = jnp.stack(
        grid.row_gather(grid.group_total(jnp.concatenate([scalars, packed], axis=0)))
    )
    summed = jnp.sum(packed[:, 0, :3], axis=0)
    packed = packed[:, 8:].reshape(grid.rows * SHARERS, -1)
    embed_grad = packed[:, :table_size].reshape(embed_table.shape).transpose(1, 0, 2)
    abd_gains_grad = packed[:, table_size:].reshape(-1, 2, width).transpose(1, 0, 2)
    abd_gains_grad = abd_gains_grad.reshape(2, model_width)

    output_table, output_first, output_second = (
        values.transpose(0, 2, 1) for values in (output_table, output_first, output_second)
    )
    embed_table, embed_first, embed_second = (
        values.transpose(1, 0, 2) for values in (embed_table, embed_first, embed_second)
    )
    replicated_sq = (
        jnp.sum(abd_gains_grad * abd_gains_grad)
        + jnp.sum(aba_grad * aba_grad)
        + jnp.sum(aba_gains_grad * aba_gains_grad)
        + jnp.sum(embed_grad * embed_grad)
    )
    grad_norm = jnp.sqrt(summed[0] + summed[1] + replicated_sq)
    loss_sum = summed[2]
    clip_factor = jnp.minimum(1.0, CLIP_LIMIT / (grad_norm + 1e-06))
    if native:
        first_view, second_view, abd_update, squares = moments_step(
            side,
            clip_factor[None],
            weight_view,
            native_view(abd_first),
            native_view(abd_second),
            gradients,
        )
        abd_first_new = from_native(first_view, grid.each)
        abd_second_new = from_native(second_view, grid.each)
        abd_update_sq, abd_weight_sq = jnp.sum(squares[0]), jnp.sum(squares[1])
    else:
        first_g, up_g, down_g = (gradients[SHARERS * i : SHARERS * (i + 1)] for i in range(3))
        split_g = (
            [g[:, : 3 * out_size] for g in first_g],
            [g[:, 3 * out_size :] for g in first_g],
            up_g,
            down_g,
        )
        merged = [
            grid.merge_plain(pieces, parts, size)
            for pieces, (_, parts, size) in zip(split_g, SECTIONS)
        ]
        abd_grad = jnp.concatenate(merged, axis=2).astype(WIDE)
        abd_first_new, abd_second_new, abd_update = moments_of(
            abd_weights, abd_grad, abd_first, abd_second, clip_factor, WEIGHT_DECAY
        )
        abd_update_sq, abd_weight_sq = (
            jnp.sum(abd_update * abd_update),
            jnp.sum(abd_weights * abd_weights),
        )
    output_first_new, output_second_new, output_update = moments_of(
        output_table, output_grad, output_first, output_second, clip_factor, WEIGHT_DECAY
    )
    trust_sums = grid.total(
        jnp.stack(
            [
                abd_update_sq,
                first_device * jnp.sum(output_update * output_update),
                abd_weight_sq,
                first_device * jnp.sum(output_table * output_table),
            ]
        )
    )
    if native:
        abd_new = from_native(
            apply_trust(weight_view, abd_update.astype(WIDE), trust_sums[2], trust_sums[0]),
            grid.each,
        )
    else:
        abd_new = apply_trust(abd_weights, abd_update, trust_sums[2], trust_sums[0])
    output_new = apply_trust(output_table, output_update, trust_sums[3], trust_sums[1])
    gain_triple = local_step(
        abd_gains, abd_gains_grad, abd_gains_first, abd_gains_second, clip_factor, 0.0
    )
    aba_triple = local_step(aba_weights, aba_grad, aba_first, aba_second, clip_factor, WEIGHT_DECAY)
    aba_gain_triple = local_step(
        aba_gains, aba_gains_grad, aba_gains_first, aba_gains_second, clip_factor, 0.0
    )
    embed_triple = local_step(
        embed_table, embed_grad, embed_first, embed_second, clip_factor, WEIGHT_DECAY
    )
    return (
        loss_sum,
        weight_total,
        grad_norm,
        abd_new,
        abd_first_new,
        abd_second_new,
        *gain_triple,
        *aba_triple,
        *aba_gain_triple,
        *[values.transpose(1, 0, 2) for values in embed_triple],
        *[values.transpose(0, 2, 1) for values in (output_new, output_first_new, output_second_new)],
    )


def solution(mesh):
    grid = Grid(mesh.shape["dp"], mesh.shape["head"])
    devices = Mesh(mesh.devices.reshape(grid.shape), ("a", "q", "p", "h"))
    rows = ("a", "q", "p")
    tokens, table = P(rows, None), P("h", None, None)
    weight = P(rows, "h", None)
    in_specs = (tokens, tokens, P(rows, "h"), weight, weight, weight) + (P(),) * 12 + (table,) * 3
    out_specs = (P(),) * 3 + (weight,) * 3 + (P(),) * 12 + (table,) * 3
    return jax.shard_map(
        functools.partial(per_device, grid),
        mesh=devices,
        in_specs=in_specs,
        out_specs=out_specs,
        check_vma=False,
    )
```

```python
import functools

import jax
import jax.experimental.pallas as pl
import jax.experimental.pallas.tpu as pltpu
import jax.numpy as jnp
from jax import lax
from jax.sharding import Mesh
from jax.sharding import PartitionSpec as P

H = 8
AH = 8
STEP = 10
HD = 512
FF = 16384


EPS_NORM = 1e-05
CLIP_LIMIT = 0.01
LEARN_RATE = 0.3
BETA_FIRST = 0.9
BETA_SECOND = 0.999
ADAM_EPSILON = 1e-08
WEIGHT_DECAY = 0.01


def layer_norm(values, gain_row):
    center = jnp.mean(values, axis=-1, keepdims=True)
    centred = values - center
    spread = jnp.mean(centred * centred, axis=-1, keepdims=True)
    return centred * lax.rsqrt(spread + EPS_NORM) * gain_row


def gelu_apply(values):
    return 0.5 * values * (1.0 + lax.erf(values * 0.7071067811865476))


def norm_back(values, gain_row, upstream):
    unused_value, pull_back = jax.vjp(layer_norm, values, gain_row)
    return pull_back(upstream)


def gelu_back(values, upstream):
    unused_value, pull_back = jax.vjp(gelu_apply, values)
    return pull_back(upstream)[0]


def attend_keys(queries, key_rows, value_rows, factor):
    scores = (
        jnp.einsum("...qd,...kd->...qk", queries, key_rows, preferred_element_type=jnp.float32)
        * factor
    )
    highest = jnp.max(scores, axis=-1, keepdims=True)
    weights = jnp.exp(scores - highest)
    totals = jnp.sum(weights, axis=-1, keepdims=True)
    result = jnp.einsum(
        "...qk,...kd->...qd",
        (weights / totals).astype(jnp.bfloat16),
        value_rows,
        preferred_element_type=jnp.float32,
    )
    return (result, highest + jnp.log(totals))


def attend_back(queries, key_rows, value_rows, log_total, result_grad, factor):
    scores = (
        jnp.einsum("...qd,...kd->...qk", queries, key_rows, preferred_element_type=jnp.float32)
        * factor
    )
    softmax_probs = jnp.exp(scores - log_total)
    prob_grad = jnp.einsum(
        "...qd,...kd->...qk", result_grad, value_rows, preferred_element_type=jnp.float32
    )
    score_grad = softmax_probs * (
        prob_grad - jnp.sum(softmax_probs * prob_grad, axis=-1, keepdims=True)
    )
    score_grad = score_grad.astype(jnp.bfloat16)
    query_grad = (
        jnp.einsum("...qk,...kd->...qd", score_grad, key_rows, preferred_element_type=jnp.float32)
        * factor
    )
    key_grad = (
        jnp.einsum("...qk,...qd->...kd", score_grad, queries, preferred_element_type=jnp.float32)
        * factor
    )
    value_grad = jnp.einsum(
        "...qk,...qd->...kd",
        softmax_probs.astype(jnp.bfloat16),
        result_grad,
        preferred_element_type=jnp.float32,
    )
    return (query_grad, key_grad, value_grad)


def aba_forward(row_block, weights, gain_rows):
    embed_width = weights.shape[0]
    row_count = row_block.shape[0]
    attr_count = row_block.shape[1] // embed_width
    size_each = embed_width // AH
    inputs = row_block.reshape(row_count, attr_count, embed_width)
    normed = layer_norm(inputs, gain_rows[0]).astype(jnp.bfloat16)
    projection = weights[:, : 3 * embed_width].reshape(embed_width, 3, AH, size_each)
    triple = jnp.einsum(
        "rfe,eshd->srhfd", normed, projection, preferred_element_type=jnp.float32
    ).astype(jnp.bfloat16)
    attended, log_total = attend_keys(triple[0], triple[1], triple[2], size_each ** (-0.5))
    attended = attended.astype(jnp.bfloat16)
    out_proj = weights[:, 3 * embed_width : 4 * embed_width].reshape(embed_width, AH, size_each)
    middle = inputs + jnp.einsum(
        "rhfd,ohd->rfo", attended, out_proj, preferred_element_type=jnp.float32
    )
    second = layer_norm(middle, gain_rows[1]).astype(jnp.bfloat16)
    before = jnp.einsum(
        "rfe,eu->rfu",
        second,
        weights[:, 4 * embed_width : 8 * embed_width],
        preferred_element_type=jnp.float32,
    )
    hidden = gelu_apply(before).astype(jnp.bfloat16)
    after = middle + jnp.einsum(
        "rfu,ou->rfo", hidden, weights[:, 8 * embed_width :], preferred_element_type=jnp.float32
    )
    return (
        after.reshape(row_count, attr_count * embed_width),
        (inputs, normed, triple, log_total, attended, middle, second, before, hidden),
    )


def aba_backward(upstream, stored, weights, gain_rows):
    inputs, normed, triple, log_total, attended, middle, second, before, hidden = stored
    row_count, attr_count, embed_width = inputs.shape
    size_each = embed_width // AH
    upstream = upstream.reshape(row_count, attr_count, embed_width)
    down_grad = upstream.astype(jnp.bfloat16)
    hidden_grad = jnp.einsum(
        "rfo,ou->rfu", down_grad, weights[:, 8 * embed_width :], preferred_element_type=jnp.float32
    )
    before_grad = gelu_back(before, hidden_grad).astype(jnp.bfloat16)
    second_grad = jnp.einsum(
        "rfu,eu->rfe",
        before_grad,
        weights[:, 4 * embed_width : 8 * embed_width],
        preferred_element_type=jnp.float32,
    )
    middle_part, gain_two = norm_back(middle, gain_rows[1], second_grad)
    middle_grad = upstream + middle_part
    branch_grad = middle_grad.astype(jnp.bfloat16)
    out_proj = weights[:, 3 * embed_width : 4 * embed_width].reshape(embed_width, AH, size_each)
    attended_grad = jnp.einsum(
        "rfo,ohd->rhfd", branch_grad, out_proj, preferred_element_type=jnp.float32
    ).astype(jnp.bfloat16)
    query_grad, key_grad, value_grad = attend_back(
        triple[0], triple[1], triple[2], log_total, attended_grad, size_each ** (-0.5)
    )
    triple_grad = jnp.stack([query_grad, key_grad, value_grad]).astype(jnp.bfloat16)
    projection = weights[:, : 3 * embed_width].reshape(embed_width, 3, AH, size_each)
    normed_grad = jnp.einsum(
        "srhfd,eshd->rfe", triple_grad, projection, preferred_element_type=jnp.float32
    )
    input_part, gain_one = norm_back(inputs, gain_rows[0], normed_grad)
    input_grad = middle_grad + input_part
    weight_grad = jnp.concatenate(
        [
            jnp.einsum(
                "rfe,srhfd->eshd", normed, triple_grad, preferred_element_type=jnp.float32
            ).reshape(embed_width, 3 * embed_width),
            jnp.einsum(
                "rfo,rhfd->ohd", branch_grad, attended, preferred_element_type=jnp.float32
            ).reshape(embed_width, embed_width),
            jnp.einsum("rfe,rfu->eu", second, before_grad, preferred_element_type=jnp.float32),
            jnp.einsum("rfo,rfu->ou", down_grad, hidden, preferred_element_type=jnp.float32),
        ],
        axis=1,
    )
    return (
        input_grad.reshape(row_count, attr_count * embed_width),
        weight_grad,
        jnp.stack([gain_one, gain_two]),
    )


def moments_of(weight, gradient, first, second, clip_factor, decay):
    scaled = gradient * clip_factor
    first_new = BETA_FIRST * first + (1.0 - BETA_FIRST) * scaled
    second_new = BETA_SECOND * second + (1.0 - BETA_SECOND) * scaled * scaled
    update = (
        first_new
        / (1.0 - BETA_FIRST**STEP)
        / (jnp.sqrt(second_new / (1.0 - BETA_SECOND**STEP)) + ADAM_EPSILON)
        + decay * weight
    )
    return (first_new, second_new, update)


def apply_trust(weight, update, weight_sq, update_sq):
    trust_ratio = jnp.sqrt(weight_sq) / (jnp.sqrt(update_sq) + 1e-06)
    return weight - LEARN_RATE * trust_ratio * update


def local_step(weight, gradient, first, second, clip_factor, decay):
    first_new, second_new, update = moments_of(weight, gradient, first, second, clip_factor, decay)
    return (
        apply_trust(weight, update, jnp.sum(weight * weight), jnp.sum(update * update)),
        first_new,
        second_new,
    )


LOW = jnp.bfloat16
WIDE = jnp.float32
SHARERS = 4
FIRST_SCALE = 1.0 / (1.0 - BETA_FIRST**STEP)
SECOND_SCALE = 1.0 / (1.0 - BETA_SECOND**STEP)
UNITS = FF // H
SOURCES = ((0, 0), (0, 3 * HD // 2), (1, 0), (2, 0))
SECTIONS = ((0, 3, HD), (3 * HD, 1, HD), (4 * HD, 1, UNITS), (4 * HD + UNITS, 1, UNITS))


def dot(left, right, left_dim=1, right_dim=0):
    return lax.dot_general(
        left, right, (((left_dim,), (right_dim,)), ((), ())), preferred_element_type=WIDE
    )


def native_view(values):
    rows, heads, columns = values.shape
    return (
        values.reshape(rows, heads, columns // 128, 128)
        .transpose(0, 2, 1, 3)
        .reshape(rows, columns // 128 * heads, 128)
    )


def from_native(values, heads):
    rows, count, width = values.shape
    return (
        values.reshape(rows, count // heads, heads, width)
        .transpose(0, 2, 1, 3)
        .reshape(rows, heads, count // heads * width)
    )


def tile_pairs(parts, width):
    each = width // 128
    return [
        (part * each + i, part * each + each // 2 + i)
        for part in range(parts)
        for i in range(each // 2)
    ]


def exchange(flag, left, right):
    return jnp.where(flag, right, left), jnp.where(flag, left, right)


def cross(q_flag, p_flag, values):
    a, b = exchange(p_flag, values[0], values[1])
    c, d = exchange(p_flag, values[2], values[3])
    a, c = exchange(q_flag, a, c)
    b, d = exchange(q_flag, b, d)
    return a, b, c, d


def split_kernel(sections, side_ref, *refs):
    weight_refs, out_refs = refs[: len(sections)], refs[len(sections) :]
    q_flag, p_flag = side_ref[0] == 1, side_ref[1] == 1
    lane = 0
    for weight_ref, (_, parts, width) in zip(weight_refs, sections):
        turned = {}
        for left, right in tile_pairs(parts, width):
            for group in (left // 4, right // 4):
                if group not in turned:
                    rows = weight_ref[:, group * 8 : group * 8 + 8, :]
                    turned[group] = jnp.swapaxes(rows, 0, 1)
            values = [
                turned[t // 4][t % 4 * 2 + head] for head in range(2) for t in (left, right)
            ]
            for ref, value in zip(out_refs, cross(q_flag, p_flag, values)):
                ref[:, lane : lane + 128] = value.astype(LOW)
            lane += 128


def split_weights(view, side, sections):
    rows = view.shape[0]
    total = sum(parts * width for _, parts, width in sections)
    block = 32

    def section_spec(offset, size):
        return pl.BlockSpec((block, size // 64, 128), lambda i: (i, offset // size, 0))

    return pl.pallas_call(
        functools.partial(split_kernel, sections),
        out_shape=[jax.ShapeDtypeStruct((rows, total // 2), LOW)] * SHARERS,
        grid=(rows // block,),
        in_specs=[pl.BlockSpec(memory_space=pltpu.SMEM)]
        + [section_spec(offset, parts * width) for offset, parts, width in sections],
        out_specs=[pl.BlockSpec((block, total // 2), lambda i: (i, 0))] * SHARERS,
        compiler_params=pltpu.CompilerParams(vmem_limit_bytes=40 * 2**20),
        cost_estimate=pl.CostEstimate(flops=1, bytes_accessed=1, transcendentals=0),
    )(side, *[view] * len(sections))


def moments_kernel(side_ref, clip_ref, weight_ref, first_ref, second_ref, *rest):
    gradients, (first_out, second_out, update_out, total_ref) = rest[:-4], rest[-4:]
    q_flag, p_flag = side_ref[0] == 1, side_ref[1] == 1
    clip = clip_ref[0]

    @pl.when(pl.program_id(0) == 0)
    def _():
        total_ref[...] = jnp.zeros_like(total_ref)

    update_sq = jnp.zeros((8, 128), WIDE)
    weight_sq = jnp.zeros((8, 128), WIDE)
    for (offset, parts, width), (index, lane) in zip(SECTIONS, SOURCES):
        refs = gradients[SHARERS * index : SHARERS * (index + 1)]
        places = {}
        for tile, (left, right) in enumerate(tile_pairs(parts, width)):
            lanes = slice(lane + tile * 128, lane + tile * 128 + 128)
            values = [ref[:, lanes].astype(WIDE) for ref in refs]
            a, b, c, d = cross(q_flag, p_flag, values)
            places[2 * left], places[2 * right] = a, b
            places[2 * left + 1], places[2 * right + 1] = c, d
            for group in (left // 4, right // 4):
                rows = range(group * 8, group * 8 + 8)
                if any(row not in places for row in rows):
                    continue
                scaled = jnp.swapaxes(jnp.stack([places.pop(r) for r in rows], axis=0), 0, 1) * clip
                here = pl.ds(offset // 64 + group * 8, 8)
                weight = weight_ref[:, here, :]
                first_new = BETA_FIRST * first_ref[:, here, :] + (1.0 - BETA_FIRST) * scaled
                second_new = (
                    BETA_SECOND * second_ref[:, here, :] + (1.0 - BETA_SECOND) * scaled * scaled
                )
                first_out[:, here, :] = first_new
                second_out[:, here, :] = second_new
                update = (
                    first_new * FIRST_SCALE / (jnp.sqrt(second_new * SECOND_SCALE) + ADAM_EPSILON)
                    + WEIGHT_DECAY * weight
                )
                update_out[:, here, :] = update.astype(update_out.dtype)
                update_sq += jnp.sum(update * update, axis=0)
                weight_sq += jnp.sum(weight * weight, axis=0)
    total_ref[0] += update_sq
    total_ref[1] += weight_sq


def moments_step(side, clip, weight, first, second, gradients):
    rows, depth, _ = weight.shape
    block = min(64, rows)
    whole = pl.BlockSpec((block, depth, 128), lambda i: (i, 0, 0))
    shape = jax.ShapeDtypeStruct(weight.shape, WIDE)
    return pl.pallas_call(
        moments_kernel,
        out_shape=[
            shape,
            shape,
            jax.ShapeDtypeStruct(weight.shape, LOW),
            jax.ShapeDtypeStruct((2, 8, 128), WIDE),
        ],
        grid=(rows // block,),
        in_specs=[pl.BlockSpec(memory_space=pltpu.SMEM)] * 2
        + [whole] * 3
        + [pl.BlockSpec((block, g.shape[1]), lambda i: (i, 0)) for g in gradients],
        out_specs=[whole] * 3 + [pl.BlockSpec((2, 8, 128), lambda i: (0, 0, 0))],
        compiler_params=pltpu.CompilerParams(vmem_limit_bytes=48 * 2**20),
        cost_estimate=pl.CostEstimate(
            flops=weight.size * 20, bytes_accessed=weight.size * 24, transcendentals=weight.size
        ),
    )(side, clip, weight, first, second, *gradients)


def embed_kernel(place_ref, picked_ref, expand_ref, entry_ref, table_ref, fold_ref, block_ref, hot_ref, out_ref):
    hot = (dot(picked_ref[...], expand_ref[0]) == entry_ref[...]).astype(LOW)
    hot_ref[0] = hot
    total = 0.0
    for i in (2, 1, 0):
        wide = (dot(table_ref[0, i], fold_ref[...], 1, 1) * block_ref[...]).astype(LOW)
        total = total + dot(hot, wide)
    out_ref[...] = total


def embed_tokens(place, picked, expand, entry, table, fold, block):
    tokens, rows, width = picked.shape[0], entry.shape[1], fold.shape[0]
    return pl.pallas_call(
        embed_kernel,
        out_shape=[
            jax.ShapeDtypeStruct((SHARERS, tokens, rows), LOW),
            jax.ShapeDtypeStruct((tokens, SHARERS * width), WIDE),
        ],
        grid_spec=pltpu.PrefetchScalarGridSpec(
            num_scalar_prefetch=1,
            grid=(SHARERS,),
            in_specs=[
                pl.BlockSpec(picked.shape, lambda j, place: (0, 0)),
                pl.BlockSpec((1, *expand.shape[1:]), lambda j, place: (j, 0, 0)),
                pl.BlockSpec(entry.shape, lambda j, place: (0, 0)),
                pl.BlockSpec((1, *table.shape[1:]), lambda j, place: (j ^ place[0], 0, 0, 0)),
                pl.BlockSpec(fold.shape, lambda j, place: (0, 0)),
                pl.BlockSpec(block.shape, lambda j, place: (0, 0)),
            ],
            out_specs=[
                pl.BlockSpec((1, tokens, rows), lambda j, place: (j, 0, 0)),
                pl.BlockSpec((tokens, width), lambda j, place: (0, j)),
            ],
        ),
        compiler_params=pltpu.CompilerParams(vmem_limit_bytes=40 * 2**20),
        cost_estimate=pl.CostEstimate(flops=1, bytes_accessed=1, transcendentals=0),
    )(place, picked, expand, entry, table, fold, block)


def join_kernel(*refs):
    rows = refs[0].shape[0]
    for k, ref in enumerate(refs[:-1]):
        refs[-1][k * rows : (k + 1) * rows, :] = ref[...]


def join_blocks(parts, turns):
    rows, columns = parts[0].shape
    width = columns // SHARERS
    return pl.pallas_call(
        join_kernel,
        out_shape=jax.ShapeDtypeStruct((len(parts) * rows, columns), parts[0].dtype),
        grid=(SHARERS,),
        in_specs=[pl.BlockSpec((rows, width), lambda j, t=t: (0, j ^ t)) for t in turns],
        out_specs=pl.BlockSpec((len(parts) * rows, width), lambda j: (0, j)),
        cost_estimate=pl.CostEstimate(
            flops=0, bytes_accessed=4 * len(parts) * rows * columns, transcendentals=0
        ),
    )(*parts)


def part_kernel(*refs):
    count = len(refs) // 3
    for left, right, out in zip(refs[:count], refs[count : 2 * count], refs[2 * count :]):
        out[...] = (left[...].astype(WIDE) + right[...].astype(WIDE)).astype(out.dtype)


def part_sums(left, right, turns):
    rows, columns = left.shape[0] // len(turns), left.shape[1]
    width = columns // SHARERS
    specs = [
        pl.BlockSpec((rows, width), lambda j, k=k, t=t: (k, j ^ t)) for k, t in enumerate(turns)
    ]
    return pl.pallas_call(
        part_kernel,
        out_shape=[
            jax.ShapeDtypeStruct((rows, columns), LOW if k else WIDE) for k in range(len(turns))
        ],
        grid=(SHARERS,),
        in_specs=specs + specs,
        out_specs=[pl.BlockSpec((rows, width), lambda j: (0, j))] * len(turns),
        cost_estimate=pl.CostEstimate(
            flops=left.size, bytes_accessed=6 * left.size, transcendentals=0
        ),
    )(*[left] * len(turns), *[right] * len(turns))


def small_kernel(decays, clip_ref, *refs):
    count = len(decays)
    clip = clip_ref[0]
    for i, decay in enumerate(decays):
        weight, gradient, first, second = (ref[...] for ref in refs[4 * i : 4 * i + 4])
        outs = refs[4 * count + 3 * i : 4 * count + 3 * i + 3]
        first_new, second_new, update = moments_of(weight, gradient, first, second, clip, decay)
        outs[0][...] = apply_trust(
            weight,
            update,
            jnp.sum(weight * weight, keepdims=True),
            jnp.sum(update * update, keepdims=True),
        )
        outs[1][...] = first_new
        outs[2][...] = second_new


def small_steps(clip, groups, decays):
    flat = [values for group in groups for values in group]
    return pl.pallas_call(
        functools.partial(small_kernel, decays),
        out_shape=[
            jax.ShapeDtypeStruct(group[0].shape, WIDE) for group in groups for _ in range(3)
        ],
        in_specs=[pl.BlockSpec(memory_space=pltpu.SMEM)]
        + [pl.BlockSpec(memory_space=pltpu.VMEM)] * len(flat),
        out_specs=[pl.BlockSpec(memory_space=pltpu.VMEM)] * (3 * len(groups)),
        compiler_params=pltpu.CompilerParams(vmem_limit_bytes=48 * 2**20),
    )(clip, *flat)


class Grid:
    def __init__(self, rows, heads):
        self.rows, self.heads = rows // SHARERS, heads
        self.each = H // heads
        self.parts = SHARERS // self.each
        self.members = SHARERS * heads
        self.shape = (self.rows, self.each, self.parts, heads)
        self.evens = range(2, self.members, 2)

    def sharer(self):
        return lax.axis_index("q") * self.parts + lax.axis_index("p")

    def pair(self, values, step):
        return lax.ppermute(values, ("q", "p", "h"), [(i, i ^ step) for i in range(self.members)])

    def trade(self, values, step):
        return lax.ppermute(values, ("q", "p"), [(i, i ^ step) for i in range(SHARERS)])

    def turns(self):
        return [0] + [d // self.heads for d in self.evens]

    def spread(self, own):
        parts = [own] + [self.pair(own, d) for d in self.evens]
        half = join_blocks(parts, self.turns())
        return half, self.pair(half, 1)

    def gathered_sum(self, half, other):
        parts = part_sums(half, self.pair(other, 1), self.turns())
        total = parts[0]
        for part, d in zip(parts[1:], self.evens):
            total = total + self.pair(part, d).astype(WIDE)
        return total

    def group_total(self, values):
        step = 1
        while step < self.members:
            values = values + self.pair(values, step)
            step *= 2
        return values

    def every(self, values):
        step = 1
        while step < self.members:
            values = jnp.concatenate([values, self.pair(values, step)], axis=0)
            step *= 2
        step = 1
        while step < self.rows:
            moved = lax.ppermute(values, "a", [(i, i ^ step) for i in range(self.rows)])
            values = jnp.concatenate([values, moved], axis=0)
            step *= 2
        return values

    def facing(self, values):
        return lax.ppermute(values, "a", [(0, 1), (1, 0)])

    def row_list(self, values):
        if self.rows == 2:
            return [values, self.facing(values)]
        every = lax.all_gather(values, "a", axis=0)
        return [every[i] for i in range(self.rows)]

    def row_gather(self, values):
        parts = self.row_list(values)
        if self.rows == 2:
            flag = lax.axis_index("a") == 1
            parts = exchange(flag, *parts)
        return list(parts)

    def row_sum(self, values):
        if self.rows == 2:
            return values.astype(WIDE) + self.facing(values).astype(WIDE)
        return lax.psum(values.astype(WIDE), "a")

    def total(self, values):
        return self.row_sum(self.group_total(values))

    def ordered(self, parts):
        place = self.sharer()
        low, high = place % 2 == 1, place // 2 == 1
        parts = [jnp.where(low, parts[j ^ 1], parts[j]) for j in range(SHARERS)]
        return [jnp.where(high, parts[j ^ 2], parts[j]) for j in range(SHARERS)]

    def absolute(self, values):
        return jnp.concatenate(self.ordered(jnp.split(values, SHARERS, axis=-1)), axis=-1)

    def to_rows(self, values):
        values = self.absolute(values)
        if self.rows != 2:
            return lax.all_to_all(values, "a", split_axis=0, concat_axis=1, tiled=True)
        flag = lax.axis_index("a") == 1
        kept, sent = exchange(flag, *jnp.split(values, 2, axis=0))
        return jnp.concatenate(exchange(flag, kept, self.facing(sent)), axis=1)

    def from_rows(self, values):
        if self.rows != 2:
            return self.absolute(
                lax.all_to_all(values, "a", split_axis=1, concat_axis=0, tiled=True)
            )
        flag = lax.axis_index("a") == 1
        kept, sent = exchange(flag, *jnp.split(values, 2, axis=1))
        moved = jnp.concatenate(exchange(flag, kept, self.facing(sent)), axis=0)
        return self.absolute(moved)

    def renamed(self, values, step):
        block = values.shape[0] // self.members
        span = 1
        while span < self.members // 2:
            if step // 2 & span:
                halves = values.reshape(-1, 2, span * block, values.shape[1])
                values = jnp.stack([halves[:, 1], halves[:, 0]], axis=1).reshape(values.shape)
            span *= 2
        return values

    def columns(self, values):
        found = [values]
        for d in range(1, self.parts):
            got = lax.ppermute(values, "p", [(i, i ^ d) for i in range(self.parts)])
            found.append(self.renamed(got, d * self.heads))
        return jnp.concatenate(found, axis=1)

    def local(self, values, axis):
        size = values.shape[axis] // (self.rows * SHARERS)
        first, place = lax.axis_index("a") * SHARERS, self.sharer()
        return [
            lax.dynamic_slice_in_dim(values, (first + (place ^ j)) * size, size, axis)
            for j in range(SHARERS)
        ]

    def stats(self, values, count):
        center = jnp.mean(values, axis=1)
        spread = jnp.sum(jnp.square(values - center[:, None]), axis=1)
        parts = self.row_list(jnp.stack([center, spread]))
        mean = sum(part[0] for part in parts) / self.rows
        size = count // self.rows
        square = sum(part[1] + size * jnp.square(part[0] - mean) for part in parts)
        return mean[:, None], lax.rsqrt(square / count + EPS_NORM)[:, None]

    def split_plain(self, values, parts, width):
        rows = values.shape[0]
        values = values.astype(LOW).reshape(rows, self.each, parts, self.parts, -1)
        values = values.transpose(1, 3, 0, 2, 4).reshape(SHARERS, rows, -1)
        return [
            lax.dynamic_index_in_dim(values, self.sharer() ^ j, 0, False) for j in range(SHARERS)
        ]

    def merge_plain(self, pieces, parts, width):
        values = jnp.stack(self.ordered(pieces))
        rows = values.shape[1]
        values = values.reshape(self.each, self.parts, rows, parts, -1)
        return values.transpose(2, 0, 3, 1, 4).reshape(rows, self.each, parts * width)


def tied(*values):
    return lax.optimization_barrier(values)


def split_three(values):
    high = lax.reduce_precision(values, 8, 7)
    rest = values - high
    middle = lax.reduce_precision(rest, 8, 7)
    return high.astype(LOW), middle.astype(LOW), (rest - middle).astype(LOW)


def per_device(grid, *arguments):
    (
        cell_ids,
        cell_mask,
        labels,
        abd_weights,
        abd_first,
        abd_second,
        abd_gains,
        abd_gains_first,
        abd_gains_second,
        aba_weights,
        aba_first,
        aba_second,
        aba_gains,
        aba_gains_first,
        aba_gains_second,
        embed_table,
        embed_first,
        embed_second,
        output_table,
        output_first,
        output_second,
    ) = arguments
    h = lax.axis_index("h")
    attr_count, entries, embed_width = embed_table.shape
    classes = output_table.shape[2]
    model_width = attr_count * embed_width
    own_tokens = cell_ids.shape[0] // grid.heads
    first_device = ((lax.axis_index("a") == 0) & (grid.sharer() == 0)).astype(WIDE)
    native = grid.each == 2
    side = jnp.stack([lax.axis_index("q"), lax.axis_index("p")]).astype(jnp.int32)

    def own_rows(values):
        return lax.dynamic_slice_in_dim(values, h * own_tokens, own_tokens, 0)

    attrs_held = labels.shape[1]
    mask_held = lax.dynamic_slice_in_dim(cell_mask, h * attrs_held, attrs_held, 1)
    codes = jnp.where(mask_held == 1, labels, -1).reshape(own_tokens, attr_count)
    picked = own_rows(jnp.where(cell_mask == 1, classes, cell_ids))
    gathered = grid.every(jnp.concatenate([picked, codes], axis=1).astype(LOW))
    tokens = gathered.shape[0]
    picked_all = gathered[:, :attr_count]
    codes_all = gathered[:, attr_count:].reshape(-1, grid.heads, own_tokens, attr_count)
    device = (lax.axis_index("a") * SHARERS + grid.sharer()) * grid.heads + h

    def by_head(parts):
        for bit in range((grid.heads - 1).bit_length()):
            flag = (h >> bit) % 2 == 1
            parts = [
                jnp.where(flag, parts[d ^ (1 << bit)], parts[d]) for d in range(grid.heads)
            ]
        return parts

    def pieces_of(sections):
        if native:
            return split_weights(weight_view, side, sections)
        found = []
        for offset, parts, size in sections:
            columns = abd_weights[:, :, offset : offset + parts * size]
            found.append(grid.split_plain(columns, parts, size))
        return [jnp.concatenate(piece, axis=1) for piece in zip(*found)]

    def traded(values):
        return [values[0]] + [grid.trade(values[j], j) for j in (1, 2, 3)]

    weight_view = native_view(abd_weights) if native else None
    qkv_pieces, picked_all, side, table = tied(
        pieces_of(SECTIONS[:1]), picked_all, side, embed_table
    )
    qkv_w = traded(qkv_pieces)
    picked_all, other_pieces = tied(picked_all, pieces_of(SECTIONS[1:3]))

    held = tokens // grid.members
    place = jnp.arange(tokens, dtype=jnp.int32)
    owner, inside = place // held, place % held
    owner = 2 * (owner % (grid.members // 2)) + owner // (grid.members // 2)
    owner = owner ^ (grid.sharer() * grid.heads + h)
    source = (inside // own_tokens * grid.members + owner) ^ device
    row_of = source * own_tokens + inside % own_tokens
    picked = dot((row_of[:, None] == place[None, :]).astype(LOW), picked_all).astype(LOW)
    picked = jnp.concatenate(grid.local(picked, 1), axis=1)
    local_attrs = picked.shape[1]
    block_attrs = local_attrs // SHARERS
    table_rows = jnp.arange(block_attrs * entries, dtype=jnp.int32)
    row_attr, row_entry = table_rows // entries, (table_rows % entries).astype(WIDE)
    block_columns = jnp.arange(block_attrs * embed_width, dtype=jnp.int32)
    own_block = row_attr[:, None] == block_columns // embed_width
    fold = (
        block_columns[:, None] % embed_width == jnp.arange(embed_width, dtype=jnp.int32)
    ).astype(LOW)
    table = lax.dynamic_slice_in_dim(table, lax.axis_index("a") * local_attrs, local_attrs, 0)
    table = table.reshape(SHARERS, row_attr.size, embed_width)
    places = jnp.arange(local_attrs, dtype=jnp.int32)
    expand = places[None, :, None] == (
        jnp.arange(SHARERS, dtype=jnp.int32)[:, None, None] * block_attrs + row_attr[None, None, :]
    )
    hots, embedded = embed_tokens(
        grid.sharer().astype(jnp.int32)[None],
        picked,
        expand.astype(LOW),
        row_entry[None, :],
        jnp.stack(split_three(table), axis=1),
        fold,
        own_block.astype(WIDE),
    )
    embedded, qkv_w, other_pieces, side = tied(embedded, qkv_w, other_pieces, side)
    qkv_w = jnp.concatenate(qkv_w, axis=0)
    others = traded(other_pieces)

    kinds = jnp.arange(classes, dtype=jnp.int32).astype(WIDE)
    mask_own = own_rows(cell_mask).astype(WIDE)
    counts, own_codes = [], []
    for d in range(grid.heads):
        found = (codes_all[:, d].reshape(-1, attr_count)[:, :, None].astype(WIDE) == kinds)
        found = jnp.sum(found.astype(WIDE), axis=0)
        counts.append(jnp.sum(found.reshape(-1, attrs_held, classes), axis=0))
        own_codes.append(own_rows(codes_all[0, d].reshape(-1, attrs_held)))
    counts = jnp.concatenate(by_head(counts), axis=0)
    own_codes = jnp.concatenate(by_head(own_codes), axis=1)
    label_hot = (own_codes.astype(WIDE)[:, :, None] == kinds).astype(WIDE)
    class_weight = lax.rsqrt(1.0 + counts)
    weight_total = jnp.sum(counts * class_weight)
    tables_low = output_table.astype(LOW)[None]
    step = 1
    while step < grid.heads:
        tables_low = jnp.concatenate([tables_low, grid.pair(tables_low, step)], axis=0)
        step *= 2
    output_low = jnp.concatenate(by_head(list(tables_low)), axis=0)

    out_size, up_size = HD * grid.each // SHARERS, UNITS * grid.each // SHARERS
    gains = jnp.concatenate(grid.local(abd_gains, 1), axis=1)
    mean_one, scale_one = grid.stats(embedded, model_width)
    hat_one = (embedded - mean_one) * scale_one
    normed = (hat_one * gains[0]).astype(LOW)
    triple = grid.row_sum(dot(normed, qkv_w).astype(LOW)).astype(LOW)
    triple, others, class_weight, weight_total, label_hot, output_low, down_pieces = tied(
        triple, others, class_weight, weight_total, label_hot, output_low, pieces_of(SECTIONS[3:])
    )
    part = HD // grid.parts
    query_own, key_own, value_own = (triple[:, i * part : (i + 1) * part] for i in range(3))
    queries, key_rows = grid.columns(query_own), grid.columns(key_own)
    value_rows = grid.columns(value_own)
    factor = HD ** (-0.5)
    scores = dot(queries, key_rows, 1, 1) * factor
    shifted = jnp.exp(scores - jnp.max(scores, axis=1, keepdims=True))
    probs = shifted / jnp.sum(shifted, axis=1, keepdims=True)
    probs_low = probs.astype(LOW)
    attended = dot(probs_low, value_own).astype(LOW)
    out_w = jnp.concatenate([piece[:, :out_size] for piece in others], axis=0)
    up_w = jnp.concatenate([piece[:, out_size:] for piece in others], axis=0)
    attended = jnp.split(attended, 2, axis=0)
    branch = [dot(a, out_w, 1, 1).astype(LOW) for a in attended]
    middle = embedded[:held] + grid.gathered_sum(*branch)
    mean_two, scale_two = grid.stats(middle, model_width)
    hat_two = (middle - mean_two) * scale_two
    second = grid.spread((hat_two * gains[1]).astype(LOW))
    before, down_pieces = tied([dot(a, up_w).astype(LOW) for a in second], down_pieces)
    before = [grid.row_sum(b) for b in before]
    before[0], down_w, up_turned, qkv_turned = tied(
        before[0], traded(down_pieces), up_w.T, qkv_w.T
    )
    down_w = jnp.concatenate(down_w, axis=0)
    hidden = [gelu_apply(before[0]).astype(LOW)]
    down = [dot(hidden[0], down_w, 1, 1).astype(LOW)]
    before[1], hidden[0], down[0] = tied(before[1], hidden[0], down[0])
    hidden.append(gelu_apply(before[1]).astype(LOW))
    down.append(dot(hidden[1], down_w, 1, 1).astype(LOW))
    after = middle + grid.gathered_sum(*down)

    aba_low = aba_weights.astype(LOW)
    final, aba_stored = aba_forward(grid.to_rows(after), aba_low, aba_gains)
    final_low = final.reshape(own_tokens, attr_count, embed_width).astype(LOW)
    logits = jnp.einsum("tfe,fec->tfc", final_low, output_low, preferred_element_type=WIDE)
    highest = jnp.max(logits, axis=-1, keepdims=True)
    exped = jnp.exp(logits - highest)
    totals = jnp.sum(exped, axis=-1, keepdims=True)
    log_total = (highest + jnp.log(totals))[:, :, 0]
    cell_weight = mask_own * jnp.sum(label_hot * class_weight[None], axis=-1)
    loss_local = jnp.sum(cell_weight * (log_total - jnp.sum(label_hot * logits, axis=-1)))
    logit_grad = ((cell_weight / weight_total)[:, :, None] * (exped / totals - label_hot)).astype(
        LOW
    )
    final_grad = jnp.einsum("tfc,fec->tfe", logit_grad, output_low, preferred_element_type=WIDE)
    output_part = jnp.einsum("tfe,tfc->fce", final_low, logit_grad, preferred_element_type=WIDE)
    rows_grad, aba_part, aba_gains_part = aba_backward(
        final_grad.reshape(own_tokens, model_width), aba_stored, aba_low, aba_gains
    )

    width = normed.shape[1] // SHARERS
    gradient_sq = []

    def row_gradients(acts, uppers):
        found = []
        for j in range(SHARERS):
            cut = slice(j * width, (j + 1) * width)
            piece = sum(dot(a[:, cut], u, 0, 0) for a, u in zip(acts, uppers)).astype(LOW)
            gradient_sq.append(jnp.sum(jnp.square(piece.astype(WIDE))))
            found.append(piece)
        return found

    upstream = grid.from_rows(rows_grad.astype(LOW))
    down_grad = grid.spread(upstream)
    hidden_grad = tied(*[dot(a, down_w).astype(LOW) for a in down_grad])
    hidden_grad = [grid.row_sum(g) for g in hidden_grad]
    down_gradient = traded(row_gradients(down_grad, hidden))

    hidden_grad[0], down_gradient, output_part, aba_part, aba_gains_part = tied(
        hidden_grad[0], down_gradient, output_part, aba_part, aba_gains_part
    )

    small = jnp.concatenate([aba_part.reshape(-1), aba_gains_part.reshape(-1)])
    blocks = output_part.reshape(grid.heads, -1)
    bits = (grid.heads - 1).bit_length()
    for bit in range(bits):
        flag = (h >> bit) % 2 == 1
        halves = blocks.reshape(-1, 2, blocks.shape[1])
        kept, sent = exchange(flag, halves[:, 0], halves[:, 1])
        got = grid.pair(jnp.concatenate([sent.reshape(-1), small]).reshape(-1, 128), 1 << bit)
        got = got.reshape(-1)
        blocks = kept + got[: sent.size].reshape(kept.shape)
        small = small + got[sent.size :]
    packed = jnp.concatenate([blocks.reshape(-1), small]).reshape(-1, 128)
    for step in (grid.heads, 2 * grid.heads):
        packed = packed + grid.pair(packed, step)
    packed = grid.row_sum(packed).reshape(-1)
    output_grad = packed[: blocks.size].reshape(-1, classes, embed_width)
    aba_grad = packed[blocks.size : blocks.size + aba_weights.size].reshape(aba_weights.shape)
    aba_gains_grad = packed[blocks.size + aba_weights.size :].reshape(aba_gains.shape)


    before_grad = [gelu_back(before[0], hidden_grad[0]).astype(LOW)]
    second_grad = [dot(before_grad[0], up_turned).astype(LOW)]
    hidden_grad[1], before_grad[0], second_grad[0] = tied(
        hidden_grad[1], before_grad[0], second_grad[0]
    )
    before_grad.append(gelu_back(before[1], hidden_grad[1]).astype(LOW))
    second_grad.append(dot(before_grad[1], up_turned).astype(LOW))
    second_grad = grid.gathered_sum(*second_grad)
    gained = second_grad * gains[1]
    sums = jnp.stack([jnp.sum(gained, axis=1), jnp.sum(gained * hat_two, axis=1)])
    sums = sum(grid.row_list(sums)) / model_width
    middle_grad = upstream.astype(WIDE) + scale_two * (
        gained - sums[0][:, None] - hat_two * sums[1][:, None]
    )
    middle_grad, up_gradient, output_grad, aba_grad, aba_gains_grad = tied(
        middle_grad, row_gradients(second, before_grad), output_grad, aba_grad, aba_gains_grad
    )
    up_gradient = traded(up_gradient)
    gain_two = jnp.sum(second_grad * hat_two, axis=0)
    branch_grad = grid.spread(middle_grad.astype(LOW))
    attended_grad = jnp.concatenate([dot(a, out_w).astype(LOW) for a in branch_grad], axis=0)
    attended_grad, attended, table_acts = tied(attended_grad, attended, middle_grad.astype(LOW))
    attended_grad, up_gradient = tied(grid.row_sum(attended_grad).astype(LOW), up_gradient)
    out_gradient = row_gradients(branch_grad, attended)
    prob_grad = dot(grid.columns(attended_grad), value_rows, 1, 1)
    score_grad = probs * (prob_grad - jnp.sum(probs * prob_grad, axis=1, keepdims=True))
    score_grad = score_grad.astype(LOW)
    query_grad = dot(score_grad, key_own) * factor
    key_grad = dot(score_grad, query_own, 0, 0) * factor
    value_grad = dot(probs_low, attended_grad, 0, 0)
    triple_grad = jnp.concatenate([query_grad, key_grad, value_grad], axis=1).astype(LOW)
    table_part = [
        dot(hot[:held], block, 0, 0)
        for hot, block in zip(hots, jnp.split(table_acts, SHARERS, axis=1))
    ]
    triple_grad, table_part, out_gradient = tied(triple_grad, table_part, out_gradient)
    qkv_gradient = row_gradients([normed], [triple_grad])
    qkv_gradient = [jnp.concatenate(pair, axis=1) for pair in zip(qkv_gradient, out_gradient)]
    triple_grad, qkv_gradient = tied(triple_grad, qkv_gradient)

    normed_grad = dot(triple_grad, qkv_turned)
    gained = normed_grad * gains[0]
    sums = jnp.stack([jnp.sum(gained, axis=1), jnp.sum(gained * hat_one, axis=1)])
    sums = sum(grid.row_list(sums)) / model_width
    gain_one = jnp.sum(normed_grad * hat_one, axis=0)
    spread_grad = scale_one * (gained - sums[0][:, None] - hat_one * sums[1][:, None])
    records = []
    for j, block in enumerate(jnp.split(spread_grad.astype(LOW), SHARERS, axis=1)):
        grad = table_part[j] + dot(hots[j], block, 0, 0)
        grad = jnp.where(own_block, grad, 0.0)
        grad = jnp.dot(grad, fold.astype(WIDE), precision=lax.Precision.HIGHEST)
        cut = slice(j * width, (j + 1) * width)
        records.append(jnp.concatenate([grad.reshape(-1), gain_one[cut], gain_two[cut]]))
    table_size = block_attrs * entries * embed_width
    packed = jnp.stack(grid.ordered(records)).reshape(-1, 128)
    output_sq = first_device * jnp.sum(output_grad * output_grad)
    scalars = jnp.stack([sum(gradient_sq), output_sq, loss_local])
    lane = jnp.arange(8 * 128, dtype=jnp.int32).reshape(8, 128)
    scalars = sum(jnp.where(lane == i, scalars[i], 0.0) for i in range(3))
    packed, qkv_gradient = tied(packed, traded(qkv_gradient))
    gradients = qkv_gradient + up_gradient + down_gradient
    packed = jnp.stack(
        grid.row_gather(grid.group_total(jnp.concatenate([scalars, packed], axis=0)))
    )
    summed = jnp.sum(packed[:, 0, :3], axis=0)
    packed = packed[:, 8:].reshape(grid.rows * SHARERS, -1)
    embed_grad = packed[:, :table_size].reshape(embed_table.shape).transpose(1, 0, 2)
    abd_gains_grad = packed[:, table_size:].reshape(-1, 2, width).transpose(1, 0, 2)
    abd_gains_grad = abd_gains_grad.reshape(2, model_width)

    output_table, output_first, output_second = (
        values.transpose(0, 2, 1) for values in (output_table, output_first, output_second)
    )
    embed_table, embed_first, embed_second = (
        values.transpose(1, 0, 2) for values in (embed_table, embed_first, embed_second)
    )
    replicated_sq = (
        jnp.sum(abd_gains_grad * abd_gains_grad)
        + jnp.sum(aba_grad * aba_grad)
        + jnp.sum(aba_gains_grad * aba_gains_grad)
        + jnp.sum(embed_grad * embed_grad)
    )
    grad_norm = jnp.sqrt(summed[0] + summed[1] + replicated_sq)
    loss_sum = summed[2]
    clip_factor = jnp.minimum(1.0, CLIP_LIMIT / (grad_norm + 1e-06))
    if native:
        first_view, second_view, abd_update, squares = moments_step(
            side,
            clip_factor[None],
            weight_view,
            native_view(abd_first),
            native_view(abd_second),
            gradients,
        )
        abd_first_new = from_native(first_view, grid.each)
        abd_second_new = from_native(second_view, grid.each)
        abd_update_sq, abd_weight_sq = jnp.sum(squares[0]), jnp.sum(squares[1])
    else:
        first_g, up_g, down_g = (gradients[SHARERS * i : SHARERS * (i + 1)] for i in range(3))
        split_g = (
            [g[:, : 3 * out_size] for g in first_g],
            [g[:, 3 * out_size :] for g in first_g],
            up_g,
            down_g,
        )
        merged = [
            grid.merge_plain(pieces, parts, size)
            for pieces, (_, parts, size) in zip(split_g, SECTIONS)
        ]
        abd_grad = jnp.concatenate(merged, axis=2).astype(WIDE)
        abd_first_new, abd_second_new, abd_update = moments_of(
            abd_weights, abd_grad, abd_first, abd_second, clip_factor, WEIGHT_DECAY
        )
        abd_update_sq, abd_weight_sq = (
            jnp.sum(abd_update * abd_update),
            jnp.sum(abd_weights * abd_weights),
        )
    output_first_new, output_second_new, output_update = moments_of(
        output_table, output_grad, output_first, output_second, clip_factor, WEIGHT_DECAY
    )
    trust_sums = grid.total(
        jnp.stack(
            [
                abd_update_sq,
                first_device * jnp.sum(output_update * output_update),
                abd_weight_sq,
                first_device * jnp.sum(output_table * output_table),
            ]
        )
    )
    if native:
        abd_new = from_native(
            apply_trust(weight_view, abd_update.astype(WIDE), trust_sums[2], trust_sums[0]),
            grid.each,
        )
    else:
        abd_new = apply_trust(abd_weights, abd_update, trust_sums[2], trust_sums[0])
    output_new = apply_trust(output_table, output_update, trust_sums[3], trust_sums[1])
    small = small_steps(
        clip_factor[None],
        (
            (abd_gains, abd_gains_grad, abd_gains_first, abd_gains_second),
            (aba_weights, aba_grad, aba_first, aba_second),
            (aba_gains, aba_gains_grad, aba_gains_first, aba_gains_second),
            (embed_table, embed_grad, embed_first, embed_second),
        ),
        (0.0, WEIGHT_DECAY, 0.0, WEIGHT_DECAY),
    )
    return (
        loss_sum,
        weight_total,
        grad_norm,
        abd_new,
        abd_first_new,
        abd_second_new,
        *small[:9],
        *[values.transpose(1, 0, 2) for values in small[9:]],
        *[values.transpose(0, 2, 1) for values in (output_new, output_first_new, output_second_new)],
    )


def solution(mesh):
    grid = Grid(mesh.shape["dp"], mesh.shape["head"])
    devices = Mesh(mesh.devices.reshape(grid.shape), ("a", "q", "p", "h"))
    rows = ("a", "q", "p")
    tokens, table = P(rows, None), P("h", None, None)
    weight = P(rows, "h", None)
    in_specs = (tokens, tokens, P(rows, "h"), weight, weight, weight) + (P(),) * 12 + (table,) * 3
    out_specs = (P(),) * 3 + (weight,) * 3 + (P(),) * 12 + (table,) * 3
    return jax.shard_map(
        functools.partial(per_device, grid),
        mesh=devices,
        in_specs=in_specs,
        out_specs=out_specs,
        check_vma=False,
    )
```

```python
import functools

import jax
import jax.experimental.pallas as pl
import jax.experimental.pallas.tpu as pltpu
import jax.numpy as jnp
from jax import lax
from jax.sharding import Mesh
from jax.sharding import PartitionSpec as P

H = 8
AH = 8
STEP = 10
HD = 512
FF = 16384


EPS_NORM = 1e-05
CLIP_LIMIT = 0.01
LEARN_RATE = 0.3
BETA_FIRST = 0.9
BETA_SECOND = 0.999
ADAM_EPSILON = 1e-08
WEIGHT_DECAY = 0.01


def layer_norm(values, gain_row):
    center = jnp.mean(values, axis=-1, keepdims=True)
    centred = values - center
    spread = jnp.mean(centred * centred, axis=-1, keepdims=True)
    return centred * lax.rsqrt(spread + EPS_NORM) * gain_row


def gelu_apply(values):
    return 0.5 * values * (1.0 + lax.erf(values * 0.7071067811865476))


def norm_back(values, gain_row, upstream):
    unused_value, pull_back = jax.vjp(layer_norm, values, gain_row)
    return pull_back(upstream)


def gelu_back(values, upstream):
    unused_value, pull_back = jax.vjp(gelu_apply, values)
    return pull_back(upstream)[0]


def attend_keys(queries, key_rows, value_rows, factor):
    scores = (
        jnp.einsum("...qd,...kd->...qk", queries, key_rows, preferred_element_type=jnp.float32)
        * factor
    )
    highest = jnp.max(scores, axis=-1, keepdims=True)
    weights = jnp.exp(scores - highest)
    totals = jnp.sum(weights, axis=-1, keepdims=True)
    result = jnp.einsum(
        "...qk,...kd->...qd",
        (weights / totals).astype(jnp.bfloat16),
        value_rows,
        preferred_element_type=jnp.float32,
    )
    return (result, highest + jnp.log(totals))


def attend_back(queries, key_rows, value_rows, log_total, result_grad, factor):
    scores = (
        jnp.einsum("...qd,...kd->...qk", queries, key_rows, preferred_element_type=jnp.float32)
        * factor
    )
    softmax_probs = jnp.exp(scores - log_total)
    prob_grad = jnp.einsum(
        "...qd,...kd->...qk", result_grad, value_rows, preferred_element_type=jnp.float32
    )
    score_grad = softmax_probs * (
        prob_grad - jnp.sum(softmax_probs * prob_grad, axis=-1, keepdims=True)
    )
    score_grad = score_grad.astype(jnp.bfloat16)
    query_grad = (
        jnp.einsum("...qk,...kd->...qd", score_grad, key_rows, preferred_element_type=jnp.float32)
        * factor
    )
    key_grad = (
        jnp.einsum("...qk,...qd->...kd", score_grad, queries, preferred_element_type=jnp.float32)
        * factor
    )
    value_grad = jnp.einsum(
        "...qk,...qd->...kd",
        softmax_probs.astype(jnp.bfloat16),
        result_grad,
        preferred_element_type=jnp.float32,
    )
    return (query_grad, key_grad, value_grad)


def aba_forward(row_block, weights, gain_rows):
    embed_width = weights.shape[0]
    row_count = row_block.shape[0]
    attr_count = row_block.shape[1] // embed_width
    size_each = embed_width // AH
    inputs = row_block.reshape(row_count, attr_count, embed_width)
    normed = layer_norm(inputs, gain_rows[0]).astype(jnp.bfloat16)
    projection = weights[:, : 3 * embed_width].reshape(embed_width, 3, AH, size_each)
    triple = jnp.einsum(
        "rfe,eshd->srhfd", normed, projection, preferred_element_type=jnp.float32
    ).astype(jnp.bfloat16)
    attended, log_total = attend_keys(triple[0], triple[1], triple[2], size_each ** (-0.5))
    attended = attended.astype(jnp.bfloat16)
    out_proj = weights[:, 3 * embed_width : 4 * embed_width].reshape(embed_width, AH, size_each)
    middle = inputs + jnp.einsum(
        "rhfd,ohd->rfo", attended, out_proj, preferred_element_type=jnp.float32
    )
    second = layer_norm(middle, gain_rows[1]).astype(jnp.bfloat16)
    before = jnp.einsum(
        "rfe,eu->rfu",
        second,
        weights[:, 4 * embed_width : 8 * embed_width],
        preferred_element_type=jnp.float32,
    )
    hidden = gelu_apply(before).astype(jnp.bfloat16)
    after = middle + jnp.einsum(
        "rfu,ou->rfo", hidden, weights[:, 8 * embed_width :], preferred_element_type=jnp.float32
    )
    return (
        after.reshape(row_count, attr_count * embed_width),
        (inputs, normed, triple, log_total, attended, middle, second, before, hidden),
    )


def aba_backward(upstream, stored, weights, gain_rows):
    inputs, normed, triple, log_total, attended, middle, second, before, hidden = stored
    row_count, attr_count, embed_width = inputs.shape
    size_each = embed_width // AH
    upstream = upstream.reshape(row_count, attr_count, embed_width)
    down_grad = upstream.astype(jnp.bfloat16)
    hidden_grad = jnp.einsum(
        "rfo,ou->rfu", down_grad, weights[:, 8 * embed_width :], preferred_element_type=jnp.float32
    )
    before_grad = gelu_back(before, hidden_grad).astype(jnp.bfloat16)
    second_grad = jnp.einsum(
        "rfu,eu->rfe",
        before_grad,
        weights[:, 4 * embed_width : 8 * embed_width],
        preferred_element_type=jnp.float32,
    )
    middle_part, gain_two = norm_back(middle, gain_rows[1], second_grad)
    middle_grad = upstream + middle_part
    branch_grad = middle_grad.astype(jnp.bfloat16)
    out_proj = weights[:, 3 * embed_width : 4 * embed_width].reshape(embed_width, AH, size_each)
    attended_grad = jnp.einsum(
        "rfo,ohd->rhfd", branch_grad, out_proj, preferred_element_type=jnp.float32
    ).astype(jnp.bfloat16)
    query_grad, key_grad, value_grad = attend_back(
        triple[0], triple[1], triple[2], log_total, attended_grad, size_each ** (-0.5)
    )
    triple_grad = jnp.stack([query_grad, key_grad, value_grad]).astype(jnp.bfloat16)
    projection = weights[:, : 3 * embed_width].reshape(embed_width, 3, AH, size_each)
    normed_grad = jnp.einsum(
        "srhfd,eshd->rfe", triple_grad, projection, preferred_element_type=jnp.float32
    )
    input_part, gain_one = norm_back(inputs, gain_rows[0], normed_grad)
    input_grad = middle_grad + input_part
    weight_grad = jnp.concatenate(
        [
            jnp.einsum(
                "rfe,srhfd->eshd", normed, triple_grad, preferred_element_type=jnp.float32
            ).reshape(embed_width, 3 * embed_width),
            jnp.einsum(
                "rfo,rhfd->ohd", branch_grad, attended, preferred_element_type=jnp.float32
            ).reshape(embed_width, embed_width),
            jnp.einsum("rfe,rfu->eu", second, before_grad, preferred_element_type=jnp.float32),
            jnp.einsum("rfo,rfu->ou", down_grad, hidden, preferred_element_type=jnp.float32),
        ],
        axis=1,
    )
    return (
        input_grad.reshape(row_count, attr_count * embed_width),
        weight_grad,
        jnp.stack([gain_one, gain_two]),
    )


def moments_of(weight, gradient, first, second, clip_factor, decay):
    scaled = gradient * clip_factor
    first_new = BETA_FIRST * first + (1.0 - BETA_FIRST) * scaled
    second_new = BETA_SECOND * second + (1.0 - BETA_SECOND) * scaled * scaled
    update = (
        first_new
        / (1.0 - BETA_FIRST**STEP)
        / (jnp.sqrt(second_new / (1.0 - BETA_SECOND**STEP)) + ADAM_EPSILON)
        + decay * weight
    )
    return (first_new, second_new, update)


def apply_trust(weight, update, weight_sq, update_sq):
    trust_ratio = jnp.sqrt(weight_sq) / (jnp.sqrt(update_sq) + 1e-06)
    return weight - LEARN_RATE * trust_ratio * update


def local_step(weight, gradient, first, second, clip_factor, decay):
    first_new, second_new, update = moments_of(weight, gradient, first, second, clip_factor, decay)
    return (
        apply_trust(weight, update, jnp.sum(weight * weight), jnp.sum(update * update)),
        first_new,
        second_new,
    )


LOW = jnp.bfloat16
WIDE = jnp.float32
SHARERS = 4
FIRST_SCALE = 1.0 / (1.0 - BETA_FIRST**STEP)
SECOND_SCALE = 1.0 / (1.0 - BETA_SECOND**STEP)
UNITS = FF // H
SOURCES = ((0, 0), (0, 3 * HD // 2), (1, 0), (2, 0))
SECTIONS = ((0, 3, HD), (3 * HD, 1, HD), (4 * HD, 1, UNITS), (4 * HD + UNITS, 1, UNITS))


def dot(left, right, left_dim=1, right_dim=0):
    return lax.dot_general(
        left, right, (((left_dim,), (right_dim,)), ((), ())), preferred_element_type=WIDE
    )


def native_view(values):
    rows, heads, columns = values.shape
    return (
        values.reshape(rows, heads, columns // 128, 128)
        .transpose(0, 2, 1, 3)
        .reshape(rows, columns // 128 * heads, 128)
    )


def from_native(values, heads):
    rows, count, width = values.shape
    return (
        values.reshape(rows, count // heads, heads, width)
        .transpose(0, 2, 1, 3)
        .reshape(rows, heads, count // heads * width)
    )


def tile_pairs(parts, width):
    each = width // 128
    return [
        (part * each + i, part * each + each // 2 + i)
        for part in range(parts)
        for i in range(each // 2)
    ]


def exchange(flag, left, right):
    return jnp.where(flag, right, left), jnp.where(flag, left, right)


def cross(q_flag, p_flag, values):
    a, b = exchange(p_flag, values[0], values[1])
    c, d = exchange(p_flag, values[2], values[3])
    a, c = exchange(q_flag, a, c)
    b, d = exchange(q_flag, b, d)
    return a, b, c, d


def split_kernel(sections, side_ref, *refs):
    weight_refs, out_refs = refs[: len(sections)], refs[len(sections) :]
    q_flag, p_flag = side_ref[0] == 1, side_ref[1] == 1
    lane = 0
    for weight_ref, (_, parts, width) in zip(weight_refs, sections):
        turned = {}
        for left, right in tile_pairs(parts, width):
            for group in (left // 4, right // 4):
                if group not in turned:
                    rows = weight_ref[:, group * 8 : group * 8 + 8, :]
                    turned[group] = jnp.swapaxes(rows, 0, 1)
            values = [
                turned[t // 4][t % 4 * 2 + head] for head in range(2) for t in (left, right)
            ]
            for ref, value in zip(out_refs, cross(q_flag, p_flag, values)):
                ref[:, lane : lane + 128] = value.astype(LOW)
            lane += 128


def split_weights(view, side, sections):
    rows = view.shape[0]
    total = sum(parts * width for _, parts, width in sections)
    block = 32

    def section_spec(offset, size):
        return pl.BlockSpec((block, size // 64, 128), lambda i: (i, offset // size, 0))

    return pl.pallas_call(
        functools.partial(split_kernel, sections),
        out_shape=[jax.ShapeDtypeStruct((rows, total // 2), LOW)] * SHARERS,
        grid=(rows // block,),
        in_specs=[pl.BlockSpec(memory_space=pltpu.SMEM)]
        + [section_spec(offset, parts * width) for offset, parts, width in sections],
        out_specs=[pl.BlockSpec((block, total // 2), lambda i: (i, 0))] * SHARERS,
        compiler_params=pltpu.CompilerParams(vmem_limit_bytes=40 * 2**20),
        cost_estimate=pl.CostEstimate(flops=1, bytes_accessed=1, transcendentals=0),
    )(side, *[view] * len(sections))


def moments_kernel(side_ref, clip_ref, weight_ref, first_ref, second_ref, *rest):
    gradients, (first_out, second_out, update_out, total_ref) = rest[:-4], rest[-4:]
    q_flag, p_flag = side_ref[0] == 1, side_ref[1] == 1
    clip = clip_ref[0]

    @pl.when(pl.program_id(0) == 0)
    def _():
        total_ref[...] = jnp.zeros_like(total_ref)

    update_sq = jnp.zeros((8, 128), WIDE)
    weight_sq = jnp.zeros((8, 128), WIDE)
    for (offset, parts, width), (index, lane) in zip(SECTIONS, SOURCES):
        refs = gradients[SHARERS * index : SHARERS * (index + 1)]
        places = {}
        for tile, (left, right) in enumerate(tile_pairs(parts, width)):
            lanes = slice(lane + tile * 128, lane + tile * 128 + 128)
            values = [ref[:, lanes].astype(WIDE) for ref in refs]
            a, b, c, d = cross(q_flag, p_flag, values)
            places[2 * left], places[2 * right] = a, b
            places[2 * left + 1], places[2 * right + 1] = c, d
            for group in (left // 4, right // 4):
                rows = range(group * 8, group * 8 + 8)
                if any(row not in places for row in rows):
                    continue
                scaled = jnp.swapaxes(jnp.stack([places.pop(r) for r in rows], axis=0), 0, 1) * clip
                here = pl.ds(offset // 64 + group * 8, 8)
                weight = weight_ref[:, here, :]
                first_new = BETA_FIRST * first_ref[:, here, :] + (1.0 - BETA_FIRST) * scaled
                second_new = (
                    BETA_SECOND * second_ref[:, here, :] + (1.0 - BETA_SECOND) * scaled * scaled
                )
                first_out[:, here, :] = first_new
                second_out[:, here, :] = second_new
                update = (
                    first_new * FIRST_SCALE / (jnp.sqrt(second_new * SECOND_SCALE) + ADAM_EPSILON)
                    + WEIGHT_DECAY * weight
                )
                update_out[:, here, :] = update.astype(update_out.dtype)
                update_sq += jnp.sum(update * update, axis=0)
                weight_sq += jnp.sum(weight * weight, axis=0)
    total_ref[0] += update_sq
    total_ref[1] += weight_sq


def moments_step(side, clip, weight, first, second, gradients):
    rows, depth, _ = weight.shape
    block = min(64, rows)
    whole = pl.BlockSpec((block, depth, 128), lambda i: (i, 0, 0))
    shape = jax.ShapeDtypeStruct(weight.shape, WIDE)
    return pl.pallas_call(
        moments_kernel,
        out_shape=[
            shape,
            shape,
            jax.ShapeDtypeStruct(weight.shape, LOW),
            jax.ShapeDtypeStruct((2, 8, 128), WIDE),
        ],
        grid=(rows // block,),
        in_specs=[pl.BlockSpec(memory_space=pltpu.SMEM)] * 2
        + [whole] * 3
        + [pl.BlockSpec((block, g.shape[1]), lambda i: (i, 0)) for g in gradients],
        out_specs=[whole] * 3 + [pl.BlockSpec((2, 8, 128), lambda i: (0, 0, 0))],
        compiler_params=pltpu.CompilerParams(vmem_limit_bytes=48 * 2**20),
        cost_estimate=pl.CostEstimate(
            flops=weight.size * 20, bytes_accessed=weight.size * 24, transcendentals=weight.size
        ),
    )(side, clip, weight, first, second, *gradients)


def embed_kernel(place_ref, picked_ref, expand_ref, entry_ref, table_ref, fold_ref, block_ref, hot_ref, out_ref):
    hot = (dot(picked_ref[...], expand_ref[0]) == entry_ref[...]).astype(LOW)
    hot_ref[0] = hot
    total = 0.0
    for i in (2, 1, 0):
        wide = (dot(table_ref[0, i], fold_ref[...], 1, 1) * block_ref[...]).astype(LOW)
        total = total + dot(hot, wide)
    out_ref[...] = total


def embed_tokens(place, picked, expand, entry, table, fold, block):
    tokens, rows, width = picked.shape[0], entry.shape[1], fold.shape[0]
    return pl.pallas_call(
        embed_kernel,
        out_shape=[
            jax.ShapeDtypeStruct((SHARERS, tokens, rows), LOW),
            jax.ShapeDtypeStruct((tokens, SHARERS * width), WIDE),
        ],
        grid_spec=pltpu.PrefetchScalarGridSpec(
            num_scalar_prefetch=1,
            grid=(SHARERS,),
            in_specs=[
                pl.BlockSpec(picked.shape, lambda j, place: (0, 0)),
                pl.BlockSpec((1, *expand.shape[1:]), lambda j, place: (j, 0, 0)),
                pl.BlockSpec(entry.shape, lambda j, place: (0, 0)),
                pl.BlockSpec((1, *table.shape[1:]), lambda j, place: (j ^ place[0], 0, 0, 0)),
                pl.BlockSpec(fold.shape, lambda j, place: (0, 0)),
                pl.BlockSpec(block.shape, lambda j, place: (0, 0)),
            ],
            out_specs=[
                pl.BlockSpec((1, tokens, rows), lambda j, place: (j, 0, 0)),
                pl.BlockSpec((tokens, width), lambda j, place: (0, j)),
            ],
        ),
        compiler_params=pltpu.CompilerParams(vmem_limit_bytes=40 * 2**20),
        cost_estimate=pl.CostEstimate(flops=1, bytes_accessed=1, transcendentals=0),
    )(place, picked, expand, entry, table, fold, block)


def join_kernel(*refs):
    rows = refs[0].shape[0]
    for k, ref in enumerate(refs[:-1]):
        refs[-1][k * rows : (k + 1) * rows, :] = ref[...]


def join_blocks(parts, turns):
    rows, columns = parts[0].shape
    width = columns // SHARERS
    return pl.pallas_call(
        join_kernel,
        out_shape=jax.ShapeDtypeStruct((len(parts) * rows, columns), parts[0].dtype),
        grid=(SHARERS,),
        in_specs=[pl.BlockSpec((rows, width), lambda j, t=t: (0, j ^ t)) for t in turns],
        out_specs=pl.BlockSpec((len(parts) * rows, width), lambda j: (0, j)),
        cost_estimate=pl.CostEstimate(
            flops=0, bytes_accessed=4 * len(parts) * rows * columns, transcendentals=0
        ),
    )(*parts)


def part_kernel(*refs):
    count = len(refs) // 3
    for left, right, out in zip(refs[:count], refs[count : 2 * count], refs[2 * count :]):
        out[...] = (left[...].astype(WIDE) + right[...].astype(WIDE)).astype(out.dtype)


def part_sums(left, right, turns):
    rows, columns = left.shape[0] // len(turns), left.shape[1]
    width = columns // SHARERS
    specs = [
        pl.BlockSpec((rows, width), lambda j, k=k, t=t: (k, j ^ t)) for k, t in enumerate(turns)
    ]
    return pl.pallas_call(
        part_kernel,
        out_shape=[
            jax.ShapeDtypeStruct((rows, columns), LOW if k else WIDE) for k in range(len(turns))
        ],
        grid=(SHARERS,),
        in_specs=specs + specs,
        out_specs=[pl.BlockSpec((rows, width), lambda j: (0, j))] * len(turns),
        cost_estimate=pl.CostEstimate(
            flops=left.size, bytes_accessed=6 * left.size, transcendentals=0
        ),
    )(*[left] * len(turns), *[right] * len(turns))


def small_kernel(decays, clip_ref, *refs):
    count = len(decays)
    clip = clip_ref[0]
    for i, decay in enumerate(decays):
        weight, gradient, first, second = (ref[...] for ref in refs[4 * i : 4 * i + 4])
        outs = refs[4 * count + 3 * i : 4 * count + 3 * i + 3]
        first_new, second_new, update = moments_of(weight, gradient, first, second, clip, decay)
        outs[0][...] = apply_trust(
            weight,
            update,
            jnp.sum(weight * weight, keepdims=True),
            jnp.sum(update * update, keepdims=True),
        )
        outs[1][...] = first_new
        outs[2][...] = second_new


def small_steps(clip, groups, decays):
    flat = [values for group in groups for values in group]
    return pl.pallas_call(
        functools.partial(small_kernel, decays),
        out_shape=[
            jax.ShapeDtypeStruct(group[0].shape, WIDE) for group in groups for _ in range(3)
        ],
        in_specs=[pl.BlockSpec(memory_space=pltpu.SMEM)]
        + [pl.BlockSpec(memory_space=pltpu.VMEM)] * len(flat),
        out_specs=[pl.BlockSpec(memory_space=pltpu.VMEM)] * (3 * len(groups)),
        compiler_params=pltpu.CompilerParams(vmem_limit_bytes=48 * 2**20),
    )(clip, *flat)


class Grid:
    def __init__(self, rows, heads):
        self.rows, self.heads = rows // SHARERS, heads
        self.each = H // heads
        self.parts = SHARERS // self.each
        self.members = SHARERS * heads
        self.shape = (self.rows, self.each, self.parts, heads)
        self.evens = range(2, self.members, 2)

    def sharer(self):
        return lax.axis_index("q") * self.parts + lax.axis_index("p")

    def pair(self, values, step):
        return lax.ppermute(values, ("q", "p", "h"), [(i, i ^ step) for i in range(self.members)])

    def trade(self, values, step):
        return lax.ppermute(values, ("q", "p"), [(i, i ^ step) for i in range(SHARERS)])

    def turns(self):
        return [0] + [d // self.heads for d in self.evens]

    def spread(self, own):
        parts = [own] + [self.pair(own, d) for d in self.evens]
        half = join_blocks(parts, self.turns())
        return half, self.pair(half, 1)

    def gathered_sum(self, half, other):
        parts = part_sums(half, self.pair(other, 1), self.turns())
        total = parts[0]
        for part, d in zip(parts[1:], self.evens):
            total = total + self.pair(part, d).astype(WIDE)
        return total

    def group_total(self, values):
        step = 1
        while step < self.members:
            values = values + self.pair(values, step)
            step *= 2
        return values

    def every(self, values):
        step = 1
        while step < self.members:
            values = jnp.concatenate([values, self.pair(values, step)], axis=0)
            step *= 2
        step = 1
        while step < self.rows:
            moved = lax.ppermute(values, "a", [(i, i ^ step) for i in range(self.rows)])
            values = jnp.concatenate([values, moved], axis=0)
            step *= 2
        return values

    def facing(self, values):
        return lax.ppermute(values, "a", [(0, 1), (1, 0)])

    def row_list(self, values):
        if self.rows == 2:
            return [values, self.facing(values)]
        every = lax.all_gather(values, "a", axis=0)
        return [every[i] for i in range(self.rows)]

    def row_gather(self, values):
        parts = self.row_list(values)
        if self.rows == 2:
            flag = lax.axis_index("a") == 1
            parts = exchange(flag, *parts)
        return list(parts)

    def row_sum(self, values):
        if self.rows == 2:
            return values.astype(WIDE) + self.facing(values).astype(WIDE)
        return lax.psum(values.astype(WIDE), "a")

    def total(self, values):
        return self.row_sum(self.group_total(values))

    def ordered(self, parts):
        place = self.sharer()
        low, high = place % 2 == 1, place // 2 == 1
        parts = [jnp.where(low, parts[j ^ 1], parts[j]) for j in range(SHARERS)]
        return [jnp.where(high, parts[j ^ 2], parts[j]) for j in range(SHARERS)]

    def absolute(self, values):
        return jnp.concatenate(self.ordered(jnp.split(values, SHARERS, axis=-1)), axis=-1)

    def to_rows(self, values):
        values = self.absolute(values)
        if self.rows != 2:
            return lax.all_to_all(values, "a", split_axis=0, concat_axis=1, tiled=True)
        flag = lax.axis_index("a") == 1
        kept, sent = exchange(flag, *jnp.split(values, 2, axis=0))
        return jnp.concatenate(exchange(flag, kept, self.facing(sent)), axis=1)

    def from_rows(self, values):
        if self.rows != 2:
            return self.absolute(
                lax.all_to_all(values, "a", split_axis=1, concat_axis=0, tiled=True)
            )
        flag = lax.axis_index("a") == 1
        kept, sent = exchange(flag, *jnp.split(values, 2, axis=1))
        moved = jnp.concatenate(exchange(flag, kept, self.facing(sent)), axis=0)
        return self.absolute(moved)

    def renamed(self, values, step):
        block = values.shape[0] // self.members
        span = 1
        while span < self.members // 2:
            if step // 2 & span:
                halves = values.reshape(-1, 2, span * block, values.shape[1])
                values = jnp.stack([halves[:, 1], halves[:, 0]], axis=1).reshape(values.shape)
            span *= 2
        return values

    def columns(self, values):
        found = [values]
        for d in range(1, self.parts):
            got = lax.ppermute(values, "p", [(i, i ^ d) for i in range(self.parts)])
            found.append(self.renamed(got, d * self.heads))
        return jnp.concatenate(found, axis=1)

    def local(self, values, axis):
        size = values.shape[axis] // (self.rows * SHARERS)
        first, place = lax.axis_index("a") * SHARERS, self.sharer()
        return [
            lax.dynamic_slice_in_dim(values, (first + (place ^ j)) * size, size, axis)
            for j in range(SHARERS)
        ]

    def stats(self, values, count):
        center = jnp.mean(values, axis=1)
        spread = jnp.sum(jnp.square(values - center[:, None]), axis=1)
        parts = self.row_list(jnp.stack([center, spread]))
        mean = sum(part[0] for part in parts) / self.rows
        size = count // self.rows
        square = sum(part[1] + size * jnp.square(part[0] - mean) for part in parts)
        return mean[:, None], lax.rsqrt(square / count + EPS_NORM)[:, None]

    def split_plain(self, values, parts, width):
        rows = values.shape[0]
        values = values.astype(LOW).reshape(rows, self.each, parts, self.parts, -1)
        values = values.transpose(1, 3, 0, 2, 4).reshape(SHARERS, rows, -1)
        return [
            lax.dynamic_index_in_dim(values, self.sharer() ^ j, 0, False) for j in range(SHARERS)
        ]

    def merge_plain(self, pieces, parts, width):
        values = jnp.stack(self.ordered(pieces))
        rows = values.shape[1]
        values = values.reshape(self.each, self.parts, rows, parts, -1)
        return values.transpose(2, 0, 3, 1, 4).reshape(rows, self.each, parts * width)


def tied(*values):
    return lax.optimization_barrier(values)


def split_three(values):
    high = lax.reduce_precision(values, 8, 7)
    rest = values - high
    middle = lax.reduce_precision(rest, 8, 7)
    return high.astype(LOW), middle.astype(LOW), (rest - middle).astype(LOW)


def per_device(grid, *arguments):
    (
        cell_ids,
        cell_mask,
        labels,
        abd_weights,
        abd_first,
        abd_second,
        abd_gains,
        abd_gains_first,
        abd_gains_second,
        aba_weights,
        aba_first,
        aba_second,
        aba_gains,
        aba_gains_first,
        aba_gains_second,
        embed_table,
        embed_first,
        embed_second,
        output_table,
        output_first,
        output_second,
    ) = arguments
    h = lax.axis_index("h")
    attr_count, entries, embed_width = embed_table.shape
    classes = output_table.shape[2]
    model_width = attr_count * embed_width
    own_tokens = cell_ids.shape[0] // grid.heads
    first_device = ((lax.axis_index("a") == 0) & (grid.sharer() == 0)).astype(WIDE)
    native = grid.each == 2
    side = jnp.stack([lax.axis_index("q"), lax.axis_index("p")]).astype(jnp.int32)

    def own_rows(values):
        return lax.dynamic_slice_in_dim(values, h * own_tokens, own_tokens, 0)

    attrs_held = labels.shape[1]
    mask_held = lax.dynamic_slice_in_dim(cell_mask, h * attrs_held, attrs_held, 1)
    codes = jnp.where(mask_held == 1, labels, -1).reshape(own_tokens, attr_count)
    picked = own_rows(jnp.where(cell_mask == 1, classes, cell_ids))
    gathered = grid.every(jnp.concatenate([picked, codes], axis=1).astype(LOW))
    tokens = gathered.shape[0]
    picked_all = gathered[:, :attr_count]
    codes_all = gathered[:, attr_count:].reshape(-1, grid.heads, own_tokens, attr_count)
    device = (lax.axis_index("a") * SHARERS + grid.sharer()) * grid.heads + h

    def by_head(parts):
        for bit in range((grid.heads - 1).bit_length()):
            flag = (h >> bit) % 2 == 1
            parts = [
                jnp.where(flag, parts[d ^ (1 << bit)], parts[d]) for d in range(grid.heads)
            ]
        return parts

    def pieces_of(sections):
        if native:
            return split_weights(weight_view, side, sections)
        found = []
        for offset, parts, size in sections:
            columns = abd_weights[:, :, offset : offset + parts * size]
            found.append(grid.split_plain(columns, parts, size))
        return [jnp.concatenate(piece, axis=1) for piece in zip(*found)]

    def traded(values):
        return [values[0]] + [grid.trade(values[j], j) for j in (1, 2, 3)]

    weight_view = native_view(abd_weights) if native else None
    qkv_pieces, table = tied(pieces_of(SECTIONS[:1]), embed_table)
    qkv_pieces, picked_all, side = tied(qkv_pieces, picked_all, side)
    qkv_w = traded(qkv_pieces)
    picked_all, other_pieces = tied(picked_all, pieces_of(SECTIONS[1:3]))

    held = tokens // grid.members
    place = jnp.arange(tokens, dtype=jnp.int32)
    owner, inside = place // held, place % held
    owner = 2 * (owner % (grid.members // 2)) + owner // (grid.members // 2)
    owner = owner ^ (grid.sharer() * grid.heads + h)
    source = (inside // own_tokens * grid.members + owner) ^ device
    row_of = source * own_tokens + inside % own_tokens
    picked = dot((row_of[:, None] == place[None, :]).astype(LOW), picked_all).astype(LOW)
    picked = jnp.concatenate(grid.local(picked, 1), axis=1)
    local_attrs = picked.shape[1]
    block_attrs = local_attrs // SHARERS
    table_rows = jnp.arange(block_attrs * entries, dtype=jnp.int32)
    row_attr, row_entry = table_rows // entries, (table_rows % entries).astype(WIDE)
    block_columns = jnp.arange(block_attrs * embed_width, dtype=jnp.int32)
    own_block = row_attr[:, None] == block_columns // embed_width
    fold = (
        block_columns[:, None] % embed_width == jnp.arange(embed_width, dtype=jnp.int32)
    ).astype(LOW)
    table = lax.dynamic_slice_in_dim(table, lax.axis_index("a") * local_attrs, local_attrs, 0)
    table = table.reshape(SHARERS, row_attr.size, embed_width)
    places = jnp.arange(local_attrs, dtype=jnp.int32)
    expand = places[None, :, None] == (
        jnp.arange(SHARERS, dtype=jnp.int32)[:, None, None] * block_attrs + row_attr[None, None, :]
    )
    hots, embedded = embed_tokens(
        grid.sharer().astype(jnp.int32)[None],
        picked,
        expand.astype(LOW),
        row_entry[None, :],
        jnp.stack(split_three(table), axis=1),
        fold,
        own_block.astype(WIDE),
    )
    embedded, qkv_w, other_pieces, side = tied(embedded, qkv_w, other_pieces, side)
    qkv_w = jnp.concatenate(qkv_w, axis=0)
    others = traded(other_pieces)

    kinds = jnp.arange(classes, dtype=jnp.int32).astype(WIDE)
    mask_own = own_rows(cell_mask).astype(WIDE)
    counts, own_codes = [], []
    for d in range(grid.heads):
        found = (codes_all[:, d].reshape(-1, attr_count)[:, :, None].astype(WIDE) == kinds)
        found = jnp.sum(found.astype(WIDE), axis=0)
        counts.append(jnp.sum(found.reshape(-1, attrs_held, classes), axis=0))
        own_codes.append(own_rows(codes_all[0, d].reshape(-1, attrs_held)))
    counts = jnp.concatenate(by_head(counts), axis=0)
    own_codes = jnp.concatenate(by_head(own_codes), axis=1)
    label_hot = (own_codes.astype(WIDE)[:, :, None] == kinds).astype(WIDE)
    class_weight = lax.rsqrt(1.0 + counts)
    weight_total = jnp.sum(counts * class_weight)
    tables_low = output_table.astype(LOW)[None]
    step = 1
    while step < grid.heads:
        tables_low = jnp.concatenate([tables_low, grid.pair(tables_low, step)], axis=0)
        step *= 2
    output_low = jnp.concatenate(by_head(list(tables_low)), axis=0)

    out_size, up_size = HD * grid.each // SHARERS, UNITS * grid.each // SHARERS
    gains = jnp.concatenate(grid.local(abd_gains, 1), axis=1)
    mean_one, scale_one = grid.stats(embedded, model_width)
    hat_one = (embedded - mean_one) * scale_one
    normed = (hat_one * gains[0]).astype(LOW)
    triple = grid.row_sum(dot(normed, qkv_w).astype(LOW)).astype(LOW)
    triple, others, class_weight, weight_total, label_hot, output_low, down_pieces = tied(
        triple, others, class_weight, weight_total, label_hot, output_low, pieces_of(SECTIONS[3:])
    )
    part = HD // grid.parts
    query_own, key_own, value_own = (triple[:, i * part : (i + 1) * part] for i in range(3))
    queries, key_rows = grid.columns(query_own), grid.columns(key_own)
    value_rows = grid.columns(value_own)
    factor = HD ** (-0.5)
    scores = dot(queries, key_rows, 1, 1) * factor
    shifted = jnp.exp(scores - jnp.max(scores, axis=1, keepdims=True))
    probs = shifted / jnp.sum(shifted, axis=1, keepdims=True)
    probs_low = probs.astype(LOW)
    attended = dot(probs_low, value_own).astype(LOW)
    out_w = jnp.concatenate([piece[:, :out_size] for piece in others], axis=0)
    up_w = jnp.concatenate([piece[:, out_size:] for piece in others], axis=0)
    attended = jnp.split(attended, 2, axis=0)
    branch = [dot(a, out_w, 1, 1).astype(LOW) for a in attended]
    middle = embedded[:held] + grid.gathered_sum(*branch)
    mean_two, scale_two = grid.stats(middle, model_width)
    hat_two = (middle - mean_two) * scale_two
    second = grid.spread((hat_two * gains[1]).astype(LOW))
    before, down_pieces = tied([dot(a, up_w).astype(LOW) for a in second], down_pieces)
    before = [grid.row_sum(b) for b in before]
    before[0], down_w, up_turned, qkv_turned = tied(
        before[0], traded(down_pieces), up_w.T, qkv_w.T
    )
    down_w = jnp.concatenate(down_w, axis=0)
    hidden = [gelu_apply(before[0]).astype(LOW)]
    down = [dot(hidden[0], down_w, 1, 1).astype(LOW)]
    before[1], hidden[0], down[0] = tied(before[1], hidden[0], down[0])
    hidden.append(gelu_apply(before[1]).astype(LOW))
    down.append(dot(hidden[1], down_w, 1, 1).astype(LOW))
    after = middle + grid.gathered_sum(*down)

    aba_low = aba_weights.astype(LOW)
    final, aba_stored = aba_forward(grid.to_rows(after), aba_low, aba_gains)
    final_low = final.reshape(own_tokens, attr_count, embed_width).astype(LOW)
    logits = jnp.einsum("tfe,fec->tfc", final_low, output_low, preferred_element_type=WIDE)
    highest = jnp.max(logits, axis=-1, keepdims=True)
    exped = jnp.exp(logits - highest)
    totals = jnp.sum(exped, axis=-1, keepdims=True)
    log_total = (highest + jnp.log(totals))[:, :, 0]
    cell_weight = mask_own * jnp.sum(label_hot * class_weight[None], axis=-1)
    loss_local = jnp.sum(cell_weight * (log_total - jnp.sum(label_hot * logits, axis=-1)))
    logit_grad = ((cell_weight / weight_total)[:, :, None] * (exped / totals - label_hot)).astype(
        LOW
    )
    final_grad = jnp.einsum("tfc,fec->tfe", logit_grad, output_low, preferred_element_type=WIDE)
    output_part = jnp.einsum("tfe,tfc->fce", final_low, logit_grad, preferred_element_type=WIDE)
    rows_grad, aba_part, aba_gains_part = aba_backward(
        final_grad.reshape(own_tokens, model_width), aba_stored, aba_low, aba_gains
    )

    width = normed.shape[1] // SHARERS
    gradient_sq = []

    def row_gradients(acts, uppers):
        found = []
        for j in range(SHARERS):
            cut = slice(j * width, (j + 1) * width)
            piece = sum(dot(a[:, cut], u, 0, 0) for a, u in zip(acts, uppers)).astype(LOW)
            gradient_sq.append(jnp.sum(jnp.square(piece.astype(WIDE))))
            found.append(piece)
        return found

    upstream = grid.from_rows(rows_grad.astype(LOW))
    down_grad = grid.spread(upstream)
    hidden_grad = tied(*[dot(a, down_w).astype(LOW) for a in down_grad])
    hidden_grad = [grid.row_sum(g) for g in hidden_grad]
    down_gradient = traded(row_gradients(down_grad, hidden))

    hidden_grad[0], down_gradient = tied(hidden_grad[0], down_gradient)

    before_grad = [gelu_back(before[0], hidden_grad[0]).astype(LOW)]
    second_grad = [dot(before_grad[0], up_turned).astype(LOW)]
    hidden_grad[1], before_grad[0], second_grad[0] = tied(
        hidden_grad[1], before_grad[0], second_grad[0]
    )
    before_grad.append(gelu_back(before[1], hidden_grad[1]).astype(LOW))
    second_grad.append(dot(before_grad[1], up_turned).astype(LOW))
    second_grad = grid.gathered_sum(*second_grad)
    gained = second_grad * gains[1]
    sums = jnp.stack([jnp.sum(gained, axis=1), jnp.sum(gained * hat_two, axis=1)])
    sums = sum(grid.row_list(sums)) / model_width
    middle_grad = upstream.astype(WIDE) + scale_two * (
        gained - sums[0][:, None] - hat_two * sums[1][:, None]
    )
    middle_grad, up_gradient = tied(middle_grad, row_gradients(second, before_grad))
    up_gradient = traded(up_gradient)
    gain_two = jnp.sum(second_grad * hat_two, axis=0)
    branch_grad = grid.spread(middle_grad.astype(LOW))
    attended_grad = jnp.concatenate([dot(a, out_w).astype(LOW) for a in branch_grad], axis=0)
    attended_grad, attended, table_acts, output_part, aba_part, aba_gains_part = tied(
        attended_grad, attended, middle_grad.astype(LOW), output_part, aba_part, aba_gains_part
    )

    small = jnp.concatenate([aba_part.reshape(-1), aba_gains_part.reshape(-1)])
    blocks = output_part.reshape(grid.heads, -1)
    bits = (grid.heads - 1).bit_length()
    for bit in range(bits):
        flag = (h >> bit) % 2 == 1
        halves = blocks.reshape(-1, 2, blocks.shape[1])
        kept, sent = exchange(flag, halves[:, 0], halves[:, 1])
        got = grid.pair(jnp.concatenate([sent.reshape(-1), small]).reshape(-1, 128), 1 << bit)
        got = got.reshape(-1)
        blocks = kept + got[: sent.size].reshape(kept.shape)
        small = small + got[sent.size :]
    packed = jnp.concatenate([blocks.reshape(-1), small]).reshape(-1, 128)
    for step in (grid.heads, 2 * grid.heads):
        packed = packed + grid.pair(packed, step)
    packed = grid.row_sum(packed.astype(LOW)).reshape(-1)
    output_grad = packed[: blocks.size].reshape(-1, classes, embed_width)
    aba_grad = packed[blocks.size : blocks.size + aba_weights.size].reshape(aba_weights.shape)
    aba_gains_grad = packed[blocks.size + aba_weights.size :].reshape(aba_gains.shape)

    attended_grad, up_gradient, output_grad, aba_grad, aba_gains_grad = tied(
        grid.row_sum(attended_grad).astype(LOW), up_gradient, output_grad, aba_grad, aba_gains_grad
    )
    out_gradient = row_gradients(branch_grad, attended)
    prob_grad = dot(grid.columns(attended_grad), value_rows, 1, 1)
    score_grad = probs * (prob_grad - jnp.sum(probs * prob_grad, axis=1, keepdims=True))
    score_grad = score_grad.astype(LOW)
    query_grad = dot(score_grad, key_own) * factor
    key_grad = dot(score_grad, query_own, 0, 0) * factor
    value_grad = dot(probs_low, attended_grad, 0, 0)
    triple_grad = jnp.concatenate([query_grad, key_grad, value_grad], axis=1).astype(LOW)
    table_part = [
        dot(hot[:held], block, 0, 0)
        for hot, block in zip(hots, jnp.split(table_acts, SHARERS, axis=1))
    ]
    triple_grad, table_part, out_gradient = tied(triple_grad, table_part, out_gradient)
    qkv_gradient = row_gradients([normed], [triple_grad])
    qkv_gradient = [jnp.concatenate(pair, axis=1) for pair in zip(qkv_gradient, out_gradient)]
    triple_grad, qkv_gradient = tied(triple_grad, qkv_gradient)

    normed_grad = dot(triple_grad, qkv_turned)
    gained = normed_grad * gains[0]
    sums = jnp.stack([jnp.sum(gained, axis=1), jnp.sum(gained * hat_one, axis=1)])
    sums = sum(grid.row_list(sums)) / model_width
    gain_one = jnp.sum(normed_grad * hat_one, axis=0)
    spread_grad = scale_one * (gained - sums[0][:, None] - hat_one * sums[1][:, None])
    records = []
    for j, block in enumerate(jnp.split(spread_grad.astype(LOW), SHARERS, axis=1)):
        grad = table_part[j] + dot(hots[j], block, 0, 0)
        grad = jnp.where(own_block, grad, 0.0)
        grad = jnp.dot(grad, fold.astype(WIDE), precision=lax.Precision.HIGHEST)
        cut = slice(j * width, (j + 1) * width)
        records.append(jnp.concatenate([grad.reshape(-1), gain_one[cut], gain_two[cut]]))
    table_size = block_attrs * entries * embed_width
    packed = jnp.stack(grid.ordered(records)).reshape(-1, 128)
    output_sq = first_device * jnp.sum(output_grad * output_grad)
    scalars = jnp.stack([sum(gradient_sq), output_sq, loss_local])
    lane = jnp.arange(8 * 128, dtype=jnp.int32).reshape(8, 128)
    scalars = sum(jnp.where(lane == i, scalars[i], 0.0) for i in range(3))
    packed, qkv_gradient = tied(packed, traded(qkv_gradient))
    gradients = qkv_gradient + up_gradient + down_gradient
    packed = jnp.stack(
        grid.row_gather(grid.group_total(jnp.concatenate([scalars, packed], axis=0)))
    )
    summed = jnp.sum(packed[:, 0, :3], axis=0)
    packed = packed[:, 8:].reshape(grid.rows * SHARERS, -1)
    embed_grad = packed[:, :table_size].reshape(embed_table.shape).transpose(1, 0, 2)
    abd_gains_grad = packed[:, table_size:].reshape(-1, 2, width).transpose(1, 0, 2)
    abd_gains_grad = abd_gains_grad.reshape(2, model_width)

    output_table, output_first, output_second = (
        values.transpose(0, 2, 1) for values in (output_table, output_first, output_second)
    )
    embed_table, embed_first, embed_second = (
        values.transpose(1, 0, 2) for values in (embed_table, embed_first, embed_second)
    )
    replicated_sq = (
        jnp.sum(abd_gains_grad * abd_gains_grad)
        + jnp.sum(aba_grad * aba_grad)
        + jnp.sum(aba_gains_grad * aba_gains_grad)
        + jnp.sum(embed_grad * embed_grad)
    )
    grad_norm = jnp.sqrt(summed[0] + summed[1] + replicated_sq)
    loss_sum = summed[2]
    clip_factor = jnp.minimum(1.0, CLIP_LIMIT / (grad_norm + 1e-06))
    if native:
        first_view, second_view, abd_update, squares = moments_step(
            side,
            clip_factor[None],
            weight_view,
            native_view(abd_first),
            native_view(abd_second),
            gradients,
        )
        abd_first_new = from_native(first_view, grid.each)
        abd_second_new = from_native(second_view, grid.each)
        abd_update_sq, abd_weight_sq = jnp.sum(squares[0]), jnp.sum(squares[1])
    else:
        first_g, up_g, down_g = (gradients[SHARERS * i : SHARERS * (i + 1)] for i in range(3))
        split_g = (
            [g[:, : 3 * out_size] for g in first_g],
            [g[:, 3 * out_size :] for g in first_g],
            up_g,
            down_g,
        )
        merged = [
            grid.merge_plain(pieces, parts, size)
            for pieces, (_, parts, size) in zip(split_g, SECTIONS)
        ]
        abd_grad = jnp.concatenate(merged, axis=2).astype(WIDE)
        abd_first_new, abd_second_new, abd_update = moments_of(
            abd_weights, abd_grad, abd_first, abd_second, clip_factor, WEIGHT_DECAY
        )
        abd_update_sq, abd_weight_sq = (
            jnp.sum(abd_update * abd_update),
            jnp.sum(abd_weights * abd_weights),
        )
    output_first_new, output_second_new, output_update = moments_of(
        output_table, output_grad, output_first, output_second, clip_factor, WEIGHT_DECAY
    )
    trust_sums = grid.total(
        jnp.stack(
            [
                abd_update_sq,
                first_device * jnp.sum(output_update * output_update),
                abd_weight_sq,
                first_device * jnp.sum(output_table * output_table),
            ]
        )
    )
    if native:
        abd_new = from_native(
            apply_trust(weight_view, abd_update.astype(WIDE), trust_sums[2], trust_sums[0]),
            grid.each,
        )
    else:
        abd_new = apply_trust(abd_weights, abd_update, trust_sums[2], trust_sums[0])
    output_new = apply_trust(output_table, output_update, trust_sums[3], trust_sums[1])
    small = small_steps(
        clip_factor[None],
        (
            (abd_gains, abd_gains_grad, abd_gains_first, abd_gains_second),
            (aba_weights, aba_grad, aba_first, aba_second),
            (aba_gains, aba_gains_grad, aba_gains_first, aba_gains_second),
            (embed_table, embed_grad, embed_first, embed_second),
        ),
        (0.0, WEIGHT_DECAY, 0.0, WEIGHT_DECAY),
    )
    return (
        loss_sum,
        weight_total,
        grad_norm,
        abd_new,
        abd_first_new,
        abd_second_new,
        *small[:9],
        *[values.transpose(1, 0, 2) for values in small[9:]],
        *[values.transpose(0, 2, 1) for values in (output_new, output_first_new, output_second_new)],
    )


def solution(mesh):
    grid = Grid(mesh.shape["dp"], mesh.shape["head"])
    devices = Mesh(mesh.devices.reshape(grid.shape), ("a", "q", "p", "h"))
    rows = ("a", "q", "p")
    tokens, table = P(rows, None), P("h", None, None)
    weight = P(rows, "h", None)
    in_specs = (tokens, tokens, P(rows, "h"), weight, weight, weight) + (P(),) * 12 + (table,) * 3
    out_specs = (P(),) * 3 + (weight,) * 3 + (P(),) * 12 + (table,) * 3
    return jax.shard_map(
        functools.partial(per_device, grid),
        mesh=devices,
        in_specs=in_specs,
        out_specs=out_specs,
        check_vma=False,
    )
```

```python
import functools

import jax
import jax.experimental.pallas as pl
import jax.experimental.pallas.tpu as pltpu
import jax.numpy as jnp
from jax import lax
from jax.sharding import Mesh
from jax.sharding import PartitionSpec as P

H = 8
AH = 8
STEP = 10
HD = 512
FF = 16384


EPS_NORM = 1e-05
CLIP_LIMIT = 0.01
LEARN_RATE = 0.3
BETA_FIRST = 0.9
BETA_SECOND = 0.999
ADAM_EPSILON = 1e-08
WEIGHT_DECAY = 0.01


def layer_norm(values, gain_row):
    center = jnp.mean(values, axis=-1, keepdims=True)
    centred = values - center
    spread = jnp.mean(centred * centred, axis=-1, keepdims=True)
    return centred * lax.rsqrt(spread + EPS_NORM) * gain_row


def gelu_apply(values):
    return 0.5 * values * (1.0 + lax.erf(values * 0.7071067811865476))


def norm_back(values, gain_row, upstream):
    unused_value, pull_back = jax.vjp(layer_norm, values, gain_row)
    return pull_back(upstream)


def gelu_back(values, upstream):
    unused_value, pull_back = jax.vjp(gelu_apply, values)
    return pull_back(upstream)[0]


def attend_keys(queries, key_rows, value_rows, factor):
    scores = (
        jnp.einsum("...qd,...kd->...qk", queries, key_rows, preferred_element_type=jnp.float32)
        * factor
    )
    highest = jnp.max(scores, axis=-1, keepdims=True)
    weights = jnp.exp(scores - highest)
    totals = jnp.sum(weights, axis=-1, keepdims=True)
    result = jnp.einsum(
        "...qk,...kd->...qd",
        (weights / totals).astype(jnp.bfloat16),
        value_rows,
        preferred_element_type=jnp.float32,
    )
    return (result, highest + jnp.log(totals))


def attend_back(queries, key_rows, value_rows, log_total, result_grad, factor):
    scores = (
        jnp.einsum("...qd,...kd->...qk", queries, key_rows, preferred_element_type=jnp.float32)
        * factor
    )
    softmax_probs = jnp.exp(scores - log_total)
    prob_grad = jnp.einsum(
        "...qd,...kd->...qk", result_grad, value_rows, preferred_element_type=jnp.float32
    )
    score_grad = softmax_probs * (
        prob_grad - jnp.sum(softmax_probs * prob_grad, axis=-1, keepdims=True)
    )
    score_grad = score_grad.astype(jnp.bfloat16)
    query_grad = (
        jnp.einsum("...qk,...kd->...qd", score_grad, key_rows, preferred_element_type=jnp.float32)
        * factor
    )
    key_grad = (
        jnp.einsum("...qk,...qd->...kd", score_grad, queries, preferred_element_type=jnp.float32)
        * factor
    )
    value_grad = jnp.einsum(
        "...qk,...qd->...kd",
        softmax_probs.astype(jnp.bfloat16),
        result_grad,
        preferred_element_type=jnp.float32,
    )
    return (query_grad, key_grad, value_grad)


def aba_forward(row_block, weights, gain_rows):
    embed_width = weights.shape[0]
    row_count = row_block.shape[0]
    attr_count = row_block.shape[1] // embed_width
    size_each = embed_width // AH
    inputs = row_block.reshape(row_count, attr_count, embed_width)
    normed = layer_norm(inputs, gain_rows[0]).astype(jnp.bfloat16)
    projection = weights[:, : 3 * embed_width].reshape(embed_width, 3, AH, size_each)
    triple = jnp.einsum(
        "rfe,eshd->srhfd", normed, projection, preferred_element_type=jnp.float32
    ).astype(jnp.bfloat16)
    attended, log_total = attend_keys(triple[0], triple[1], triple[2], size_each ** (-0.5))
    attended = attended.astype(jnp.bfloat16)
    out_proj = weights[:, 3 * embed_width : 4 * embed_width].reshape(embed_width, AH, size_each)
    middle = inputs + jnp.einsum(
        "rhfd,ohd->rfo", attended, out_proj, preferred_element_type=jnp.float32
    )
    second = layer_norm(middle, gain_rows[1]).astype(jnp.bfloat16)
    before = jnp.einsum(
        "rfe,eu->rfu",
        second,
        weights[:, 4 * embed_width : 8 * embed_width],
        preferred_element_type=jnp.float32,
    )
    hidden = gelu_apply(before).astype(jnp.bfloat16)
    after = middle + jnp.einsum(
        "rfu,ou->rfo", hidden, weights[:, 8 * embed_width :], preferred_element_type=jnp.float32
    )
    return (
        after.reshape(row_count, attr_count * embed_width),
        (inputs, normed, triple, log_total, attended, middle, second, before, hidden),
    )


def aba_backward(upstream, stored, weights, gain_rows):
    inputs, normed, triple, log_total, attended, middle, second, before, hidden = stored
    row_count, attr_count, embed_width = inputs.shape
    size_each = embed_width // AH
    upstream = upstream.reshape(row_count, attr_count, embed_width)
    down_grad = upstream.astype(jnp.bfloat16)
    hidden_grad = jnp.einsum(
        "rfo,ou->rfu", down_grad, weights[:, 8 * embed_width :], preferred_element_type=jnp.float32
    )
    before_grad = gelu_back(before, hidden_grad).astype(jnp.bfloat16)
    second_grad = jnp.einsum(
        "rfu,eu->rfe",
        before_grad,
        weights[:, 4 * embed_width : 8 * embed_width],
        preferred_element_type=jnp.float32,
    )
    middle_part, gain_two = norm_back(middle, gain_rows[1], second_grad)
    middle_grad = upstream + middle_part
    branch_grad = middle_grad.astype(jnp.bfloat16)
    out_proj = weights[:, 3 * embed_width : 4 * embed_width].reshape(embed_width, AH, size_each)
    attended_grad = jnp.einsum(
        "rfo,ohd->rhfd", branch_grad, out_proj, preferred_element_type=jnp.float32
    ).astype(jnp.bfloat16)
    query_grad, key_grad, value_grad = attend_back(
        triple[0], triple[1], triple[2], log_total, attended_grad, size_each ** (-0.5)
    )
    triple_grad = jnp.stack([query_grad, key_grad, value_grad]).astype(jnp.bfloat16)
    projection = weights[:, : 3 * embed_width].reshape(embed_width, 3, AH, size_each)
    normed_grad = jnp.einsum(
        "srhfd,eshd->rfe", triple_grad, projection, preferred_element_type=jnp.float32
    )
    input_part, gain_one = norm_back(inputs, gain_rows[0], normed_grad)
    input_grad = middle_grad + input_part
    weight_grad = jnp.concatenate(
        [
            jnp.einsum(
                "rfe,srhfd->eshd", normed, triple_grad, preferred_element_type=jnp.float32
            ).reshape(embed_width, 3 * embed_width),
            jnp.einsum(
                "rfo,rhfd->ohd", branch_grad, attended, preferred_element_type=jnp.float32
            ).reshape(embed_width, embed_width),
            jnp.einsum("rfe,rfu->eu", second, before_grad, preferred_element_type=jnp.float32),
            jnp.einsum("rfo,rfu->ou", down_grad, hidden, preferred_element_type=jnp.float32),
        ],
        axis=1,
    )
    return (
        input_grad.reshape(row_count, attr_count * embed_width),
        weight_grad,
        jnp.stack([gain_one, gain_two]),
    )


def moments_of(weight, gradient, first, second, clip_factor, decay):
    scaled = gradient * clip_factor
    first_new = BETA_FIRST * first + (1.0 - BETA_FIRST) * scaled
    second_new = BETA_SECOND * second + (1.0 - BETA_SECOND) * scaled * scaled
    update = (
        first_new
        / (1.0 - BETA_FIRST**STEP)
        / (jnp.sqrt(second_new / (1.0 - BETA_SECOND**STEP)) + ADAM_EPSILON)
        + decay * weight
    )
    return (first_new, second_new, update)


def apply_trust(weight, update, weight_sq, update_sq):
    trust_ratio = jnp.sqrt(weight_sq) / (jnp.sqrt(update_sq) + 1e-06)
    return weight - LEARN_RATE * trust_ratio * update


def local_step(weight, gradient, first, second, clip_factor, decay):
    first_new, second_new, update = moments_of(weight, gradient, first, second, clip_factor, decay)
    return (
        apply_trust(weight, update, jnp.sum(weight * weight), jnp.sum(update * update)),
        first_new,
        second_new,
    )


LOW = jnp.bfloat16
WIDE = jnp.float32
SHARERS = 4
FIRST_SCALE = 1.0 / (1.0 - BETA_FIRST**STEP)
SECOND_SCALE = 1.0 / (1.0 - BETA_SECOND**STEP)
UNITS = FF // H
SOURCES = ((0, 0), (0, 3 * HD // 2), (1, 0), (2, 0))
SECTIONS = ((0, 3, HD), (3 * HD, 1, HD), (4 * HD, 1, UNITS), (4 * HD + UNITS, 1, UNITS))


def dot(left, right, left_dim=1, right_dim=0):
    return lax.dot_general(
        left, right, (((left_dim,), (right_dim,)), ((), ())), preferred_element_type=WIDE
    )


def native_view(values):
    rows, heads, columns = values.shape
    return (
        values.reshape(rows, heads, columns // 128, 128)
        .transpose(0, 2, 1, 3)
        .reshape(rows, columns // 128 * heads, 128)
    )


def from_native(values, heads):
    rows, count, width = values.shape
    return (
        values.reshape(rows, count // heads, heads, width)
        .transpose(0, 2, 1, 3)
        .reshape(rows, heads, count // heads * width)
    )


def tile_pairs(parts, width):
    each = width // 128
    return [
        (part * each + i, part * each + each // 2 + i)
        for part in range(parts)
        for i in range(each // 2)
    ]


def exchange(flag, left, right):
    return jnp.where(flag, right, left), jnp.where(flag, left, right)


def cross(q_flag, p_flag, values):
    a, b = exchange(p_flag, values[0], values[1])
    c, d = exchange(p_flag, values[2], values[3])
    a, c = exchange(q_flag, a, c)
    b, d = exchange(q_flag, b, d)
    return a, b, c, d


def split_kernel(sections, side_ref, *refs):
    weight_refs, out_refs = refs[: len(sections)], refs[len(sections) :]
    q_flag, p_flag = side_ref[0] == 1, side_ref[1] == 1
    lane = 0
    for weight_ref, (_, parts, width) in zip(weight_refs, sections):
        turned = {}
        for left, right in tile_pairs(parts, width):
            for group in (left // 4, right // 4):
                if group not in turned:
                    rows = weight_ref[:, group * 8 : group * 8 + 8, :]
                    turned[group] = jnp.swapaxes(rows, 0, 1)
            values = [
                turned[t // 4][t % 4 * 2 + head] for head in range(2) for t in (left, right)
            ]
            for ref, value in zip(out_refs, cross(q_flag, p_flag, values)):
                ref[:, lane : lane + 128] = value.astype(LOW)
            lane += 128


def split_weights(view, side, sections):
    rows = view.shape[0]
    total = sum(parts * width for _, parts, width in sections)
    block = 32

    def section_spec(offset, size):
        return pl.BlockSpec((block, size // 64, 128), lambda i: (i, offset // size, 0))

    return pl.pallas_call(
        functools.partial(split_kernel, sections),
        out_shape=[jax.ShapeDtypeStruct((rows, total // 2), LOW)] * SHARERS,
        grid=(rows // block,),
        in_specs=[pl.BlockSpec(memory_space=pltpu.SMEM)]
        + [section_spec(offset, parts * width) for offset, parts, width in sections],
        out_specs=[pl.BlockSpec((block, total // 2), lambda i: (i, 0))] * SHARERS,
        compiler_params=pltpu.CompilerParams(vmem_limit_bytes=40 * 2**20),
        cost_estimate=pl.CostEstimate(flops=1, bytes_accessed=1, transcendentals=0),
    )(side, *[view] * len(sections))


def moments_kernel(side_ref, clip_ref, weight_ref, first_ref, second_ref, *rest):
    gradients, (first_out, second_out, update_out, total_ref) = rest[:-4], rest[-4:]
    q_flag, p_flag = side_ref[0] == 1, side_ref[1] == 1
    clip = clip_ref[0]

    @pl.when(pl.program_id(0) == 0)
    def _():
        total_ref[...] = jnp.zeros_like(total_ref)

    update_sq = jnp.zeros((8, 128), WIDE)
    weight_sq = jnp.zeros((8, 128), WIDE)
    for (offset, parts, width), (index, lane) in zip(SECTIONS, SOURCES):
        refs = gradients[SHARERS * index : SHARERS * (index + 1)]
        places = {}
        for tile, (left, right) in enumerate(tile_pairs(parts, width)):
            lanes = slice(lane + tile * 128, lane + tile * 128 + 128)
            values = [ref[:, lanes].astype(WIDE) for ref in refs]
            a, b, c, d = cross(q_flag, p_flag, values)
            places[2 * left], places[2 * right] = a, b
            places[2 * left + 1], places[2 * right + 1] = c, d
            for group in (left // 4, right // 4):
                rows = range(group * 8, group * 8 + 8)
                if any(row not in places for row in rows):
                    continue
                scaled = jnp.swapaxes(jnp.stack([places.pop(r) for r in rows], axis=0), 0, 1) * clip
                here = pl.ds(offset // 64 + group * 8, 8)
                weight = weight_ref[:, here, :]
                first_new = BETA_FIRST * first_ref[:, here, :] + (1.0 - BETA_FIRST) * scaled
                second_new = (
                    BETA_SECOND * second_ref[:, here, :] + (1.0 - BETA_SECOND) * scaled * scaled
                )
                first_out[:, here, :] = first_new
                second_out[:, here, :] = second_new
                update = (
                    first_new * FIRST_SCALE / (jnp.sqrt(second_new * SECOND_SCALE) + ADAM_EPSILON)
                    + WEIGHT_DECAY * weight
                )
                update_out[:, here, :] = update.astype(update_out.dtype)
                update_sq += jnp.sum(update * update, axis=0)
                weight_sq += jnp.sum(weight * weight, axis=0)
    total_ref[0] += update_sq
    total_ref[1] += weight_sq


def moments_step(side, clip, weight, first, second, gradients):
    rows, depth, _ = weight.shape
    block = min(64, rows)
    whole = pl.BlockSpec((block, depth, 128), lambda i: (i, 0, 0))
    shape = jax.ShapeDtypeStruct(weight.shape, WIDE)
    return pl.pallas_call(
        moments_kernel,
        out_shape=[
            shape,
            shape,
            jax.ShapeDtypeStruct(weight.shape, LOW),
            jax.ShapeDtypeStruct((2, 8, 128), WIDE),
        ],
        grid=(rows // block,),
        in_specs=[pl.BlockSpec(memory_space=pltpu.SMEM)] * 2
        + [whole] * 3
        + [pl.BlockSpec((block, g.shape[1]), lambda i: (i, 0)) for g in gradients],
        out_specs=[whole] * 3 + [pl.BlockSpec((2, 8, 128), lambda i: (0, 0, 0))],
        compiler_params=pltpu.CompilerParams(vmem_limit_bytes=48 * 2**20),
        cost_estimate=pl.CostEstimate(
            flops=weight.size * 20, bytes_accessed=weight.size * 24, transcendentals=weight.size
        ),
    )(side, clip, weight, first, second, *gradients)


def embed_kernel(place_ref, picked_ref, expand_ref, entry_ref, table_ref, fold_ref, block_ref, hot_ref, out_ref):
    hot = (dot(picked_ref[...], expand_ref[0]) == entry_ref[...]).astype(LOW)
    hot_ref[0] = hot
    total = 0.0
    for i in (2, 1, 0):
        wide = (dot(table_ref[0, i], fold_ref[...], 1, 1) * block_ref[...]).astype(LOW)
        total = total + dot(hot, wide)
    out_ref[...] = total


def embed_tokens(place, picked, expand, entry, table, fold, block):
    tokens, rows, width = picked.shape[0], entry.shape[1], fold.shape[0]
    return pl.pallas_call(
        embed_kernel,
        out_shape=[
            jax.ShapeDtypeStruct((SHARERS, tokens, rows), LOW),
            jax.ShapeDtypeStruct((tokens, SHARERS * width), WIDE),
        ],
        grid_spec=pltpu.PrefetchScalarGridSpec(
            num_scalar_prefetch=1,
            grid=(SHARERS,),
            in_specs=[
                pl.BlockSpec(picked.shape, lambda j, place: (0, 0)),
                pl.BlockSpec((1, *expand.shape[1:]), lambda j, place: (j, 0, 0)),
                pl.BlockSpec(entry.shape, lambda j, place: (0, 0)),
                pl.BlockSpec((1, *table.shape[1:]), lambda j, place: (j ^ place[0], 0, 0, 0)),
                pl.BlockSpec(fold.shape, lambda j, place: (0, 0)),
                pl.BlockSpec(block.shape, lambda j, place: (0, 0)),
            ],
            out_specs=[
                pl.BlockSpec((1, tokens, rows), lambda j, place: (j, 0, 0)),
                pl.BlockSpec((tokens, width), lambda j, place: (0, j)),
            ],
        ),
        compiler_params=pltpu.CompilerParams(vmem_limit_bytes=40 * 2**20),
        cost_estimate=pl.CostEstimate(flops=1, bytes_accessed=1, transcendentals=0),
    )(place, picked, expand, entry, table, fold, block)


def join_kernel(*refs):
    rows = refs[0].shape[0]
    for k, ref in enumerate(refs[:-1]):
        refs[-1][k * rows : (k + 1) * rows, :] = ref[...]


def join_blocks(parts, turns):
    rows, columns = parts[0].shape
    width = columns // SHARERS
    return pl.pallas_call(
        join_kernel,
        out_shape=jax.ShapeDtypeStruct((len(parts) * rows, columns), parts[0].dtype),
        grid=(SHARERS,),
        in_specs=[pl.BlockSpec((rows, width), lambda j, t=t: (0, j ^ t)) for t in turns],
        out_specs=pl.BlockSpec((len(parts) * rows, width), lambda j: (0, j)),
        cost_estimate=pl.CostEstimate(
            flops=0, bytes_accessed=4 * len(parts) * rows * columns, transcendentals=0
        ),
    )(*parts)


def part_kernel(*refs):
    count = len(refs) // 3
    for left, right, out in zip(refs[:count], refs[count : 2 * count], refs[2 * count :]):
        out[...] = (left[...].astype(WIDE) + right[...].astype(WIDE)).astype(out.dtype)


def part_sums(left, right, turns):
    rows, columns = left.shape[0] // len(turns), left.shape[1]
    width = columns // SHARERS
    specs = [
        pl.BlockSpec((rows, width), lambda j, k=k, t=t: (k, j ^ t)) for k, t in enumerate(turns)
    ]
    return pl.pallas_call(
        part_kernel,
        out_shape=[
            jax.ShapeDtypeStruct((rows, columns), LOW if k else WIDE) for k in range(len(turns))
        ],
        grid=(SHARERS,),
        in_specs=specs + specs,
        out_specs=[pl.BlockSpec((rows, width), lambda j: (0, j))] * len(turns),
        cost_estimate=pl.CostEstimate(
            flops=left.size, bytes_accessed=6 * left.size, transcendentals=0
        ),
    )(*[left] * len(turns), *[right] * len(turns))


def small_kernel(decays, clip_ref, *refs):
    count = len(decays)
    clip = clip_ref[0]
    for i, decay in enumerate(decays):
        weight, gradient, first, second = (ref[...] for ref in refs[4 * i : 4 * i + 4])
        outs = refs[4 * count + 3 * i : 4 * count + 3 * i + 3]
        first_new, second_new, update = moments_of(weight, gradient, first, second, clip, decay)
        outs[0][...] = apply_trust(
            weight,
            update,
            jnp.sum(weight * weight, keepdims=True),
            jnp.sum(update * update, keepdims=True),
        )
        outs[1][...] = first_new
        outs[2][...] = second_new


def small_steps(clip, groups, decays):
    flat = [values for group in groups for values in group]
    return pl.pallas_call(
        functools.partial(small_kernel, decays),
        out_shape=[
            jax.ShapeDtypeStruct(group[0].shape, WIDE) for group in groups for _ in range(3)
        ],
        in_specs=[pl.BlockSpec(memory_space=pltpu.SMEM)]
        + [pl.BlockSpec(memory_space=pltpu.VMEM)] * len(flat),
        out_specs=[pl.BlockSpec(memory_space=pltpu.VMEM)] * (3 * len(groups)),
        compiler_params=pltpu.CompilerParams(vmem_limit_bytes=48 * 2**20),
    )(clip, *flat)


class Grid:
    def __init__(self, rows, heads):
        self.rows, self.heads = rows // SHARERS, heads
        self.each = H // heads
        self.parts = SHARERS // self.each
        self.members = SHARERS * heads
        self.shape = (self.rows, self.each, self.parts, heads)
        self.evens = range(2, self.members, 2)

    def sharer(self):
        return lax.axis_index("q") * self.parts + lax.axis_index("p")

    def pair(self, values, step):
        return lax.ppermute(values, ("q", "p", "h"), [(i, i ^ step) for i in range(self.members)])

    def trade(self, values, step):
        return lax.ppermute(values, ("q", "p"), [(i, i ^ step) for i in range(SHARERS)])

    def turns(self):
        return [0] + [d // self.heads for d in self.evens]

    def spread(self, own):
        parts = [own] + [self.pair(own, d) for d in self.evens]
        half = join_blocks(parts, self.turns())
        return half, self.pair(half, 1)

    def gathered_sum(self, half, other):
        parts = part_sums(half, self.pair(other, 1), self.turns())
        total = parts[0]
        for part, d in zip(parts[1:], self.evens):
            total = total + self.pair(part, d).astype(WIDE)
        return total

    def group_total(self, values):
        step = 1
        while step < self.members:
            values = values + self.pair(values, step)
            step *= 2
        return values

    def every(self, values):
        step = 1
        while step < self.members:
            values = jnp.concatenate([values, self.pair(values, step)], axis=0)
            step *= 2
        step = 1
        while step < self.rows:
            moved = lax.ppermute(values, "a", [(i, i ^ step) for i in range(self.rows)])
            values = jnp.concatenate([values, moved], axis=0)
            step *= 2
        return values

    def facing(self, values):
        return lax.ppermute(values, "a", [(0, 1), (1, 0)])

    def row_list(self, values):
        if self.rows == 2:
            return [values, self.facing(values)]
        every = lax.all_gather(values, "a", axis=0)
        return [every[i] for i in range(self.rows)]

    def row_gather(self, values):
        parts = self.row_list(values)
        if self.rows == 2:
            flag = lax.axis_index("a") == 1
            parts = exchange(flag, *parts)
        return list(parts)

    def row_sum(self, values):
        if self.rows == 2:
            return values.astype(WIDE) + self.facing(values).astype(WIDE)
        return lax.psum(values.astype(WIDE), "a")

    def total(self, values):
        return self.row_sum(self.group_total(values))

    def ordered(self, parts):
        place = self.sharer()
        low, high = place % 2 == 1, place // 2 == 1
        parts = [jnp.where(low, parts[j ^ 1], parts[j]) for j in range(SHARERS)]
        return [jnp.where(high, parts[j ^ 2], parts[j]) for j in range(SHARERS)]

    def absolute(self, values):
        return jnp.concatenate(self.ordered(jnp.split(values, SHARERS, axis=-1)), axis=-1)

    def to_rows(self, values):
        values = self.absolute(values)
        if self.rows != 2:
            return lax.all_to_all(values, "a", split_axis=0, concat_axis=1, tiled=True)
        flag = lax.axis_index("a") == 1
        kept, sent = exchange(flag, *jnp.split(values, 2, axis=0))
        return jnp.concatenate(exchange(flag, kept, self.facing(sent)), axis=1)

    def from_rows(self, values):
        if self.rows != 2:
            return self.absolute(
                lax.all_to_all(values, "a", split_axis=1, concat_axis=0, tiled=True)
            )
        flag = lax.axis_index("a") == 1
        kept, sent = exchange(flag, *jnp.split(values, 2, axis=1))
        moved = jnp.concatenate(exchange(flag, kept, self.facing(sent)), axis=0)
        return self.absolute(moved)

    def renamed(self, values, step):
        block = values.shape[0] // self.members
        span = 1
        while span < self.members // 2:
            if step // 2 & span:
                halves = values.reshape(-1, 2, span * block, values.shape[1])
                values = jnp.stack([halves[:, 1], halves[:, 0]], axis=1).reshape(values.shape)
            span *= 2
        return values

    def columns(self, values):
        found = [values]
        for d in range(1, self.parts):
            got = lax.ppermute(values, "p", [(i, i ^ d) for i in range(self.parts)])
            found.append(self.renamed(got, d * self.heads))
        return jnp.concatenate(found, axis=1)

    def local(self, values, axis):
        size = values.shape[axis] // (self.rows * SHARERS)
        first, place = lax.axis_index("a") * SHARERS, self.sharer()
        return [
            lax.dynamic_slice_in_dim(values, (first + (place ^ j)) * size, size, axis)
            for j in range(SHARERS)
        ]

    def stats(self, values, count):
        center = jnp.mean(values, axis=1)
        spread = jnp.sum(jnp.square(values - center[:, None]), axis=1)
        parts = self.row_list(jnp.stack([center, spread]))
        mean = sum(part[0] for part in parts) / self.rows
        size = count // self.rows
        square = sum(part[1] + size * jnp.square(part[0] - mean) for part in parts)
        return mean[:, None], lax.rsqrt(square / count + EPS_NORM)[:, None]

    def split_plain(self, values, parts, width):
        rows = values.shape[0]
        values = values.astype(LOW).reshape(rows, self.each, parts, self.parts, -1)
        values = values.transpose(1, 3, 0, 2, 4).reshape(SHARERS, rows, -1)
        return [
            lax.dynamic_index_in_dim(values, self.sharer() ^ j, 0, False) for j in range(SHARERS)
        ]

    def merge_plain(self, pieces, parts, width):
        values = jnp.stack(self.ordered(pieces))
        rows = values.shape[1]
        values = values.reshape(self.each, self.parts, rows, parts, -1)
        return values.transpose(2, 0, 3, 1, 4).reshape(rows, self.each, parts * width)


def tied(*values):
    return lax.optimization_barrier(values)


def split_three(values):
    high = lax.reduce_precision(values, 8, 7)
    rest = values - high
    middle = lax.reduce_precision(rest, 8, 7)
    return high.astype(LOW), middle.astype(LOW), (rest - middle).astype(LOW)


def per_device(grid, *arguments):
    (
        cell_ids,
        cell_mask,
        labels,
        abd_weights,
        abd_first,
        abd_second,
        abd_gains,
        abd_gains_first,
        abd_gains_second,
        aba_weights,
        aba_first,
        aba_second,
        aba_gains,
        aba_gains_first,
        aba_gains_second,
        embed_table,
        embed_first,
        embed_second,
        output_table,
        output_first,
        output_second,
    ) = arguments
    h = lax.axis_index("h")
    attr_count, entries, embed_width = embed_table.shape
    classes = output_table.shape[2]
    model_width = attr_count * embed_width
    own_tokens = cell_ids.shape[0] // grid.heads
    first_device = ((lax.axis_index("a") == 0) & (grid.sharer() == 0)).astype(WIDE)
    native = grid.each == 2
    side = jnp.stack([lax.axis_index("q"), lax.axis_index("p")]).astype(jnp.int32)

    def own_rows(values):
        return lax.dynamic_slice_in_dim(values, h * own_tokens, own_tokens, 0)

    attrs_held = labels.shape[1]
    mask_held = lax.dynamic_slice_in_dim(cell_mask, h * attrs_held, attrs_held, 1)
    codes = jnp.where(mask_held == 1, labels, -1).reshape(own_tokens, attr_count)
    picked = own_rows(jnp.where(cell_mask == 1, classes, cell_ids))
    gathered = grid.every(jnp.concatenate([picked, codes], axis=1).astype(LOW))
    tokens = gathered.shape[0]
    picked_all = gathered[:, :attr_count]
    codes_all = gathered[:, attr_count:].reshape(-1, grid.heads, own_tokens, attr_count)
    device = (lax.axis_index("a") * SHARERS + grid.sharer()) * grid.heads + h

    def by_head(parts):
        for bit in range((grid.heads - 1).bit_length()):
            flag = (h >> bit) % 2 == 1
            parts = [
                jnp.where(flag, parts[d ^ (1 << bit)], parts[d]) for d in range(grid.heads)
            ]
        return parts

    def pieces_of(sections):
        if native:
            return split_weights(weight_view, side, sections)
        found = []
        for offset, parts, size in sections:
            columns = abd_weights[:, :, offset : offset + parts * size]
            found.append(grid.split_plain(columns, parts, size))
        return [jnp.concatenate(piece, axis=1) for piece in zip(*found)]

    def traded(values):
        return [values[0]] + [grid.trade(values[j], j) for j in (1, 2, 3)]

    weight_view = native_view(abd_weights) if native else None
    qkv_pieces, table = tied(pieces_of(SECTIONS[:1]), embed_table)
    qkv_pieces, picked_all, side = tied(qkv_pieces, picked_all, side)
    qkv_w = traded(qkv_pieces)
    picked_all, other_pieces = tied(picked_all, pieces_of(SECTIONS[1:3]))

    held = tokens // grid.members
    place = jnp.arange(tokens, dtype=jnp.int32)
    owner, inside = place // held, place % held
    owner = 2 * (owner % (grid.members // 2)) + owner // (grid.members // 2)
    owner = owner ^ (grid.sharer() * grid.heads + h)
    source = (inside // own_tokens * grid.members + owner) ^ device
    row_of = source * own_tokens + inside % own_tokens
    picked = dot((row_of[:, None] == place[None, :]).astype(LOW), picked_all).astype(LOW)
    picked = jnp.concatenate(grid.local(picked, 1), axis=1)
    local_attrs = picked.shape[1]
    block_attrs = local_attrs // SHARERS
    table_rows = jnp.arange(block_attrs * entries, dtype=jnp.int32)
    row_attr, row_entry = table_rows // entries, (table_rows % entries).astype(WIDE)
    block_columns = jnp.arange(block_attrs * embed_width, dtype=jnp.int32)
    own_block = row_attr[:, None] == block_columns // embed_width
    fold = (
        block_columns[:, None] % embed_width == jnp.arange(embed_width, dtype=jnp.int32)
    ).astype(LOW)
    table = lax.dynamic_slice_in_dim(table, lax.axis_index("a") * local_attrs, local_attrs, 0)
    table = table.reshape(SHARERS, row_attr.size, embed_width)
    places = jnp.arange(local_attrs, dtype=jnp.int32)
    expand = places[None, :, None] == (
        jnp.arange(SHARERS, dtype=jnp.int32)[:, None, None] * block_attrs + row_attr[None, None, :]
    )
    hots, embedded = embed_tokens(
        grid.sharer().astype(jnp.int32)[None],
        picked,
        expand.astype(LOW),
        row_entry[None, :],
        jnp.stack(split_three(table), axis=1),
        fold,
        own_block.astype(WIDE),
    )
    embedded, qkv_w, other_pieces, side = tied(embedded, qkv_w, other_pieces, side)
    qkv_w = jnp.concatenate(qkv_w, axis=0)
    others = traded(other_pieces)

    kinds = jnp.arange(classes, dtype=jnp.int32).astype(WIDE)
    mask_own = own_rows(cell_mask).astype(WIDE)
    counts, own_codes = [], []
    for d in range(grid.heads):
        found = (codes_all[:, d].reshape(-1, attr_count)[:, :, None].astype(WIDE) == kinds)
        found = jnp.sum(found.astype(WIDE), axis=0)
        counts.append(jnp.sum(found.reshape(-1, attrs_held, classes), axis=0))
        own_codes.append(own_rows(codes_all[0, d].reshape(-1, attrs_held)))
    counts = jnp.concatenate(by_head(counts), axis=0)
    own_codes = jnp.concatenate(by_head(own_codes), axis=1)
    label_hot = (own_codes.astype(WIDE)[:, :, None] == kinds).astype(WIDE)
    class_weight = lax.rsqrt(1.0 + counts)
    weight_total = jnp.sum(counts * class_weight)
    tables_low = output_table.astype(LOW)[None]
    step = 1
    while step < grid.heads:
        tables_low = jnp.concatenate([tables_low, grid.pair(tables_low, step)], axis=0)
        step *= 2
    output_low = jnp.concatenate(by_head(list(tables_low)), axis=0)

    out_size, up_size = HD * grid.each // SHARERS, UNITS * grid.each // SHARERS
    gains = jnp.concatenate(grid.local(abd_gains, 1), axis=1)
    mean_one, scale_one = grid.stats(embedded, model_width)
    hat_one = (embedded - mean_one) * scale_one
    normed = (hat_one * gains[0]).astype(LOW)
    triple = grid.row_sum(dot(normed, qkv_w).astype(LOW)).astype(LOW)
    triple, others, class_weight, weight_total, label_hot, output_low, down_pieces = tied(
        triple, others, class_weight, weight_total, label_hot, output_low, pieces_of(SECTIONS[3:])
    )
    part = HD // grid.parts
    query_own, key_own, value_own = (triple[:, i * part : (i + 1) * part] for i in range(3))
    queries, key_rows = grid.columns(query_own), grid.columns(key_own)
    value_rows = grid.columns(value_own)
    factor = HD ** (-0.5)
    scores = dot(queries, key_rows, 1, 1) * factor
    shifted = jnp.exp(scores - jnp.max(scores, axis=1, keepdims=True))
    probs = shifted / jnp.sum(shifted, axis=1, keepdims=True)
    probs_low = probs.astype(LOW)
    attended = dot(probs_low, value_own).astype(LOW)
    out_w = jnp.concatenate([piece[:, :out_size] for piece in others], axis=0)
    up_w = jnp.concatenate([piece[:, out_size:] for piece in others], axis=0)
    attended = jnp.split(attended, 2, axis=0)
    branch = [dot(a, out_w, 1, 1).astype(LOW) for a in attended]
    middle = embedded[:held] + grid.gathered_sum(*branch)
    mean_two, scale_two = grid.stats(middle, model_width)
    hat_two = (middle - mean_two) * scale_two
    second = grid.spread((hat_two * gains[1]).astype(LOW))
    before, down_pieces = tied([dot(a, up_w).astype(LOW) for a in second], down_pieces)
    before = [grid.row_sum(b) for b in before]
    before[0], down_w, up_turned, qkv_turned = tied(
        before[0], traded(down_pieces), up_w.T, qkv_w.T
    )
    down_w = jnp.concatenate(down_w, axis=0)
    hidden = [gelu_apply(before[0]).astype(LOW)]
    down = [dot(hidden[0], down_w, 1, 1).astype(LOW)]
    before[1], hidden[0], down[0] = tied(before[1], hidden[0], down[0])
    hidden.append(gelu_apply(before[1]).astype(LOW))
    down.append(dot(hidden[1], down_w, 1, 1).astype(LOW))
    after = middle + grid.gathered_sum(*down)

    aba_low = aba_weights.astype(LOW)
    final, aba_stored = aba_forward(grid.to_rows(after), aba_low, aba_gains)
    final_low = final.reshape(own_tokens, attr_count, embed_width).astype(LOW)
    logits = jnp.einsum("tfe,fec->tfc", final_low, output_low, preferred_element_type=WIDE)
    highest = jnp.max(logits, axis=-1, keepdims=True)
    exped = jnp.exp(logits - highest)
    totals = jnp.sum(exped, axis=-1, keepdims=True)
    log_total = (highest + jnp.log(totals))[:, :, 0]
    cell_weight = mask_own * jnp.sum(label_hot * class_weight[None], axis=-1)
    loss_local = jnp.sum(cell_weight * (log_total - jnp.sum(label_hot * logits, axis=-1)))
    logit_grad = ((cell_weight / weight_total)[:, :, None] * (exped / totals - label_hot)).astype(
        LOW
    )
    final_grad = jnp.einsum("tfc,fec->tfe", logit_grad, output_low, preferred_element_type=WIDE)
    output_part = jnp.einsum("tfe,tfc->fce", final_low, logit_grad, preferred_element_type=WIDE)
    rows_grad, aba_part, aba_gains_part = aba_backward(
        final_grad.reshape(own_tokens, model_width), aba_stored, aba_low, aba_gains
    )

    width = normed.shape[1] // SHARERS
    gradient_sq = []

    def row_gradients(acts, uppers):
        found = []
        for j in range(SHARERS):
            cut = slice(j * width, (j + 1) * width)
            piece = sum(dot(a[:, cut], u, 0, 0) for a, u in zip(acts, uppers)).astype(LOW)
            gradient_sq.append(jnp.sum(jnp.square(piece.astype(WIDE))))
            found.append(piece)
        return found

    upstream = grid.from_rows(rows_grad.astype(LOW))
    down_grad = grid.spread(upstream)
    hidden_grad = tied(*[dot(a, down_w).astype(LOW) for a in down_grad])
    hidden_grad = [grid.row_sum(g) for g in hidden_grad]
    down_gradient = traded(row_gradients(down_grad, hidden))

    hidden_grad[0], down_gradient = tied(hidden_grad[0], down_gradient)

    before_grad = [gelu_back(before[0], hidden_grad[0]).astype(LOW)]
    second_grad = [dot(before_grad[0], up_turned).astype(LOW)]
    hidden_grad[1], before_grad[0], second_grad[0] = tied(
        hidden_grad[1], before_grad[0], second_grad[0]
    )
    before_grad.append(gelu_back(before[1], hidden_grad[1]).astype(LOW))
    second_grad.append(dot(before_grad[1], up_turned).astype(LOW))
    second_grad = grid.gathered_sum(*second_grad)
    gained = second_grad * gains[1]
    sums = jnp.stack([jnp.sum(gained, axis=1), jnp.sum(gained * hat_two, axis=1)])
    sums = sum(grid.row_list(sums)) / model_width
    middle_grad = upstream.astype(WIDE) + scale_two * (
        gained - sums[0][:, None] - hat_two * sums[1][:, None]
    )
    middle_grad, up_gradient = tied(middle_grad, row_gradients(second, before_grad))
    up_gradient = traded(up_gradient)
    gain_two = jnp.sum(second_grad * hat_two, axis=0)
    branch_grad = grid.spread(middle_grad.astype(LOW))
    attended_grad = jnp.concatenate([dot(a, out_w).astype(LOW) for a in branch_grad], axis=0)
    attended_grad, attended, table_acts, output_part, aba_part, aba_gains_part = tied(
        attended_grad, attended, middle_grad.astype(LOW), output_part, aba_part, aba_gains_part
    )

    small = jnp.concatenate([aba_part.reshape(-1), aba_gains_part.reshape(-1)])
    blocks = output_part.reshape(grid.heads, -1)
    bits = (grid.heads - 1).bit_length()
    for bit in range(bits):
        flag = (h >> bit) % 2 == 1
        halves = blocks.reshape(-1, 2, blocks.shape[1])
        kept, sent = exchange(flag, halves[:, 0], halves[:, 1])
        got = grid.pair(jnp.concatenate([sent.reshape(-1), small]).reshape(-1, 128), 1 << bit)
        got = got.reshape(-1)
        blocks = kept + got[: sent.size].reshape(kept.shape)
        small = small + got[sent.size :]
    packed = jnp.concatenate([blocks.reshape(-1), small]).reshape(-1, 128)
    for step in (grid.heads, 2 * grid.heads):
        packed = packed + grid.pair(packed, step)
    packed = grid.row_sum(lax.reduce_precision(packed, 8, 7).astype(LOW)).reshape(-1)
    output_grad = packed[: blocks.size].reshape(-1, classes, embed_width)
    aba_grad = packed[blocks.size : blocks.size + aba_weights.size].reshape(aba_weights.shape)
    aba_gains_grad = packed[blocks.size + aba_weights.size :].reshape(aba_gains.shape)

    attended_grad, up_gradient, output_grad, aba_grad, aba_gains_grad = tied(
        grid.row_sum(attended_grad).astype(LOW), up_gradient, output_grad, aba_grad, aba_gains_grad
    )
    out_gradient = row_gradients(branch_grad, attended)
    prob_grad = dot(grid.columns(attended_grad), value_rows, 1, 1)
    score_grad = probs * (prob_grad - jnp.sum(probs * prob_grad, axis=1, keepdims=True))
    score_grad = score_grad.astype(LOW)
    query_grad = dot(score_grad, key_own) * factor
    key_grad = dot(score_grad, query_own, 0, 0) * factor
    value_grad = dot(probs_low, attended_grad, 0, 0)
    triple_grad = jnp.concatenate([query_grad, key_grad, value_grad], axis=1).astype(LOW)
    table_part = [
        dot(hot[:held], block, 0, 0)
        for hot, block in zip(hots, jnp.split(table_acts, SHARERS, axis=1))
    ]
    triple_grad, table_part, out_gradient = tied(triple_grad, table_part, out_gradient)
    qkv_gradient = row_gradients([normed], [triple_grad])
    qkv_gradient = [jnp.concatenate(pair, axis=1) for pair in zip(qkv_gradient, out_gradient)]
    triple_grad, qkv_gradient = tied(triple_grad, qkv_gradient)

    normed_grad = dot(triple_grad, qkv_turned)
    gained = normed_grad * gains[0]
    sums = jnp.stack([jnp.sum(gained, axis=1), jnp.sum(gained * hat_one, axis=1)])
    sums = sum(grid.row_list(sums)) / model_width
    gain_one = jnp.sum(normed_grad * hat_one, axis=0)
    spread_grad = scale_one * (gained - sums[0][:, None] - hat_one * sums[1][:, None])
    records = []
    for j, block in enumerate(jnp.split(spread_grad.astype(LOW), SHARERS, axis=1)):
        grad = table_part[j] + dot(hots[j], block, 0, 0)
        grad = jnp.where(own_block, grad, 0.0)
        grad = jnp.dot(grad, fold.astype(WIDE), precision=lax.Precision.HIGHEST)
        cut = slice(j * width, (j + 1) * width)
        records.append(jnp.concatenate([grad.reshape(-1), gain_one[cut], gain_two[cut]]))
    table_size = block_attrs * entries * embed_width
    packed = jnp.stack(grid.ordered(records)).reshape(-1, 128)
    output_sq = first_device * jnp.sum(output_grad * output_grad)
    scalars = jnp.stack([sum(gradient_sq), output_sq, loss_local])
    lane = jnp.arange(8 * 128, dtype=jnp.int32).reshape(8, 128)
    scalars = sum(jnp.where(lane == i, scalars[i], 0.0) for i in range(3))
    packed, qkv_gradient = tied(packed, traded(qkv_gradient))
    gradients = qkv_gradient + up_gradient + down_gradient
    packed = grid.group_total(jnp.concatenate([scalars, packed], axis=0))
    summed = grid.row_sum(packed[:8])[0, :3]
    packed = lax.reduce_precision(packed[8:], 8, 7).astype(LOW)
    packed = jnp.stack(grid.row_gather(packed)).astype(WIDE)
    packed = packed.reshape(grid.rows * SHARERS, -1)
    embed_grad = packed[:, :table_size].reshape(embed_table.shape).transpose(1, 0, 2)
    abd_gains_grad = packed[:, table_size:].reshape(-1, 2, width).transpose(1, 0, 2)
    abd_gains_grad = abd_gains_grad.reshape(2, model_width)

    output_table, output_first, output_second = (
        values.transpose(0, 2, 1) for values in (output_table, output_first, output_second)
    )
    embed_table, embed_first, embed_second = (
        values.transpose(1, 0, 2) for values in (embed_table, embed_first, embed_second)
    )
    replicated_sq = (
        jnp.sum(abd_gains_grad * abd_gains_grad)
        + jnp.sum(aba_grad * aba_grad)
        + jnp.sum(aba_gains_grad * aba_gains_grad)
        + jnp.sum(embed_grad * embed_grad)
    )
    grad_norm = jnp.sqrt(summed[0] + summed[1] + replicated_sq)
    loss_sum = summed[2]
    clip_factor = jnp.minimum(1.0, CLIP_LIMIT / (grad_norm + 1e-06))
    if native:
        first_view, second_view, abd_update, squares = moments_step(
            side,
            clip_factor[None],
            weight_view,
            native_view(abd_first),
            native_view(abd_second),
            gradients,
        )
        abd_first_new = from_native(first_view, grid.each)
        abd_second_new = from_native(second_view, grid.each)
        abd_update_sq, abd_weight_sq = jnp.sum(squares[0]), jnp.sum(squares[1])
    else:
        first_g, up_g, down_g = (gradients[SHARERS * i : SHARERS * (i + 1)] for i in range(3))
        split_g = (
            [g[:, : 3 * out_size] for g in first_g],
            [g[:, 3 * out_size :] for g in first_g],
            up_g,
            down_g,
        )
        merged = [
            grid.merge_plain(pieces, parts, size)
            for pieces, (_, parts, size) in zip(split_g, SECTIONS)
        ]
        abd_grad = jnp.concatenate(merged, axis=2).astype(WIDE)
        abd_first_new, abd_second_new, abd_update = moments_of(
            abd_weights, abd_grad, abd_first, abd_second, clip_factor, WEIGHT_DECAY
        )
        abd_update_sq, abd_weight_sq = (
            jnp.sum(abd_update * abd_update),
            jnp.sum(abd_weights * abd_weights),
        )
    output_first_new, output_second_new, output_update = moments_of(
        output_table, output_grad, output_first, output_second, clip_factor, WEIGHT_DECAY
    )
    trust_sums = grid.total(
        jnp.stack(
            [
                abd_update_sq,
                first_device * jnp.sum(output_update * output_update),
                abd_weight_sq,
                first_device * jnp.sum(output_table * output_table),
            ]
        )
    )
    if native:
        abd_new = from_native(
            apply_trust(weight_view, abd_update.astype(WIDE), trust_sums[2], trust_sums[0]),
            grid.each,
        )
    else:
        abd_new = apply_trust(abd_weights, abd_update, trust_sums[2], trust_sums[0])
    output_new = apply_trust(output_table, output_update, trust_sums[3], trust_sums[1])
    small = small_steps(
        clip_factor[None],
        (
            (abd_gains, abd_gains_grad, abd_gains_first, abd_gains_second),
            (aba_weights, aba_grad, aba_first, aba_second),
            (aba_gains, aba_gains_grad, aba_gains_first, aba_gains_second),
            (embed_table, embed_grad, embed_first, embed_second),
        ),
        (0.0, WEIGHT_DECAY, 0.0, WEIGHT_DECAY),
    )
    return (
        loss_sum,
        weight_total,
        grad_norm,
        abd_new,
        abd_first_new,
        abd_second_new,
        *small[:9],
        *[values.transpose(1, 0, 2) for values in small[9:]],
        *[values.transpose(0, 2, 1) for values in (output_new, output_first_new, output_second_new)],
    )


def solution(mesh):
    grid = Grid(mesh.shape["dp"], mesh.shape["head"])
    devices = Mesh(mesh.devices.reshape(grid.shape), ("a", "q", "p", "h"))
    rows = ("a", "q", "p")
    tokens, table = P(rows, None), P("h", None, None)
    weight = P(rows, "h", None)
    in_specs = (tokens, tokens, P(rows, "h"), weight, weight, weight) + (P(),) * 12 + (table,) * 3
    out_specs = (P(),) * 3 + (weight,) * 3 + (P(),) * 12 + (table,) * 3
    return jax.shard_map(
        functools.partial(per_device, grid),
        mesh=devices,
        in_specs=in_specs,
        out_specs=out_specs,
        check_vma=False,
    )
```
